32 devices in a mesh: gz: 8 (over z, y), pa: 4 (over x, core).
Axes of the slice: x: 2, y: 2, z: 4, core: 2. Of those that a mesh axis runs over, the one named last changes fastest.
Arguments:
- velocity: float32 [3, 8, 192, 512], P(None, 'gz', None, 'pa'), may hold values from -4 to 4
- viscosity: float32 [8, 192, 512], P('gz', None, 'pa'), may hold values from 0.2 to 2
- parcels: float32 [32768, 16], P(('gz', 'pa')), may hold values from -4 to 4, as said below
- dest_rank: int32 [32768, 1], P(('gz', 'pa')), may hold values from 0 to 7; in each aligned block of 1024 rows (0 to 1023, 1024 to 2047, ...) at most 384 rows name the same one
- dest_cell: int32 [32768], P(('gz', 'pa')), may hold values from 0 to 24575
- counts: int32 [32], P(('gz', 'pa')), may hold values from 1 to 1024, 24576 in all
Outputs:
- velocity_out: float32 [3, 8, 192, 512], P(None, 'gz', None, 'pa')
- parcels_out: float32 [98304, 16], P(('gz', 'pa'))
The draws below stay inside these ranges and needn't reach their ends.
Inputs may be any that keep to these rules, and one draw needn't show every extreme that they name: `dest_rank`: among the 1024 rows of one device no slab is named more than 384 times, and some block names one slab exactly 384 times. `counts`: some device has all 1024 rows live. `parcels`: columns 4 k + 3 hold positive drag rates.
All inputs are finite; a program needn't handle non-finite values.
Results may differ from the reference program's by a relative error of at most 0.0011.
Values sent between devices are 32-bit elements; how exact they have to be, the bound alone decides.
A program may use at most 64 MiB of HBM per device.

```python
import math
import jax
import jax.numpy as jnp
import numpy as np
from jax import lax

NR = 192
NTH = 512
CZ = 1
PAR_DEV = 1024
CAP = 384
NZ = 8
CT = 128
CELLS_DEV = 24576
PARCELS = 32768
N_GZ = 8
N_PA = 4
DEVICES = 32


def draw_velocity(key, part):
    key = jax.random.fold_in(key, 5)
    shape = (3, NZ, NR, NTH)
    values = jnp.clip(jax.random.normal(key, shape, jnp.float32), -4.0, 4.0)
    return values


def draw_parcels(key, part):
    key = jax.random.fold_in(key, 9)
    speed_key, rate_key = jax.random.split(key)
    speeds = jnp.clip(jax.random.normal(speed_key, (PARCELS, 4, 3), jnp.float32), -4.0, 4.0)
    rates = jnp.exp(jax.random.uniform(rate_key, (PARCELS, 4, 1), jnp.float32, math.log(0.2), math.log(3.0)))
    return jnp.concatenate([speeds, rates], -1).reshape(PARCELS, 16)


def set_ends(result, rng, least, top_value):
    longest = result.shape.index(max(result.shape))
    spots = []
    for shift in (0, 1):
        where = [jax.random.randint(jax.random.fold_in(rng, axis), (), 0, length) for axis, length in enumerate(result.shape)]
        where[longest] = (where[longest] + shift) % result.shape[longest]
        spots.append(tuple(where))
    return result.at[spots[0]].set(least).at[spots[1]].set(top_value)


def levels(key, extent, cuts, least, largest):
    level, own = 1.0, jax.random.fold_in(key, 6)
    for position, blocks in cuts:
        steps = jnp.exp(jax.random.uniform(jax.random.fold_in(own, position), (blocks,), jnp.float32, least / len(cuts), largest / len(cuts)))
        level = level * jnp.repeat(steps, extent[position] // blocks).reshape([-1 if axis == position else 1 for axis in range(len(extent))])
    return level


def split_up(number_of, total, bound, slope):
    weights = [(1 << 20) // math.isqrt(grade ** slope) + 1 for grade in range(2, number_of + 1)]
    spare, given = total - bound - (number_of - 1), [1] * (number_of - 1)
    while spare > 0:
        movable = [i for i in range(number_of - 1) if given[i] < bound]
        mass, left = sum([weights[i] for i in movable]), spare
        for i in movable:
            more = min(bound - given[i], max(1, left * weights[i] // mass), spare)
            given[i] = given[i] + more
            spare = spare - more
    return np.array([bound] + given)


def uneven(key, amount, total, most, slope):
    if amount == 2:
        one = jax.random.randint(key, (), max(1, total - most), min(most, total - 1) + 1)
        return jnp.stack([one, total - one])
    sizes = jnp.asarray(split_up(amount, total, most, slope), jnp.int32)
    pairs = (amount - 1) // 2
    donor, taker = sizes[1:1 + 2 * pairs:2], sizes[2:2 + 2 * pairs:2]
    room = jnp.minimum(donor - 1, most - taker)
    shifted = jax.random.randint(jax.random.fold_in(key, 1), (pairs,), 0, 1 << 20) % (room + 1)
    sizes = sizes.at[1:1 + 2 * pairs:2].set(donor - shifted).at[2:2 + 2 * pairs:2].set(taker + shifted)
    return sizes[jax.random.permutation(jax.random.fold_in(key, 2), amount)]


def shared_out(key, own, number, rows, number_of, top, bound, slope):
    order = jax.random.permutation(key, number_of)
    crowded, ordinary = portions_of(number_of, rows * top, bound, slope, True), portions_of(number_of, rows * top, bound, slope, False)
    places = jnp.arange(number_of)

    def named(sizes, offset_by):
        used = int((sizes > 0).sum())
        fixed = max(1, used // 4)
        moved = fixed + (places - fixed + offset_by * (used - fixed)) % max(1, number_of - fixed)
        return jnp.zeros((number_of,), jnp.int32).at[order[jnp.where(places < fixed, places, moved)]].set(jnp.asarray(sizes, jnp.int32))

    sizes = jnp.where(number % 4 == 0, named(crowded, number // 4), named(ordinary, number - number // 4 - 1))
    mixed = jax.random.permutation(jax.random.fold_in(own, 3), number_of)
    giver, taker = mixed[0:number_of // 2 * 2:2], mixed[1:number_of // 2 * 2:2]
    room = jnp.minimum(sizes[giver] - 1, bound - sizes[taker]) // 2
    room = jnp.where((giver == order[0]) | (taker == order[0]) | (sizes[taker] == 0), 0, jnp.maximum(room, 0))
    moved = jax.random.randint(jax.random.fold_in(own, 4), (number_of // 2,), 0, 1 << 20) % (room + 1)
    sizes = sizes.at[giver].add(-moved).at[taker].add(moved)
    members = jnp.searchsorted(jnp.cumsum(sizes), jnp.arange(rows * top), side="right").astype(jnp.int32)
    listing = members.reshape(top, rows).T
    listing = listing[jax.random.permutation(jax.random.fold_in(own, 1), rows)]
    offset_by = jax.random.randint(jax.random.fold_in(own, 2), (rows, 1), 0, top)
    return jnp.take_along_axis(listing, (jnp.arange(top)[None, :] + offset_by) % top, axis=1)


def portions_of(amount, total, limit, slope, full):
    portions = [(1 << 20) // math.isqrt(grade ** slope) + 1 for grade in range(1, amount + 1)]
    largest = limit if full else min(limit, max(-(-total // amount), total * portions[0] // sum(portions)))
    least = 1 if total - largest >= amount - 1 else 0
    holding, surplus = [largest] + [least] * (amount - 1), total - largest - least * (amount - 1)
    while surplus > 0:
        free = [i for i in range(1, amount) if holding[i] < largest] or [i for i in range(1, amount) if holding[i] < limit]
        pool, budget = sum([portions[i] for i in free]), surplus
        for i in free:
            extra = min(limit - holding[i], max(1, budget * portions[i] // pool), surplus)
            holding[i] = holding[i] + extra
            surplus = surplus - extra
    return np.array(holding)


def setup_inputs(seed: int = 0) -> dict:
    key_list = jax.random.split(jax.random.key(seed), 7)
    velocity = draw_velocity(jax.random.fold_in(key_list[6], 71), 0)
    viscosity = jnp.clip(jnp.exp(math.log(2.0) - 2.3025851 * jax.random.uniform(key_list[1], (NZ, NR, NTH), jnp.float32) ** levels(key_list[1], (NZ, NR, NTH), ((0, 8), (2, 4)), -0.2, 0.2)), 0.2, 2.0)
    parcels = draw_parcels(jax.random.fold_in(key_list[6], 71), 0)
    dest_rank_keys = jax.random.split(jax.random.fold_in(key_list[3], 1), PARCELS // PAR_DEV)
    dest_rank_turns = jax.random.permutation(jax.random.fold_in(key_list[3], 3), PARCELS // PAR_DEV)
    dest_rank = jax.vmap(lambda own, number: shared_out(jax.random.fold_in(key_list[3], 2), own, number, PAR_DEV, N_GZ, 1, CAP, 2))(dest_rank_keys, dest_rank_turns).reshape((PARCELS, 1))
    dest_cell = set_ends(jax.random.randint(key_list[4], (PARCELS,), 0, CELLS_DEV), jax.random.fold_in(key_list[4], 1), 0, CELLS_DEV - 1).astype(jnp.int32)
    counts = uneven(key_list[5], DEVICES, 3 * PAR_DEV * DEVICES // 4, PAR_DEV, 0).astype(jnp.int32)
    return dict(velocity=velocity, viscosity=viscosity, parcels=parcels, dest_rank=dest_rank, dest_cell=dest_cell, counts=counts)


time_step = 0.1
shift_plane = 0.0001

def radius_column(first, number):
    return (NR + first + jnp.arange(number) + 0.5).astype(jnp.float32)[:, None]

def viscous(extended, speeds, viscosity):
    planes, radii, columns = viscosity.shape
    radius = radius_column(0, radii)
    step_angle = 2.0 * math.pi / NTH
    arc_weight = 1.0 / (radius * step_angle) ** 2
    offsets = ((1, 0, 0, 1.0), (-1, 0, 0, 1.0), (0, 1, 0, (radius + 0.5) / radius), (0, -1, 0, (radius - 0.5) / radius), (0, 0, 1, arc_weight), (0, 0, -1, arc_weight))
    total = jnp.zeros_like(speeds)
    for shift_z, shift_r, shift_t, weight in offsets:
        beside = extended[:, 1 + shift_z:1 + shift_z + planes, 1 + shift_r:1 + shift_r + radii, 1 + shift_t:1 + shift_t + columns]
        face_mean = 0.5 * (viscosity + beside[3])
        total = total + weight * face_mean * (beside[:3] - speeds)
    return total

def radial_divergence(radial_speed):
    radii = radial_speed.shape[-2]
    radius = radius_column(0, radii)
    mean_face = 0.5 * (radial_speed[..., 1:, :] + radial_speed[..., :-1, :])
    inner = (radius[1:] - 0.5) * mean_face
    zeros = jnp.zeros_like(radial_speed[..., :1, :])
    flux = jnp.concatenate([zeros, inner, zeros], axis=-2)
    return (flux[..., 1:, :] - flux[..., :-1, :]) / radius

def theta_difference(values, radius):
    step_angle = 2.0 * math.pi / NTH
    return (jnp.roll(values, -1, -1) - jnp.roll(values, 1, -1)) / (2.0 * step_angle * radius)

def radial_system(modes):
    radius = radius_column(0, NR)[:, 0]
    step_angle = 2.0 * math.pi / NTH
    arc_weight = 1.0 / (radius * step_angle) ** 2
    nothing = jnp.zeros((1,), jnp.float32)
    upper = jnp.concatenate([(radius[:-1] + 0.5) / radius[:-1], nothing])
    lower = jnp.concatenate([nothing, (radius[1:] - 0.5) / radius[1:]])
    spectrum = 2.0 - 2.0 * jnp.cos(step_angle * modes.astype(jnp.float32))
    diagonal = shift_plane + arc_weight[None, :] * spectrum[:, None] + upper[None, :] + lower[None, :]
    return (jnp.broadcast_to(-lower, diagonal.shape), diagonal, jnp.broadcast_to(-upper, diagonal.shape))

def mirror_gradient(values):
    padded = jnp.concatenate([values[..., :1, :], values, values[..., -1:, :]], axis=-2)
    return 0.5 * (padded[..., 2:, :] - padded[..., :-2, :])

def hartley(values):
    spectrum = jnp.fft.fft(values, axis=-1)
    return spectrum.real - spectrum.imag

def block_slots(pair):
    target_block, live_block = pair
    marks = ((target_block[:, None] == jnp.arange(N_GZ)[None, :]) & live_block[:, None]).astype(jnp.int32)
    before = jnp.cumsum(marks, axis=0) - marks
    return jnp.sum(before * marks, axis=1)

def reference(velocity, viscosity, parcels, dest_rank, dest_cell, counts):
    positions = jnp.arange(DEVICES * PAR_DEV)
    owner_block = positions // PAR_DEV
    live = positions % PAR_DEV < counts[owner_block]
    target = dest_rank[:, 0]
    slot = lax.map(block_slots, (target.reshape(DEVICES, PAR_DEV), live.reshape(DEVICES, PAR_DEV))).reshape(-1)
    source_gz = owner_block // N_PA
    source_pa = owner_block % N_PA
    receiver = target * N_PA + source_pa
    row_index = (receiver * N_GZ + source_gz) * CAP + slot
    row_index = jnp.where(live, row_index, DEVICES * N_GZ * CAP)
    axial = target * CZ + dest_cell // (NR * CT)
    radial = dest_cell // CT % NR
    azimuth = source_pa * CT + dest_cell % CT
    fluid = velocity[:, axial, radial, azimuth].T
    classes = parcels.reshape(-1, 4, 4)
    speed = classes[..., :3]
    rate = classes[..., 3:]
    moved = (speed + time_step * rate * fluid[:, None, :]) / (1.0 + time_step * rate)
    drag = jnp.sum(rate * (moved - fluid[:, None, :]), axis=1).astype(jnp.bfloat16)
    drag = lax.optimization_barrier(drag).astype(jnp.float32)
    drag = jnp.where(live[:, None], drag, 0.0)
    updated = jnp.concatenate([moved, rate], -1).reshape(-1, 16)
    parcels_out = jnp.zeros((DEVICES * N_GZ * CAP, 16), jnp.float32).at[row_index].set(updated, mode='drop')
    deposit = jnp.zeros_like(velocity).at[:, axial, radial, azimuth].add(drag.T)
    fields = jnp.concatenate([velocity, viscosity[None]], 0)
    fields = jnp.pad(fields, ((0, 0), (1, 1), (1, 1), (0, 0)))
    extended = jnp.concatenate([fields[..., -1:], fields, fields[..., :1]], -1)
    ustar = velocity + time_step * (viscous(extended, velocity, viscosity) + deposit)
    radius = radius_column(0, NR)
    source = -(radial_divergence(ustar[1]) + theta_difference(ustar[2], radius))
    spectral = jnp.transpose(hartley(source), (2, 1, 0))
    weights = radius[:, 0]
    correction = jnp.sum(weights[:, None] * spectral[0], axis=0) / jnp.sum(weights)
    spectral = spectral.at[0].add(-correction[None, :])
    lower, diagonal, upper = radial_system(jnp.arange(NTH))
    potential_hat = lax.linalg.tridiagonal_solve(lower, diagonal, upper, spectral)
    radial_hat = mirror_gradient(potential_hat)
    both = jnp.transpose(jnp.stack([radial_hat, potential_hat]), (0, 3, 2, 1))
    physical = hartley(both) / NTH
    grad_r = physical[0]
    grad_t = theta_difference(physical[1], radius)
    velocity_out = jnp.stack([ustar[0], ustar[1] - grad_r, ustar[2] - grad_t])
    return (velocity_out, parcels_out)
```

```python
import functools
import math

import jax
import jax.numpy as jnp
import ml_dtypes
import numpy as np
from jax import lax
from jax.experimental import pallas as pl
from jax.experimental.pallas import tpu as pltpu
from jax.sharding import PartitionSpec as P

NR = 192
NTH = 512
STEP = 0.1
SHIFT = 0.0001
LIMIT = 48 * 1024 * 1024
MESH = pl.DeviceIdType.MESH
f32 = jnp.float32
bf16 = jnp.bfloat16
VM = pl.BlockSpec(memory_space=pltpu.VMEM)


def cas(n):
    x = 2.0 * np.pi / NTH * (n % NTH)
    return np.cos(x) + np.sin(x)


def halves(table):
    high = table.astype(np.float32).astype(ml_dtypes.bfloat16)
    low = (table - high.astype(np.float64)).astype(np.float32).astype(ml_dtypes.bfloat16)
    return high, low


@functools.lru_cache(None)
def forward_table(pa):
    columns = NTH // pa
    k = np.arange(NTH)[None, :]
    j = np.arange(NTH)[:, None]
    same = -cas(k * j)
    beside = -(cas(k * (j - 1)) - cas(k * (j + 1)))
    both = [np.concatenate([same[p * columns:(p + 1) * columns], beside[p * columns:(p + 1) * columns]], 0) for p in range(pa)]
    return halves(np.stack(both))


@functools.lru_cache(None)
def inverse_table(pa):
    columns = NTH // pa
    k = np.arange(NTH)[:, None]
    j = np.arange(NTH)[None, :]
    same = cas(k * j) / NTH
    beside = (cas(k * (j + 1)) - cas(k * (j - 1))) / NTH
    parts = []
    for p in range(pa):
        part = slice(p * columns, (p + 1) * columns)
        parts.append(np.stack([same[:, part], beside[:, part]]))
    return halves(np.stack(parts))


@functools.lru_cache(None)
def radial_ratios(pa):
    radius = NR + np.arange(NR) + 0.5
    step = 2.0 * np.pi / NTH
    arc = 1.0 / (radius * step) ** 2
    up = (radius + 0.5) / radius
    down = (radius - 0.5) / radius
    up[-1] = 0.0
    down[0] = 0.0
    k = np.arange(NTH)
    diagonal = SHIFT + arc[:, None] * (2.0 - 2.0 * np.cos(step * k))[None, :] + up[:, None] + down[:, None]
    lower = np.broadcast_to(-down[:, None], diagonal.shape)
    upper = np.broadcast_to(-up[:, None], diagonal.shape)

    def moved(x, s, fill):
        pad = np.full((abs(s), NTH), fill)
        return np.concatenate([pad, x[:-s]], 0) if s > 0 else np.concatenate([x[-s:], pad], 0)

    out = []
    stride = 1
    while stride < NR:
        low = lower / moved(diagonal, stride, 1.0)
        high = upper / moved(diagonal, -stride, 1.0)
        out += [low, high]
        diagonal = diagonal - low * moved(upper, stride, 0.0) - high * moved(lower, -stride, 0.0)
        lower = -low * moved(lower, stride, 0.0)
        upper = -high * moved(upper, -stride, 0.0)
        stride *= 2
    out.append(1.0 / diagonal)
    whole = np.stack(out).astype(np.float32)
    columns = NTH // pa
    return np.stack([whole[:, :, p * columns:(p + 1) * columns] for p in range(pa)])


def iota(shape, axis):
    return lax.broadcasted_iota(jnp.int32, shape, axis)


def radii():
    return (iota((NR, 1), 0) + NR).astype(f32) + 0.5


def rolled(x, s):
    return jnp.concatenate([x[s:], x[:s]], 0)


def rates_of(x):
    is_rate = iota(x.shape, 0) % 4 == 3
    w = jnp.where(is_rate, x, 0.0)
    return is_rate, w + rolled(w, 1) + rolled(w, 2) + rolled(w, 3)


def pack_kernel(gz, capacity, counts, rank, cell, parcels, first, second):
    block = rank.shape[1]
    tiles = capacity // 128
    live = iota((1, block), 1) < counts[0]
    target = jnp.where(live, rank[...], gz)
    marks = (iota((gz, block), 0) == target).astype(f32)
    earlier = (iota((128, 128), 0) < iota((128, 128), 1)).astype(f32).astype(bf16)
    carry = jnp.zeros((gz, 1), f32)
    slots = []
    for b in range(block // 128):
        part = marks[:, 128 * b:128 * b + 128]
        before = jnp.dot(part.astype(bf16), earlier, preferred_element_type=f32) + carry
        slots.append(jnp.sum(before * part, axis=0, keepdims=True))
        carry = carry + jnp.sum(part, axis=1, keepdims=True)
    slot = jnp.concatenate(slots, 1).astype(jnp.int32)
    place = jnp.where(live, target * capacity + slot, -1)
    high = place >> 7
    low = place & 127
    low_hot = (iota((128, block), 0) == low).astype(f32).astype(bf16)
    values = parcels[...]
    one = values.astype(bf16).astype(f32)
    two = (values - one).astype(bf16).astype(f32)
    three = values - one - two
    cells = cell[...]
    line = ((cells >> 7) + 1).astype(f32)
    column = (cells & 127).astype(f32)
    table = jnp.concatenate([one, two, three, line, column, jnp.zeros((14, block), f32)], 0)

    def slab(g, _):
        left = [jnp.where(high == g * tiles + i, table, 0.0).astype(bf16) for i in range(tiles)]
        got = lax.dot_general(jnp.concatenate(left, 0), low_hot, (((1,), (1,)), ((), ())), preferred_element_type=f32)
        for i in range(tiles):
            r = got[64 * i:64 * i + 64]
            rows = r[0:16] + r[16:32] + r[32:48]
            lanes = slice(128 * i, 128 * i + 128)
            second[g, :, lanes] = rows
            code = r[48:49] * 128.0 + r[49:50]
            total = 0.0
            for half in (rows[0:8], rows[8:16]):
                is_rate, rate = rates_of(half)
                weight = rate / (1.0 + STEP * rate)
                total = total + jnp.where(is_rate, weight, weight * half)
            total = total + rolled(total, 4)
            first[g, :, lanes] = jnp.where(iota(total.shape, 0) == 4, code, total)
        return 0

    lax.fori_loop(0, gz, slab, 0, unroll=gz <= 8)


def loop(first, last, step):
    if last - first <= 8:
        for i in range(first, last):
            step(i)
    else:
        lax.fori_loop(first, last, lambda i, _: (step(i), 0)[1], 0)


def route_kernel(gz, pa, first, edges, first_out, left_out, right_out, send, recv, esend, erecv):
    me = lax.axis_index("gz")
    mp = lax.axis_index("pa")
    right = lax.rem(mp + 1, pa)
    left = lax.rem(mp + pa - 1, pa)
    barrier = pltpu.get_barrier_semaphore()

    def greet(o):
        pl.semaphore_signal(barrier, inc=1, device_id=(lax.rem(me + o, gz), mp), device_id_type=MESH)

    loop(1, gz, greet)
    for q in (left, right):
        pl.semaphore_signal(barrier, inc=1, device_id=(me, q), device_id_type=MESH)
    pl.semaphore_wait(barrier, gz + 1)

    def copy(o):
        to = lax.rem(me + o, gz)
        return pltpu.make_async_remote_copy(
            src_ref=first.at[to], dst_ref=first_out.at[me], send_sem=send.at[o], recv_sem=recv.at[o],
            device_id=(to, mp), device_id_type=MESH)

    to_right = pltpu.make_async_remote_copy(
        src_ref=edges, dst_ref=left_out, send_sem=esend.at[0], recv_sem=erecv.at[0],
        device_id=(me, right), device_id_type=MESH)
    to_left = pltpu.make_async_remote_copy(
        src_ref=edges, dst_ref=right_out, send_sem=esend.at[1], recv_sem=erecv.at[1],
        device_id=(me, left), device_id_type=MESH)
    loop(1, gz, lambda o: copy(o).start())
    to_right.start()
    to_left.start()
    first_out[me] = first[me]
    loop(1, gz, lambda o: copy(o).wait())
    to_right.wait()
    to_left.wait()


def deposit_kernel(gz, first, velocity, fluid, deposit):
    columns = velocity.shape[2]
    capacity = first.shape[2]
    pieces = []
    for c in range(3):
        turned = velocity[c].T
        top = turned.astype(bf16)
        pieces += [top, (turned - top.astype(f32)).astype(bf16)]
    turned = jnp.concatenate(pieces, 0)
    deposit[...] = jnp.zeros_like(deposit)

    def slab(g, _):
        rows = first[g]
        code = rows[4:5].astype(jnp.int32)
        line = (code >> 7) - 1
        column = code & 127
        line_hot = (iota((NR, capacity), 0) == line).astype(f32).astype(bf16)
        column_hot = iota((columns, capacity), 0) == column
        picked = jnp.dot(turned, line_hot, preferred_element_type=f32)
        looked, pushes = [], []
        for c in range(3):
            both = picked[2 * c * columns:(2 * c + 1) * columns] + picked[(2 * c + 1) * columns:(2 * c + 2) * columns]
            speed = jnp.sum(jnp.where(column_hot, both, 0.0), axis=0, keepdims=True)
            drag = (rows[c:c + 1] - speed * rows[3:4]).astype(bf16).astype(f32)
            looked.append(speed)
            pushes.append(jnp.where(column_hot, drag, 0.0).astype(bf16))
        nothing = jnp.zeros_like(looked[0])
        fluid[g] = jnp.concatenate((looked + [nothing]) * 2, 0)
        added = lax.dot_general(line_hot, jnp.concatenate(pushes, 0), (((1,), (1,)), ((), ())), preferred_element_type=f32)
        for c in range(3):
            deposit[c] += added[:, c * columns:(c + 1) * columns]
        return 0

    lax.fori_loop(0, gz, slab, 0, unroll=gz <= 8)


def split_dot(x, high, low):
    top = x.astype(bf16)
    rest = (x - top.astype(f32)).astype(bf16)
    out = jnp.dot(top, low, preferred_element_type=f32) + jnp.dot(rest, high, preferred_element_type=f32)
    return out + jnp.dot(top, high, preferred_element_type=f32)


def momentum_kernel(pa, where, velocity, viscosity, above, below, edge_left, edge_right, deposit, high, low, ustar, partial):
    columns = velocity.shape[2]
    radius = radii()
    arc = 1.0 / (radius * (2.0 * math.pi / NTH)) ** 2
    nu = viscosity[...]
    row = iota((NR, columns), 0)
    lane = iota((NR, columns), 1)

    def outward(x):
        return jnp.concatenate([x[1:], jnp.zeros_like(x[:1])], 0)

    def inward(x):
        return jnp.concatenate([jnp.zeros_like(x[:1]), x[:-1]], 0)

    def ahead(x, f):
        return jnp.where(lane == columns - 1, edge_right[:, f:f + 1], pltpu.roll(x, columns - 1, 1))

    def behind(x, f):
        return jnp.where(lane == 0, edge_left[:, 4 + f:5 + f], pltpu.roll(x, 1, 1))

    weights = [
        0.5 * (nu + above[3]),
        0.5 * (nu + below[3]),
        (radius + 0.5) / radius * 0.5 * (nu + outward(nu)),
        (radius - 0.5) / radius * 0.5 * (nu + inward(nu)),
        arc * 0.5 * (nu + ahead(nu, 3)),
        arc * 0.5 * (nu + behind(nu, 3)),
    ]
    new = []
    for c in range(3):
        u = velocity[c]
        sides = (above[c], below[c], outward(u), inward(u), ahead(u, c), behind(u, c))
        total = weights[0] * (sides[0] - u)
        for w, s in zip(weights[1:], sides[1:]):
            total = total + w * (s - u)
        new.append(u + STEP * (total + deposit[c]))
        ustar[c] = new[c]
    radial = new[1]
    flux = jnp.where(row == NR - 1, 0.0, (radius + 0.5) * 0.5 * (radial + outward(radial)))
    divergence = (flux - inward(flux)) / radius
    across = new[2] / (2.0 * (2.0 * math.pi / NTH) * radius)
    out = split_dot(jnp.concatenate([divergence, across], 1), high[0], low[0])
    for q in range(pa):
        partial[q] = out[:, q * columns:(q + 1) * columns]


def solve_kernel(gz, pa, second, partial, ratios, second_out, hat, came, held, send, recv, rsend, rrecv, gsend, grecv, lsem):
    me = lax.axis_index("gz")
    mp = lax.axis_index("pa")
    columns = partial.shape[2]
    load = pltpu.make_async_copy(ratios.at[mp], held, lsem)
    load.start()
    barrier = pltpu.get_barrier_semaphore()

    def greet(o):
        pl.semaphore_signal(barrier, inc=1, device_id=(lax.rem(me + o, gz), mp), device_id_type=MESH)

    loop(1, gz, greet)
    others = [lax.rem(mp + o, pa) for o in range(1, pa)]
    for q in others:
        pl.semaphore_signal(barrier, inc=1, device_id=(me, q), device_id_type=MESH)
    pl.semaphore_wait(barrier, gz + pa - 2)

    sums = [
        pltpu.make_async_remote_copy(
            src_ref=partial.at[q], dst_ref=came.at[i], send_sem=rsend.at[i], recv_sem=rrecv.at[i],
            device_id=(me, q), device_id_type=MESH)
        for i, q in enumerate(others)
    ]
    for c in sums:
        c.start()

    def copy(o):
        to = lax.rem(me + o, gz)
        return pltpu.make_async_remote_copy(
            src_ref=second.at[to], dst_ref=second_out.at[me], send_sem=send.at[o], recv_sem=recv.at[o],
            device_id=(to, mp), device_id_type=MESH)

    loop(1, gz, lambda o: copy(o).start())
    second_out[me] = second[me]
    load.wait()
    for c in sums:
        c.wait()
    x = partial[mp]
    for i in range(pa - 1):
        x = x + came[i]
    radius = radii()
    mean = jnp.sum(radius * x, axis=0, keepdims=True) * (1.0 / (NR * (NR + NR / 2)))
    x = x - jnp.where(iota((1, columns), 1) + mp * columns == 0, mean, 0.0)
    stride, n = 1, 0
    while stride < NR:
        pad = jnp.zeros((stride, columns), f32)
        lower = jnp.concatenate([pad, x[:-stride]], 0)
        upper = jnp.concatenate([x[stride:], pad], 0)
        x = x - held[n] * lower - held[n + 1] * upper
        stride, n = stride * 2, n + 2
    hat[mp] = x * held[n]
    spread = [
        pltpu.make_async_remote_copy(
            src_ref=hat.at[mp], dst_ref=hat.at[mp], send_sem=gsend.at[i], recv_sem=grecv.at[i],
            device_id=(me, q), device_id_type=MESH)
        for i, q in enumerate(others)
    ]
    for c in spread:
        c.start()
    for c in spread:
        c.wait()
    loop(1, gz, lambda o: copy(o).wait())


def finish_kernel(gz, pa, flat, where, hat, ustar, high, low, second, fluid, velocity_out, parcels_out):
    capacity = second.shape[2]
    x = jnp.concatenate([hat[q] for q in range(pa)], 1)
    slope = 0.5 * (jnp.concatenate([x[1:], x[-1:]], 0) - jnp.concatenate([x[:1], x[:-1]], 0))
    velocity_out[0] = ustar[0]
    velocity_out[1] = ustar[1] - split_dot(slope, high[0, 0], low[0, 0])
    turn = split_dot(x, high[0, 1], low[0, 1]) / (2.0 * (2.0 * math.pi / NTH) * radii())
    velocity_out[2] = ustar[2] - turn

    def slab(g, _):
        speed = fluid[g]
        for h in (0, 8):
            rows = second[g, h:h + 8]
            is_rate, rate = rates_of(rows)
            moved = (rows + STEP * rate * speed) / (1.0 + STEP * rate)
            rows = jnp.where(is_rate, rows, moved)
            if flat:
                parcels_out[h:h + 8, pl.ds(pl.multiple_of(g * capacity, 128), capacity)] = rows
            else:
                parcels_out[g, h:h + 8] = rows
        return 0

    lax.fori_loop(0, gz, slab, 0, unroll=gz <= 8)


def body(velocity, viscosity, parcels, dest_rank, dest_cell, counts):
    gz = lax.axis_size("gz")
    pa = lax.axis_size("pa")
    columns = viscosity.shape[2]
    block = parcels.shape[0]
    slots = 3 * block // gz
    capacity = -(-slots // 128) * 128
    flat = capacity == slots
    velocity = velocity.reshape(3, NR, columns)
    viscosity = viscosity.reshape(NR, columns)
    fields = jnp.concatenate([velocity, viscosity[None]], 0)
    above = lax.ppermute(fields, "gz", [(i + 1, i) for i in range(gz - 1)])
    below = lax.ppermute(fields, "gz", [(i, i + 1) for i in range(gz - 1)])
    edges = jnp.concatenate([fields[:, :, 0], fields[:, :, -1]], 0)

    def shape(*s):
        return jax.ShapeDtypeStruct(s, f32)

    plain = pltpu.CompilerParams(vmem_limit_bytes=LIMIT)
    first, second = pl.pallas_call(
        functools.partial(pack_kernel, gz, capacity),
        out_shape=(shape(gz, 8, capacity), shape(gz, 16, capacity)),
        in_specs=[pl.BlockSpec(memory_space=pltpu.SMEM), VM, VM, VM],
        out_specs=(VM, VM),
        compiler_params=plain,
        name="pack",
    )(counts, dest_rank.reshape(1, block), dest_cell.reshape(1, block), parcels.T)
    dma = pltpu.SemaphoreType.DMA
    first, edge_left, edge_right = pl.pallas_call(
        functools.partial(route_kernel, gz, pa),
        out_shape=(shape(gz, 8, capacity), shape(8, NR), shape(8, NR)),
        in_specs=[VM, VM],
        out_specs=(VM, VM, VM),
        scratch_shapes=[dma((gz,)), dma((gz,)), dma((2,)), dma((2,))],
        compiler_params=pltpu.CompilerParams(collective_id=0, has_side_effects=True, vmem_limit_bytes=LIMIT),
        name="route",
    )(first, edges)
    fluid, deposit = pl.pallas_call(
        functools.partial(deposit_kernel, gz),
        out_shape=(shape(gz, 8, capacity), shape(3, NR, columns)),
        in_specs=[VM, VM],
        out_specs=(VM, VM),
        compiler_params=plain,
        name="deposit",
    )(first, velocity)
    where = lax.axis_index("pa").astype(jnp.int32).reshape(1)
    high, low = forward_table(pa)
    chosen = pl.BlockSpec((1, 2 * columns, NTH), lambda i, w: (w[0], 0, 0))
    ustar, partial = pl.pallas_call(
        functools.partial(momentum_kernel, pa),
        out_shape=(shape(3, NR, columns), shape(pa, NR, columns)),
        grid_spec=pltpu.PrefetchScalarGridSpec(
            num_scalar_prefetch=1, grid=(1,),
            in_specs=[VM] * 7 + [chosen, chosen],
            out_specs=(VM, VM)),
        compiler_params=plain,
        name="momentum",
    )(where, velocity, viscosity, above, below, edge_left.T, edge_right.T, deposit, high, low)
    ratios = radial_ratios(pa)
    second, hat = pl.pallas_call(
        functools.partial(solve_kernel, gz, pa),
        out_shape=(shape(gz, 16, capacity), shape(pa, NR, columns)),
        in_specs=[VM, VM, pl.BlockSpec(memory_space=pl.ANY)],
        out_specs=(VM, VM),
        scratch_shapes=[
            pltpu.VMEM((pa - 1, NR, columns), f32), pltpu.VMEM(ratios.shape[1:], f32),
            dma((gz,)), dma((gz,)), dma((pa - 1,)), dma((pa - 1,)), dma((pa - 1,)), dma((pa - 1,)), dma(()),
        ],
        compiler_params=pltpu.CompilerParams(collective_id=1, has_side_effects=True, vmem_limit_bytes=LIMIT),
        name="solve",
    )(second, partial, ratios)
    high, low = inverse_table(pa)
    chosen = pl.BlockSpec((1, 2, NTH, columns), lambda i, w: (w[0], 0, 0, 0))
    velocity_out, parcels_out = pl.pallas_call(
        functools.partial(finish_kernel, gz, pa, flat),
        out_shape=(shape(3, NR, columns), shape(16, gz * slots) if flat else shape(gz, 16, capacity)),
        grid_spec=pltpu.PrefetchScalarGridSpec(
            num_scalar_prefetch=1, grid=(1,),
            in_specs=[VM, VM, chosen, chosen, VM, VM],
            out_specs=(VM, VM)),
        compiler_params=plain,
        name="finish",
    )(where, hat, ustar, high, low, second, fluid)
    if not flat:
        parcels_out = parcels_out[:, :, :slots].transpose(1, 0, 2).reshape(16, gz * slots)
    return velocity_out.reshape(3, 1, NR, columns), parcels_out.T


def solution(mesh):
    in_specs = (
        P(None, "gz", None, "pa"),
        P("gz", None, "pa"),
        P(("gz", "pa"), None),
        P(("gz", "pa"), None),
        P(("gz", "pa")),
        P(("gz", "pa")),
    )
    out_specs = (P(None, "gz", None, "pa"), P(("gz", "pa"), None))
    return jax.shard_map(body, mesh=mesh, in_specs=in_specs, out_specs=out_specs, check_vma=False)
```

```python
import functools
import math

import jax
import jax.numpy as jnp
import ml_dtypes
import numpy as np
from jax import lax
from jax.experimental import pallas as pl
from jax.experimental.pallas import tpu as pltpu
from jax.sharding import PartitionSpec as P

NR = 192
NTH = 512
STEP = 0.1
SHIFT = 0.0001
LIMIT = 56 * 1024 * 1024
MESH = pl.DeviceIdType.MESH
f32 = jnp.float32
bf16 = jnp.bfloat16
VM = pl.BlockSpec(memory_space=pltpu.VMEM)


def cas(n):
    x = 2.0 * np.pi / NTH * (n % NTH)
    return np.cos(x) + np.sin(x)


def halves(table):
    high = table.astype(np.float32).astype(ml_dtypes.bfloat16)
    low = (table - high.astype(np.float64)).astype(np.float32).astype(ml_dtypes.bfloat16)
    return high, low


@functools.lru_cache(None)
def forward_table(pa):
    columns = NTH // pa
    k = np.arange(NTH)[None, :]
    j = np.arange(NTH)[:, None]
    same = -cas(k * j)
    beside = -(cas(k * (j - 1)) - cas(k * (j + 1)))
    both = [np.concatenate([same[p * columns:(p + 1) * columns], beside[p * columns:(p + 1) * columns]], 0) for p in range(pa)]
    return halves(np.stack(both))


@functools.lru_cache(None)
def inverse_table(pa):
    columns = NTH // pa
    k = np.arange(NTH)[:, None]
    j = np.arange(NTH)[None, :]
    same = cas(k * j) / NTH
    beside = (cas(k * (j + 1)) - cas(k * (j - 1))) / NTH
    parts = []
    for p in range(pa):
        part = slice(p * columns, (p + 1) * columns)
        parts.append(np.stack([same[:, part], beside[:, part]]))
    return halves(np.stack(parts))


@functools.lru_cache(None)
def radial_ratios(pa):
    radius = NR + np.arange(NR) + 0.5
    step = 2.0 * np.pi / NTH
    arc = 1.0 / (radius * step) ** 2
    up = (radius + 0.5) / radius
    down = (radius - 0.5) / radius
    up[-1] = 0.0
    down[0] = 0.0
    k = np.arange(NTH)
    diagonal = SHIFT + arc[:, None] * (2.0 - 2.0 * np.cos(step * k))[None, :] + up[:, None] + down[:, None]
    lower = np.broadcast_to(-down[:, None], diagonal.shape)
    upper = np.broadcast_to(-up[:, None], diagonal.shape)

    def moved(x, s, fill):
        pad = np.full((abs(s), NTH), fill)
        return np.concatenate([pad, x[:-s]], 0) if s > 0 else np.concatenate([x[-s:], pad], 0)

    out = []
    stride = 1
    while stride < NR:
        low = lower / moved(diagonal, stride, 1.0)
        high = upper / moved(diagonal, -stride, 1.0)
        out += [low, high]
        diagonal = diagonal - low * moved(upper, stride, 0.0) - high * moved(lower, -stride, 0.0)
        lower = -low * moved(lower, stride, 0.0)
        upper = -high * moved(upper, -stride, 0.0)
        stride *= 2
    out.append(1.0 / diagonal)
    whole = np.stack(out).astype(np.float32)
    columns = NTH // pa
    return np.stack([whole[:, :, p * columns:(p + 1) * columns] for p in range(pa)])


def iota(shape, axis):
    return lax.broadcasted_iota(jnp.int32, shape, axis)


def radii():
    return (iota((NR, 1), 0) + NR).astype(f32) + 0.5


def rolled(x, s):
    return jnp.concatenate([x[s:], x[:s]], 0)


def rates_of(x):
    is_rate = iota(x.shape, 0) % 4 == 3
    w = jnp.where(is_rate, x, 0.0)
    return is_rate, w + rolled(w, 1) + rolled(w, 2) + rolled(w, 3)


def loop(first, last, step):
    if last - first <= 8:
        for i in range(first, last):
            step(i)
    else:
        lax.fori_loop(first, last, lambda i, _: (step(i), 0)[1], 0)


def pack(gz, counts, rank, cell, parcels, first, second):
    block = rank.shape[1]
    capacity = first.shape[2]
    tiles = capacity // 128
    live = iota((1, block), 1) < counts[0]
    target = jnp.where(live, rank[...], gz)
    marks = (iota((gz, block), 0) == target).astype(f32)
    earlier = (iota((128, 128), 0) < iota((128, 128), 1)).astype(f32).astype(bf16)
    carry = jnp.zeros((gz, 1), f32)
    slots = []
    for b in range(block // 128):
        part = marks[:, 128 * b:128 * b + 128]
        before = jnp.dot(part.astype(bf16), earlier, preferred_element_type=f32) + carry
        slots.append(jnp.sum(before * part, axis=0, keepdims=True))
        carry = carry + jnp.sum(part, axis=1, keepdims=True)
    slot = jnp.concatenate(slots, 1).astype(jnp.int32)
    place = jnp.where(live, target * capacity + slot, -1)
    high = place >> 7
    low = place & 127
    low_hot = (iota((128, block), 0) == low).astype(f32).astype(bf16)
    values = parcels[...]
    one = values.astype(bf16).astype(f32)
    two = (values - one).astype(bf16).astype(f32)
    three = values - one - two
    cells = cell[...]
    line = ((cells >> 7) + 1).astype(f32)
    column = (cells & 127).astype(f32)
    table = jnp.concatenate([one, two, three, line, column, jnp.zeros((14, block), f32)], 0)

    def slab(g):
        left = [jnp.where(high == g * tiles + i, table, 0.0).astype(bf16) for i in range(tiles)]
        got = lax.dot_general(jnp.concatenate(left, 0), low_hot, (((1,), (1,)), ((), ())), preferred_element_type=f32)
        for i in range(tiles):
            r = got[64 * i:64 * i + 64]
            rows = r[0:16] + r[16:32] + r[32:48]
            lanes = slice(128 * i, 128 * i + 128)
            second[g, :, lanes] = rows
            code = r[48:49] * 128.0 + r[49:50]
            total = 0.0
            for half in (rows[0:8], rows[8:16]):
                is_rate, rate = rates_of(half)
                weight = rate / (1.0 + STEP * rate)
                total = total + jnp.where(is_rate, weight, weight * half)
            total = total + rolled(total, 4)
            first[g, :, lanes] = jnp.where(iota(total.shape, 0) == 4, code, total)

    loop(0, gz, slab)


def deposit_slab(g, came, turned, fluid, deposit):
    columns = deposit.shape[2]
    rows = came[g]
    capacity = rows.shape[1]
    code = rows[4:5].astype(jnp.int32)
    line = (code >> 7) - 1
    column = code & 127
    line_hot = (iota((NR, capacity), 0) == line).astype(f32).astype(bf16)
    column_hot = iota((columns, capacity), 0) == column
    picked = jnp.dot(turned, line_hot, preferred_element_type=f32)
    looked, pushes = [], []
    for c in range(3):
        both = picked[2 * c * columns:(2 * c + 1) * columns] + picked[(2 * c + 1) * columns:(2 * c + 2) * columns]
        speed = jnp.sum(jnp.where(column_hot, both, 0.0), axis=0, keepdims=True)
        drag = (rows[c:c + 1] - speed * rows[3:4]).astype(bf16).astype(f32)
        looked.append(speed)
        pushes.append(jnp.where(column_hot, drag, 0.0).astype(bf16))
    nothing = jnp.zeros_like(looked[0])
    fluid[g] = jnp.concatenate((looked + [nothing]) * 2, 0)
    added = lax.dot_general(line_hot, jnp.concatenate(pushes, 0), (((1,), (1,)), ((), ())), preferred_element_type=f32)
    for c in range(3):
        deposit[c] += added[:, c * columns:(c + 1) * columns]


def split_dot(x, high, low):
    top = x.astype(bf16)
    rest = (x - top.astype(f32)).astype(bf16)
    out = jnp.dot(top, low, preferred_element_type=f32) + jnp.dot(rest, high, preferred_element_type=f32)
    return out + jnp.dot(top, high, preferred_element_type=f32)


def momentum(pa, speeds, viscosity, above, below, edge_left, edge_right, deposit, high, low, ustar, partial):
    columns = speeds.shape[2]
    radius = radii()
    arc = 1.0 / (radius * (2.0 * math.pi / NTH)) ** 2
    nu = viscosity[...]
    row = iota((NR, columns), 0)
    lane = iota((NR, columns), 1)

    def outward(x):
        return jnp.concatenate([x[1:], jnp.zeros_like(x[:1])], 0)

    def inward(x):
        return jnp.concatenate([jnp.zeros_like(x[:1]), x[:-1]], 0)

    def ahead(x, f):
        return jnp.where(lane == columns - 1, edge_right[:, f:f + 1], pltpu.roll(x, columns - 1, 1))

    def behind(x, f):
        return jnp.where(lane == 0, edge_left[:, 4 + f:5 + f], pltpu.roll(x, 1, 1))

    weights = [
        0.5 * (nu + above[3]),
        0.5 * (nu + below[3]),
        (radius + 0.5) / radius * 0.5 * (nu + outward(nu)),
        (radius - 0.5) / radius * 0.5 * (nu + inward(nu)),
        arc * 0.5 * (nu + ahead(nu, 3)),
        arc * 0.5 * (nu + behind(nu, 3)),
    ]
    new = []
    for c in range(3):
        u = speeds[c]
        sides = (above[c], below[c], outward(u), inward(u), ahead(u, c), behind(u, c))
        total = weights[0] * (sides[0] - u)
        for w, s in zip(weights[1:], sides[1:]):
            total = total + w * (s - u)
        new.append(u + STEP * (total + deposit[c]))
        ustar[c] = new[c]
    radial = new[1]
    flux = jnp.where(row == NR - 1, 0.0, (radius + 0.5) * 0.5 * (radial + outward(radial)))
    divergence = (flux - inward(flux)) / radius
    across = new[2] / (2.0 * (2.0 * math.pi / NTH) * radius)
    out = split_dot(jnp.concatenate([divergence, across], 1), high[...], low[...])
    for q in range(pa):
        partial[q] = out[:, q * columns:(q + 1) * columns]


def main_kernel(gz, pa, counts, rank_in, cell_in, parcels_in, velocity, viscosity, high_in, low_in, ratios,
                ustar, hat, second_in, fluid,
                rank, cell, parcels, speeds, nu, high, low, held, first, second, first_in,
                above, below, edges, edge_left, edge_right, deposit, partial, came,
                lsem, fsend, frecv, send, recv, zsend, zrecv, esend, erecv, rsend, rrecv, gsend, grecv):
    me = lax.axis_index("gz")
    mp = lax.axis_index("pa")
    columns = nu.shape[1]
    loads = [
        pltpu.make_async_copy(a, b, lsem.at[i])
        for i, (a, b) in enumerate((
            (rank_in, rank), (cell_in, cell), (parcels_in, parcels), (velocity, speeds), (viscosity.at[0], nu),
            (high_in.at[mp], high), (low_in.at[mp], low), (ratios.at[mp], held)))
    ]
    for c in loads:
        c.start()
    barrier = pltpu.get_barrier_semaphore()

    def greet(o):
        pl.semaphore_signal(barrier, inc=1, device_id=(lax.rem(me + o, gz), mp), device_id_type=MESH)

    loop(1, gz, greet)
    others = [lax.rem(mp + o, pa) for o in range(1, pa)]
    for q in others:
        pl.semaphore_signal(barrier, inc=1, device_id=(me, q), device_id_type=MESH)
    for c in loads[:5]:
        c.wait()
    pack(gz, counts, rank, cell, parcels, first, second)
    pl.semaphore_wait(barrier, gz + pa - 2)

    def slab_copy(source, target, ssem, rsem, o):
        to = lax.rem(me + o, gz)
        return pltpu.make_async_remote_copy(
            src_ref=source.at[to], dst_ref=target.at[me], send_sem=ssem.at[o], recv_sem=rsem.at[o],
            device_id=(to, mp), device_id_type=MESH)

    def first_copy(o):
        return slab_copy(first, first_in, fsend, frecv, o)

    def second_copy(o):
        return slab_copy(second, second_in, send, recv, o)

    loop(1, gz, lambda o: first_copy(o).start())

    def plane(source, target, part, i, to):
        return pltpu.make_async_remote_copy(
            src_ref=source, dst_ref=target.at[part], send_sem=zsend.at[i], recv_sem=zrecv.at[i],
            device_id=(to, mp), device_id_type=MESH)

    up, down = lax.rem(me + 1, gz), lax.rem(me + gz - 1, gz)
    to_up = [plane(velocity, below, pl.ds(0, 3), 0, up), plane(viscosity, below, pl.ds(3, 1), 1, up)]
    to_down = [plane(velocity, above, pl.ds(0, 3), 2, down), plane(viscosity, above, pl.ds(3, 1), 3, down)]

    @pl.when(me < gz - 1)
    def _():
        for c in to_up:
            c.start()

    @pl.when(me > 0)
    def _():
        for c in to_down:
            c.start()

    pieces, ends = [], []
    for c in range(3):
        turned = speeds[c].T
        top = turned.astype(bf16)
        pieces += [top, (turned - top.astype(f32)).astype(bf16)]
        ends.append(turned)
    ends.append(nu[...].T)
    edges[...] = jnp.concatenate([x[:1] for x in ends] + [x[columns - 1:] for x in ends], 0)
    right, left = lax.rem(mp + 1, pa), lax.rem(mp + pa - 1, pa)
    sides = [
        pltpu.make_async_remote_copy(
            src_ref=edges, dst_ref=target, send_sem=esend.at[i], recv_sem=erecv.at[i],
            device_id=(me, q), device_id_type=MESH)
        for i, (target, q) in enumerate(((edge_left, right), (edge_right, left)))
    ]
    for c in sides:
        c.start()
    loop(1, gz, lambda o: second_copy(o).start())
    turned = jnp.concatenate(pieces, 0)
    deposit[...] = jnp.zeros_like(deposit)
    first_in[me] = first[me]
    second_in[me] = second[me]
    deposit_slab(me, first_in, turned, fluid, deposit)

    def take(o):
        first_copy(o).wait()
        deposit_slab(lax.rem(me + gz - o, gz), first_in, turned, fluid, deposit)

    loop(1, gz, take)
    for c in sides:
        c.wait()
    for c in loads[5:]:
        c.wait()

    @pl.when(me < gz - 1)
    def _():
        for c in to_up:
            c.wait_send()
        for c in to_down:
            c.wait_recv()

    @pl.when(me == gz - 1)
    def _():
        above[...] = jnp.zeros_like(above)

    @pl.when(me > 0)
    def _():
        for c in to_down:
            c.wait_send()
        for c in to_up:
            c.wait_recv()

    @pl.when(me == 0)
    def _():
        below[...] = jnp.zeros_like(below)

    momentum(pa, speeds, nu, above, below, edge_left[...].T, edge_right[...].T, deposit, high, low, ustar, partial)
    sums = [
        pltpu.make_async_remote_copy(
            src_ref=partial.at[q], dst_ref=came.at[i], send_sem=rsend.at[i], recv_sem=rrecv.at[i],
            device_id=(me, q), device_id_type=MESH)
        for i, q in enumerate(others)
    ]
    for c in sums:
        c.start()
    for c in sums:
        c.wait()
    x = partial[mp]
    for i in range(pa - 1):
        x = x + came[i]
    radius = radii()
    mean = jnp.sum(radius * x, axis=0, keepdims=True) * (1.0 / (NR * (NR + NR / 2)))
    x = x - jnp.where(iota((1, columns), 1) + mp * columns == 0, mean, 0.0)
    stride, n = 1, 0
    while stride < NR:
        pad = jnp.zeros((stride, columns), f32)
        lower = jnp.concatenate([pad, x[:-stride]], 0)
        upper = jnp.concatenate([x[stride:], pad], 0)
        x = x - held[n] * lower - held[n + 1] * upper
        stride, n = stride * 2, n + 2
    hat[mp] = x * held[n]
    spread = [
        pltpu.make_async_remote_copy(
            src_ref=hat.at[mp], dst_ref=hat.at[mp], send_sem=gsend.at[i], recv_sem=grecv.at[i],
            device_id=(me, q), device_id_type=MESH)
        for i, q in enumerate(others)
    ]
    for c in spread:
        c.start()
    for c in spread:
        c.wait()
    loop(1, gz, lambda o: second_copy(o).wait())


def finish_kernel(gz, pa, flat, where, hat, ustar, high, low, second, fluid, velocity_out, parcels_out):
    capacity = second.shape[2]
    x = jnp.concatenate([hat[q] for q in range(pa)], 1)
    slope = 0.5 * (jnp.concatenate([x[1:], x[-1:]], 0) - jnp.concatenate([x[:1], x[:-1]], 0))
    velocity_out[0] = ustar[0]
    velocity_out[1] = ustar[1] - split_dot(slope, high[0, 0], low[0, 0])
    turn = split_dot(x, high[0, 1], low[0, 1]) / (2.0 * (2.0 * math.pi / NTH) * radii())
    velocity_out[2] = ustar[2] - turn

    def slab(g, _):
        speed = fluid[g]
        for h in (0, 8):
            rows = second[g, h:h + 8]
            is_rate, rate = rates_of(rows)
            moved = (rows + STEP * rate * speed) / (1.0 + STEP * rate)
            rows = jnp.where(is_rate, rows, moved)
            if flat:
                parcels_out[h:h + 8, pl.ds(pl.multiple_of(g * capacity, 128), capacity)] = rows
            else:
                parcels_out[g, h:h + 8] = rows
        return 0

    lax.fori_loop(0, gz, slab, 0, unroll=gz <= 8)


def body(velocity, viscosity, parcels, dest_rank, dest_cell, counts):
    gz = lax.axis_size("gz")
    pa = lax.axis_size("pa")
    columns = viscosity.shape[2]
    block = parcels.shape[0]
    slots = 3 * block // gz
    capacity = -(-slots // 128) * 128
    flat = capacity == slots
    velocity = velocity.reshape(3, NR, columns)

    def shape(*s):
        return jax.ShapeDtypeStruct(s, f32)

    plain = pltpu.CompilerParams(vmem_limit_bytes=LIMIT)
    dma = pltpu.SemaphoreType.DMA
    where = lax.axis_index("pa").astype(jnp.int32).reshape(1)
    high, low = forward_table(pa)
    ratios = radial_ratios(pa)
    ANY = pl.BlockSpec(memory_space=pl.ANY)

    def hold(*s):
        return pltpu.VMEM(s, f32)

    ustar, hat, second, fluid = pl.pallas_call(
        functools.partial(main_kernel, gz, pa),
        out_shape=(shape(3, NR, columns), shape(pa, NR, columns), shape(gz, 16, capacity), shape(gz, 8, capacity)),
        in_specs=[pl.BlockSpec(memory_space=pltpu.SMEM)] + [ANY] * 8,
        out_specs=(VM,) * 4,
        scratch_shapes=[
            pltpu.VMEM((1, block), jnp.int32), pltpu.VMEM((1, block), jnp.int32), hold(16, block),
            hold(3, NR, columns), hold(NR, columns),
            pltpu.VMEM((2 * columns, NTH), bf16), pltpu.VMEM((2 * columns, NTH), bf16), hold(*ratios.shape[1:]),
            hold(gz, 8, capacity), hold(gz, 16, capacity), hold(gz, 8, capacity),
            hold(4, NR, columns), hold(4, NR, columns), hold(8, NR), hold(8, NR), hold(8, NR),
            hold(3, NR, columns), hold(pa, NR, columns), hold(pa - 1, NR, columns),
            dma((8,)), dma((gz,)), dma((gz,)), dma((gz,)), dma((gz,)), dma((4,)), dma((4,)), dma((2,)), dma((2,)),
            dma((pa - 1,)), dma((pa - 1,)), dma((pa - 1,)), dma((pa - 1,)),
        ],
        compiler_params=pltpu.CompilerParams(collective_id=0, has_side_effects=True, vmem_limit_bytes=LIMIT),
        name="step",
    )(counts, dest_rank.reshape(1, block), dest_cell.reshape(1, block), parcels.T, velocity,
      viscosity, high, low, ratios)
    high, low = inverse_table(pa)
    chosen = pl.BlockSpec((1, 2, NTH, columns), lambda i, w: (w[0], 0, 0, 0))
    velocity_out, parcels_out = pl.pallas_call(
        functools.partial(finish_kernel, gz, pa, flat),
        out_shape=(shape(3, NR, columns), shape(16, gz * slots) if flat else shape(gz, 16, capacity)),
        grid_spec=pltpu.PrefetchScalarGridSpec(
            num_scalar_prefetch=1, grid=(1,),
            in_specs=[VM, VM, chosen, chosen, VM, VM],
            out_specs=(VM, VM)),
        compiler_params=plain,
        name="finish",
    )(where, hat, ustar, high, low, second, fluid)
    if not flat:
        parcels_out = parcels_out[:, :, :slots].transpose(1, 0, 2).reshape(16, gz * slots)
    return velocity_out.reshape(3, 1, NR, columns), parcels_out.T


def solution(mesh):
    in_specs = (
        P(None, "gz", None, "pa"),
        P("gz", None, "pa"),
        P(("gz", "pa"), None),
        P(("gz", "pa"), None),
        P(("gz", "pa")),
        P(("gz", "pa")),
    )
    out_specs = (P(None, "gz", None, "pa"), P(("gz", "pa"), None))
    return jax.shard_map(body, mesh=mesh, in_specs=in_specs, out_specs=out_specs, check_vma=False)
```

```python
import functools
import math

import jax
import jax.numpy as jnp
import ml_dtypes
import numpy as np
from jax import lax
from jax.experimental import pallas as pl
from jax.experimental.pallas import tpu as pltpu
from jax.sharding import PartitionSpec as P

NR = 192
NTH = 512
STEP = 0.1
SHIFT = 0.0001
LIMIT = 56 * 1024 * 1024
MESH = pl.DeviceIdType.MESH
f32 = jnp.float32
bf16 = jnp.bfloat16
VM = pl.BlockSpec(memory_space=pltpu.VMEM)


def cas(n):
    x = 2.0 * np.pi / NTH * (n % NTH)
    return np.cos(x) + np.sin(x)


def halves(table):
    high = table.astype(np.float32).astype(ml_dtypes.bfloat16)
    low = (table - high.astype(np.float64)).astype(np.float32).astype(ml_dtypes.bfloat16)
    return high, low


@functools.lru_cache(None)
def forward_table(pa):
    columns = NTH // pa
    k = np.arange(NTH)[None, :]
    j = np.arange(NTH)[:, None]
    same = -cas(k * j)
    beside = -(cas(k * (j - 1)) - cas(k * (j + 1)))
    both = [np.concatenate([same[p * columns:(p + 1) * columns], beside[p * columns:(p + 1) * columns]], 0) for p in range(pa)]
    return halves(np.stack(both))


@functools.lru_cache(None)
def inverse_table(pa):
    columns = NTH // pa
    k = np.arange(NTH)[:, None]
    j = np.arange(NTH)[None, :]
    same = cas(k * j) / NTH
    beside = (cas(k * (j + 1)) - cas(k * (j - 1))) / NTH
    parts = []
    for p in range(pa):
        part = slice(p * columns, (p + 1) * columns)
        parts.append(np.stack([same[:, part], beside[:, part]]))
    return halves(np.stack(parts))


@functools.lru_cache(None)
def radial_ratios(pa):
    radius = NR + np.arange(NR) + 0.5
    step = 2.0 * np.pi / NTH
    arc = 1.0 / (radius * step) ** 2
    up = (radius + 0.5) / radius
    down = (radius - 0.5) / radius
    up[-1] = 0.0
    down[0] = 0.0
    k = np.arange(NTH)
    diagonal = SHIFT + arc[:, None] * (2.0 - 2.0 * np.cos(step * k))[None, :] + up[:, None] + down[:, None]
    lower = np.broadcast_to(-down[:, None], diagonal.shape)
    upper = np.broadcast_to(-up[:, None], diagonal.shape)

    def moved(x, s, fill):
        pad = np.full((abs(s), NTH), fill)
        return np.concatenate([pad, x[:-s]], 0) if s > 0 else np.concatenate([x[-s:], pad], 0)

    out = []
    stride = 1
    while stride < NR:
        low = lower / moved(diagonal, stride, 1.0)
        high = upper / moved(diagonal, -stride, 1.0)
        out += [low, high]
        diagonal = diagonal - low * moved(upper, stride, 0.0) - high * moved(lower, -stride, 0.0)
        lower = -low * moved(lower, stride, 0.0)
        upper = -high * moved(upper, -stride, 0.0)
        stride *= 2
    out.append(1.0 / diagonal)
    whole = np.stack(out).astype(np.float32)
    columns = NTH // pa
    return np.stack([whole[:, :, p * columns:(p + 1) * columns] for p in range(pa)])


def iota(shape, axis):
    return lax.broadcasted_iota(jnp.int32, shape, axis)


def radii():
    return (iota((NR, 1), 0) + NR).astype(f32) + 0.5


def rolled(x, s):
    return jnp.concatenate([x[s:], x[:s]], 0)


def rates_of(x):
    is_rate = iota(x.shape, 0) % 4 == 3
    w = jnp.where(is_rate, x, 0.0)
    return is_rate, w + rolled(w, 1) + rolled(w, 2) + rolled(w, 3)


def loop(first, last, step):
    if last - first <= 8:
        for i in range(first, last):
            step(i)
    else:
        lax.fori_loop(first, last, lambda i, _: (step(i), 0)[1], 0)


def pack(gz, counts, rank, cell, parcels, first, second):
    block = rank.shape[1]
    capacity = first.shape[2]
    tiles = capacity // 128
    live = iota((1, block), 1) < counts[0]
    target = jnp.where(live, rank[...], gz)
    marks = (iota((gz, block), 0) == target).astype(f32)
    earlier = (iota((128, 128), 0) < iota((128, 128), 1)).astype(f32).astype(bf16)
    carry = jnp.zeros((gz, 1), f32)
    slots = []
    for b in range(block // 128):
        part = marks[:, 128 * b:128 * b + 128]
        before = jnp.dot(part.astype(bf16), earlier, preferred_element_type=f32) + carry
        slots.append(jnp.sum(before * part, axis=0, keepdims=True))
        carry = carry + jnp.sum(part, axis=1, keepdims=True)
    slot = jnp.concatenate(slots, 1).astype(jnp.int32)
    place = jnp.where(live, target * capacity + slot, -1)
    high = place >> 7
    low = place & 127
    low_hot = (iota((128, block), 0) == low).astype(f32).astype(bf16)
    values = parcels[...]
    one = values.astype(bf16).astype(f32)
    two = (values - one).astype(bf16).astype(f32)
    three = values - one - two
    cells = cell[...]
    line = ((cells >> 7) + 1).astype(f32)
    column = (cells & 127).astype(f32)
    table = jnp.concatenate([one, two, three, line, column, jnp.zeros((14, block), f32)], 0)

    def slab(g):
        left = [jnp.where(high == g * tiles + i, table, 0.0).astype(bf16) for i in range(tiles)]
        got = lax.dot_general(jnp.concatenate(left, 0), low_hot, (((1,), (1,)), ((), ())), preferred_element_type=f32)
        for i in range(tiles):
            r = got[64 * i:64 * i + 64]
            rows = r[0:16] + r[16:32] + r[32:48]
            lanes = slice(128 * i, 128 * i + 128)
            second[g, :, lanes] = rows
            code = r[48:49] * 128.0 + r[49:50]
            total = 0.0
            for half in (rows[0:8], rows[8:16]):
                is_rate, rate = rates_of(half)
                weight = rate / (1.0 + STEP * rate)
                total = total + jnp.where(is_rate, weight, weight * half)
            total = total + rolled(total, 4)
            first[g, :, lanes] = jnp.where(iota(total.shape, 0) == 4, code, total)

    loop(0, gz, slab)


def deposit_slab(g, came, turned, fluid, deposit):
    columns = deposit.shape[2]
    rows = came[g]
    capacity = rows.shape[1]
    code = rows[4:5].astype(jnp.int32)
    line = (code >> 7) - 1
    column = code & 127
    line_hot = (iota((NR, capacity), 0) == line).astype(f32).astype(bf16)
    column_hot = iota((columns, capacity), 0) == column
    picked = jnp.dot(turned, line_hot, preferred_element_type=f32)
    looked, pushes = [], []
    for c in range(3):
        both = picked[2 * c * columns:(2 * c + 1) * columns] + picked[(2 * c + 1) * columns:(2 * c + 2) * columns]
        speed = jnp.sum(jnp.where(column_hot, both, 0.0), axis=0, keepdims=True)
        drag = (rows[c:c + 1] - speed * rows[3:4]).astype(bf16).astype(f32)
        looked.append(speed)
        pushes.append(jnp.where(column_hot, drag, 0.0).astype(bf16))
    nothing = jnp.zeros_like(looked[0])
    fluid[g] = jnp.concatenate((looked + [nothing]) * 2, 0)
    added = lax.dot_general(line_hot, jnp.concatenate(pushes, 0), (((1,), (1,)), ((), ())), preferred_element_type=f32)
    for c in range(3):
        deposit[c] += added[:, c * columns:(c + 1) * columns]


def split_dot(x, high, low):
    top = x.astype(bf16)
    rest = (x - top.astype(f32)).astype(bf16)
    out = jnp.dot(top, low, preferred_element_type=f32) + jnp.dot(rest, high, preferred_element_type=f32)
    return out + jnp.dot(top, high, preferred_element_type=f32)


def momentum(pa, speeds, viscosity, near, far, far_ready, edge_left, edge_right, deposit, high, low, ustar, partial):
    columns = speeds.shape[2]
    radius = radii()
    arc = 1.0 / (radius * (2.0 * math.pi / NTH)) ** 2
    nu = viscosity[...]
    row = iota((NR, columns), 0)
    lane = iota((NR, columns), 1)

    def outward(x):
        return jnp.concatenate([x[1:], jnp.zeros_like(x[:1])], 0)

    def inward(x):
        return jnp.concatenate([jnp.zeros_like(x[:1]), x[:-1]], 0)

    def ahead(x, f):
        return jnp.where(lane == columns - 1, edge_right[:, f:f + 1], pltpu.roll(x, columns - 1, 1))

    def behind(x, f):
        return jnp.where(lane == 0, edge_left[:, 4 + f:5 + f], pltpu.roll(x, 1, 1))

    weights = [
        0.5 * (nu + near[3]),
        (radius + 0.5) / radius * 0.5 * (nu + outward(nu)),
        (radius - 0.5) / radius * 0.5 * (nu + inward(nu)),
        arc * 0.5 * (nu + ahead(nu, 3)),
        arc * 0.5 * (nu + behind(nu, 3)),
    ]
    for c in range(3):
        u = speeds[c]
        sides = (near[c], outward(u), inward(u), ahead(u, c), behind(u, c))
        total = weights[0] * (sides[0] - u)
        for w, s in zip(weights[1:], sides[1:]):
            total = total + w * (s - u)
        ustar[c] = u + STEP * (total + deposit[c])
    far_ready()
    weight = (0.5 * STEP) * (nu + far[3])
    new = [ustar[c] + weight * (far[c] - speeds[c]) for c in range(3)]
    for c in range(3):
        ustar[c] = new[c]
    radial = new[1]
    flux = jnp.where(row == NR - 1, 0.0, (radius + 0.5) * 0.5 * (radial + outward(radial)))
    divergence = (flux - inward(flux)) / radius
    across = new[2] / (2.0 * (2.0 * math.pi / NTH) * radius)
    out = split_dot(jnp.concatenate([divergence, across], 1), high[...], low[...])
    for q in range(pa):
        partial[q % 2, q // 2] = out[:, q * columns:(q + 1) * columns]


def main_kernel(gz, pa, counts, rank_in, cell_in, parcels_in, velocity, viscosity, high_in, low_in, ratios,
                ustar, hat, second_in, fluid,
                rank, cell, parcels, speeds, nu, high, low, held, first, second, first_in,
                near, far, edges, edge_left, edge_right, deposit, partial, came, rest,
                lsem, fsend, frecv, send, recv, zsend, zrecv, wsend, wrecv, esend, erecv, psend, precv, rsend, rrecv,
                gsend, grecv, hsend, hrecv):
    me = lax.axis_index("gz")
    mp = lax.axis_index("pa")
    columns = nu.shape[1]
    loads = [
        pltpu.make_async_copy(a, b, lsem.at[i])
        for i, (a, b) in enumerate((
            (rank_in, rank), (cell_in, cell), (parcels_in, parcels), (velocity, speeds), (viscosity.at[0], nu),
            (high_in.at[mp], high), (low_in.at[mp], low), (ratios.at[mp], held)))
    ]
    for c in loads:
        c.start()
    barrier = pltpu.get_barrier_semaphore()

    def greet(o):
        pl.semaphore_signal(barrier, inc=1, device_id=(lax.rem(me + o, gz), mp), device_id_type=MESH)

    loop(1, gz, greet)
    others = [lax.rem(mp + o, pa) for o in range(1, pa)]
    for q in others:
        pl.semaphore_signal(barrier, inc=1, device_id=(me, q), device_id_type=MESH)
    for c in loads[:5]:
        c.wait()
    pack(gz, counts, rank, cell, parcels, first, second)
    pl.semaphore_wait(barrier, gz + pa - 2)

    def slab_copy(source, target, ssem, rsem, o):
        to = lax.rem(me + o, gz)
        return pltpu.make_async_remote_copy(
            src_ref=source.at[to], dst_ref=target.at[me], send_sem=ssem.at[o], recv_sem=rsem.at[o],
            device_id=(to, mp), device_id_type=MESH)

    def first_copy(o):
        return slab_copy(first, first_in, fsend, frecv, o)

    def second_copy(o):
        return slab_copy(second, second_in, send, recv, o)

    loop(1, gz, lambda o: first_copy(o).start())

    odd = lax.rem(me, 2)
    mate = me + 1 - 2 * odd
    stride = 2 - 4 * odd
    beyond, behind = me + stride, me - stride
    has_beyond = jnp.logical_and(beyond >= 0, beyond < gz)
    has_behind = jnp.logical_and(behind >= 0, behind < gz)
    half = NR // 2
    spots = [(f, pl.ds(r, half)) for r in (0, half) for f in range(4)]

    def trade(i):
        f, rows = spots[i]
        source = velocity.at[f, rows] if f < 3 else viscosity.at[0, rows]
        return pltpu.make_async_remote_copy(
            src_ref=source, dst_ref=near.at[f, rows], send_sem=zsend.at[i], recv_sem=zrecv.at[i],
            device_id=(mate, mp), device_id_type=MESH)

    def hand_on(i):
        f, rows = spots[i]
        return pltpu.make_async_remote_copy(
            src_ref=near.at[f, rows], dst_ref=far.at[f, rows], send_sem=wsend.at[i], recv_sem=wrecv.at[i],
            device_id=(lax.rem(beyond + gz, gz), mp), device_id_type=MESH)

    for i in range(8):
        trade(i).start()

    def pass_on(i):
        trade(i).wait_recv()

        @pl.when(has_beyond)
        def _():
            hand_on(i).start()

    def far_ready():
        @pl.when(has_behind)
        def _():
            for i in range(8):
                hand_on(i).wait_recv()

        @pl.when(jnp.logical_not(has_behind))
        def _():
            far[...] = jnp.zeros_like(far)

    pieces, ends = [], []
    for c in range(3):
        turned = speeds[c].T
        top = turned.astype(bf16)
        pieces += [top, (turned - top.astype(f32)).astype(bf16)]
        ends.append(turned)
    ends.append(nu[...].T)
    edges[...] = jnp.concatenate([x[:1] for x in ends] + [x[columns - 1:] for x in ends], 0)
    right, left = lax.rem(mp + 1, pa), lax.rem(mp + pa - 1, pa)
    sides = [
        pltpu.make_async_remote_copy(
            src_ref=edges, dst_ref=target, send_sem=esend.at[i], recv_sem=erecv.at[i],
            device_id=(me, q), device_id_type=MESH)
        for i, (target, q) in enumerate(((edge_left, right), (edge_right, left)))
    ]
    for c in sides:
        c.start()
    turned = jnp.concatenate(pieces, 0)
    deposit[...] = jnp.zeros_like(deposit)
    first_in[me] = first[me]
    second_in[me] = second[me]
    deposit_slab(me, first_in, turned, fluid, deposit)

    def take(o):
        first_copy(o).wait()
        deposit_slab(lax.rem(me + gz - o, gz), first_in, turned, fluid, deposit)

    done = 1
    for i in range(8):
        upto = 1 + (i + 1) * (gz - 1) // 8
        loop(done, upto, take)
        done = upto
        pass_on(i)
    for c in sides:
        c.wait()
    for c in loads[5:]:
        c.wait()
    momentum(pa, speeds, nu, near, far, far_ready, edge_left[...].T, edge_right[...].T, deposit, high, low, ustar, partial)
    core = lax.rem(mp, 2)
    pair = mp + 1 - 2 * core
    place = mp // 2
    pairs = pa // 2
    order = [lax.rem(place + 1 + i, pairs) for i in range(pairs)]
    inner = [
        pltpu.make_async_remote_copy(
            src_ref=partial.at[1 - core, q], dst_ref=came.at[q], send_sem=psend.at[i], recv_sem=precv.at[i],
            device_id=(me, pair), device_id_type=MESH)
        for i, q in enumerate(order)
    ]
    for c in inner:
        c.start()
    outer = []
    for i, q in enumerate(order[:-1]):
        inner[i].wait_recv()
        came[q] = came[q] + partial[core, q]
        outer.append(pltpu.make_async_remote_copy(
            src_ref=came.at[q], dst_ref=rest.at[i], send_sem=rsend.at[i], recv_sem=rrecv.at[i],
            device_id=(me, 2 * q + core), device_id_type=MESH))
        outer[-1].start()
    loop(1, gz, lambda o: second_copy(o).start())
    inner[-1].wait_recv()
    x = partial[core, place] + came[place]
    for i, c in enumerate(outer):
        c.wait()
        x = x + rest[i]
    radius = radii()
    mean = jnp.sum(radius * x, axis=0, keepdims=True) * (1.0 / (NR * (NR + NR / 2)))
    x = x - jnp.where(iota((1, columns), 1) + mp * columns == 0, mean, 0.0)
    stride, n = 1, 0
    while stride < NR:
        pad = jnp.zeros((stride, columns), f32)
        lower = jnp.concatenate([pad, x[:-stride]], 0)
        upper = jnp.concatenate([x[stride:], pad], 0)
        x = x - held[n] * lower - held[n + 1] * upper
        stride, n = stride * 2, n + 2
    hat[mp] = x * held[n]
    spread = [
        pltpu.make_async_remote_copy(
            src_ref=hat.at[mp], dst_ref=hat.at[mp], send_sem=gsend.at[i], recv_sem=grecv.at[i],
            device_id=(me, q), device_id_type=MESH)
        for i, q in enumerate([2 * q + core for q in order[:-1]] + [pair])
    ]
    for c in spread:
        c.start()
    again = []
    for i in range(pairs - 1):
        q = 2 * lax.rem(place + 2 * pairs - 1 - i, pairs) + core
        spread[i].wait_recv()
        again.append(pltpu.make_async_remote_copy(
            src_ref=hat.at[q], dst_ref=hat.at[q], send_sem=hsend.at[i], recv_sem=hrecv.at[i],
            device_id=(me, pair), device_id_type=MESH))
        again[-1].start()
    spread[-1].wait_recv()
    for c in again:
        c.wait()
    for c in spread + inner:
        c.wait_send()
    for i in range(8):
        trade(i).wait_send()

    @pl.when(has_beyond)
    def _():
        for i in range(8):
            hand_on(i).wait_send()

    loop(1, gz, lambda o: second_copy(o).wait())


def finish_kernel(gz, pa, flat, where, hat, ustar, high, low, second, fluid, velocity_out, parcels_out):
    capacity = second.shape[2]
    x = jnp.concatenate([hat[q] for q in range(pa)], 1)
    slope = 0.5 * (jnp.concatenate([x[1:], x[-1:]], 0) - jnp.concatenate([x[:1], x[:-1]], 0))
    velocity_out[0] = ustar[0]
    velocity_out[1] = ustar[1] - split_dot(slope, high[0, 0], low[0, 0])
    turn = split_dot(x, high[0, 1], low[0, 1]) / (2.0 * (2.0 * math.pi / NTH) * radii())
    velocity_out[2] = ustar[2] - turn

    def slab(g, _):
        speed = fluid[g]
        for h in (0, 8):
            rows = second[g, h:h + 8]
            is_rate, rate = rates_of(rows)
            moved = (rows + STEP * rate * speed) / (1.0 + STEP * rate)
            rows = jnp.where(is_rate, rows, moved)
            if flat:
                parcels_out[h:h + 8, pl.ds(pl.multiple_of(g * capacity, 128), capacity)] = rows
            else:
                parcels_out[g, h:h + 8] = rows
        return 0

    lax.fori_loop(0, gz, slab, 0, unroll=gz <= 8)


def body(velocity, viscosity, parcels, dest_rank, dest_cell, counts):
    gz = lax.axis_size("gz")
    pa = lax.axis_size("pa")
    columns = viscosity.shape[2]
    block = parcels.shape[0]
    slots = 3 * block // gz
    capacity = -(-slots // 128) * 128
    flat = capacity == slots
    velocity = velocity.reshape(3, NR, columns)

    def shape(*s):
        return jax.ShapeDtypeStruct(s, f32)

    plain = pltpu.CompilerParams(vmem_limit_bytes=LIMIT)
    dma = pltpu.SemaphoreType.DMA
    where = lax.axis_index("pa").astype(jnp.int32).reshape(1)
    high, low = forward_table(pa)
    ratios = radial_ratios(pa)
    ANY = pl.BlockSpec(memory_space=pl.ANY)

    def hold(*s):
        return pltpu.VMEM(s, f32)

    ustar, hat, second, fluid = pl.pallas_call(
        functools.partial(main_kernel, gz, pa),
        out_shape=(shape(3, NR, columns), shape(pa, NR, columns), shape(gz, 16, capacity), shape(gz, 8, capacity)),
        in_specs=[pl.BlockSpec(memory_space=pltpu.SMEM)] + [ANY] * 8,
        out_specs=(VM,) * 4,
        scratch_shapes=[
            pltpu.VMEM((1, block), jnp.int32), pltpu.VMEM((1, block), jnp.int32), hold(16, block),
            hold(3, NR, columns), hold(NR, columns),
            pltpu.VMEM((2 * columns, NTH), bf16), pltpu.VMEM((2 * columns, NTH), bf16), hold(*ratios.shape[1:]),
            hold(gz, 8, capacity), hold(gz, 16, capacity), hold(gz, 8, capacity),
            hold(4, NR, columns), hold(4, NR, columns), hold(8, NR), hold(8, NR), hold(8, NR),
            hold(3, NR, columns), hold(2, pa // 2, NR, columns), hold(pa // 2, NR, columns), hold(pa // 2 - 1, NR, columns),
            dma((8,)), dma((gz,)), dma((gz,)), dma((gz,)), dma((gz,)), dma((8,)), dma((8,)), dma((8,)), dma((8,)),
            dma((2,)), dma((2,)), dma((pa // 2,)), dma((pa // 2,)), dma((pa // 2 - 1,)), dma((pa // 2 - 1,)),
            dma((pa // 2,)), dma((pa // 2,)), dma((pa // 2 - 1,)), dma((pa // 2 - 1,)),
        ],
        compiler_params=pltpu.CompilerParams(collective_id=0, has_side_effects=True, vmem_limit_bytes=LIMIT),
        name="step",
    )(counts, dest_rank.reshape(1, block), dest_cell.reshape(1, block), parcels.T, velocity,
      viscosity, high, low, ratios)
    high, low = inverse_table(pa)
    chosen = pl.BlockSpec((1, 2, NTH, columns), lambda i, w: (w[0], 0, 0, 0))
    velocity_out, parcels_out = pl.pallas_call(
        functools.partial(finish_kernel, gz, pa, flat),
        out_shape=(shape(3, NR, columns), shape(16, gz * slots) if flat else shape(gz, 16, capacity)),
        grid_spec=pltpu.PrefetchScalarGridSpec(
            num_scalar_prefetch=1, grid=(1,),
            in_specs=[VM, VM, chosen, chosen, VM, VM],
            out_specs=(VM, VM)),
        compiler_params=plain,
        name="finish",
    )(where, hat, ustar, high, low, second, fluid)
    if not flat:
        parcels_out = parcels_out[:, :, :slots].transpose(1, 0, 2).reshape(16, gz * slots)
    return velocity_out.reshape(3, 1, NR, columns), parcels_out.T


def solution(mesh):
    in_specs = (
        P(None, "gz", None, "pa"),
        P("gz", None, "pa"),
        P(("gz", "pa"), None),
        P(("gz", "pa"), None),
        P(("gz", "pa")),
        P(("gz", "pa")),
    )
    out_specs = (P(None, "gz", None, "pa"), P(("gz", "pa"), None))
    return jax.shard_map(body, mesh=mesh, in_specs=in_specs, out_specs=out_specs, check_vma=False)
```

```python
import functools
import math

import jax
import jax.numpy as jnp
import ml_dtypes
import numpy as np
from jax import lax
from jax.experimental import pallas as pl
from jax.experimental.pallas import tpu as pltpu
from jax.sharding import PartitionSpec as P

NR = 192
NTH = 512
STEP = 0.1
SHIFT = 0.0001
LIMIT = 56 * 1024 * 1024
MESH = pl.DeviceIdType.MESH
f32 = jnp.float32
bf16 = jnp.bfloat16
VM = pl.BlockSpec(memory_space=pltpu.VMEM)


def cas(n):
    x = 2.0 * np.pi / NTH * (n % NTH)
    return np.cos(x) + np.sin(x)


def halves(table):
    high = table.astype(np.float32).astype(ml_dtypes.bfloat16)
    low = (table - high.astype(np.float64)).astype(np.float32).astype(ml_dtypes.bfloat16)
    return high, low


@functools.lru_cache(None)
def forward_table(pa):
    columns = NTH // pa
    k = np.arange(NTH)[None, :]
    j = np.arange(NTH)[:, None]
    same = -cas(k * j)
    beside = -(cas(k * (j - 1)) - cas(k * (j + 1)))
    both = [np.concatenate([same[p * columns:(p + 1) * columns], beside[p * columns:(p + 1) * columns]], 0) for p in range(pa)]
    return halves(np.stack(both))


@functools.lru_cache(None)
def inverse_table(pa):
    columns = NTH // pa
    k = np.arange(NTH)[:, None]
    j = np.arange(NTH)[None, :]
    same = cas(k * j) / NTH
    beside = (cas(k * (j + 1)) - cas(k * (j - 1))) / NTH
    parts = []
    for p in range(pa):
        part = slice(p * columns, (p + 1) * columns)
        parts.append(np.stack([same[:, part], beside[:, part]]))
    return halves(np.stack(parts))


@functools.lru_cache(None)
def radial_ratios(pa):
    radius = NR + np.arange(NR) + 0.5
    step = 2.0 * np.pi / NTH
    arc = 1.0 / (radius * step) ** 2
    up = (radius + 0.5) / radius
    down = (radius - 0.5) / radius
    up[-1] = 0.0
    down[0] = 0.0
    k = np.arange(NTH)
    diagonal = SHIFT + arc[:, None] * (2.0 - 2.0 * np.cos(step * k))[None, :] + up[:, None] + down[:, None]
    lower = np.broadcast_to(-down[:, None], diagonal.shape)
    upper = np.broadcast_to(-up[:, None], diagonal.shape)

    def moved(x, s, fill):
        pad = np.full((abs(s), NTH), fill)
        return np.concatenate([pad, x[:-s]], 0) if s > 0 else np.concatenate([x[-s:], pad], 0)

    out = []
    stride = 1
    while stride < NR:
        low = lower / moved(diagonal, stride, 1.0)
        high = upper / moved(diagonal, -stride, 1.0)
        out += [low, high]
        diagonal = diagonal - low * moved(upper, stride, 0.0) - high * moved(lower, -stride, 0.0)
        lower = -low * moved(lower, stride, 0.0)
        upper = -high * moved(upper, -stride, 0.0)
        stride *= 2
    out.append(1.0 / diagonal)
    whole = np.stack(out).astype(np.float32)
    columns = NTH // pa
    return np.stack([whole[:, :, p * columns:(p + 1) * columns] for p in range(pa)])


def iota(shape, axis):
    return lax.broadcasted_iota(jnp.int32, shape, axis)


def radii():
    return (iota((NR, 1), 0) + NR).astype(f32) + 0.5


def rolled(x, s):
    return jnp.concatenate([x[s:], x[:s]], 0)


def rates_of(x):
    is_rate = iota(x.shape, 0) % 4 == 3
    w = jnp.where(is_rate, x, 0.0)
    return is_rate, w + rolled(w, 1) + rolled(w, 2) + rolled(w, 3)


def loop(first, last, step):
    if last - first <= 8:
        for i in range(first, last):
            step(i)
    else:
        lax.fori_loop(first, last, lambda i, _: (step(i), 0)[1], 0)


def pack(gz, counts, rank, cell, parcels, first, second):
    block = rank.shape[1]
    capacity = first.shape[2]
    tiles = capacity // 128
    live = iota((1, block), 1) < counts[0]
    target = jnp.where(live, rank[...], gz)
    marks = (iota((gz, block), 0) == target).astype(f32)
    earlier = (iota((128, 128), 0) < iota((128, 128), 1)).astype(f32).astype(bf16)
    carry = jnp.zeros((gz, 1), f32)
    slots = []
    for b in range(block // 128):
        part = marks[:, 128 * b:128 * b + 128]
        before = jnp.dot(part.astype(bf16), earlier, preferred_element_type=f32) + carry
        slots.append(jnp.sum(before * part, axis=0, keepdims=True))
        carry = carry + jnp.sum(part, axis=1, keepdims=True)
    slot = jnp.concatenate(slots, 1).astype(jnp.int32)
    place = jnp.where(live, target * capacity + slot, -1)
    high = place >> 7
    low = place & 127
    low_hot = (iota((128, block), 0) == low).astype(f32).astype(bf16)
    values = parcels[...]
    one = values.astype(bf16).astype(f32)
    two = (values - one).astype(bf16).astype(f32)
    three = values - one - two
    cells = cell[...]
    line = ((cells >> 7) + 1).astype(f32)
    column = (cells & 127).astype(f32)
    table = jnp.concatenate([one, two, three, line, column, jnp.zeros((14, block), f32)], 0)

    def slab(g):
        left = [jnp.where(high == g * tiles + i, table, 0.0).astype(bf16) for i in range(tiles)]
        got = lax.dot_general(jnp.concatenate(left, 0), low_hot, (((1,), (1,)), ((), ())), preferred_element_type=f32)
        for i in range(tiles):
            r = got[64 * i:64 * i + 64]
            rows = r[0:16] + r[16:32] + r[32:48]
            lanes = slice(128 * i, 128 * i + 128)
            second[g, :, lanes] = rows
            code = r[48:49] * 128.0 + r[49:50]
            total = 0.0
            for half in (rows[0:8], rows[8:16]):
                is_rate, rate = rates_of(half)
                weight = rate / (1.0 + STEP * rate)
                total = total + jnp.where(is_rate, weight, weight * half)
            total = total + rolled(total, 4)
            first[g, :, lanes] = jnp.where(iota(total.shape, 0) == 4, code, total)

    loop(0, gz, slab)


def deposit_slab(g, came, turned, fluid, deposit):
    columns = deposit.shape[2]
    rows = came[g]
    capacity = rows.shape[1]
    code = rows[4:5].astype(jnp.int32)
    line = (code >> 7) - 1
    column = code & 127
    line_hot = (iota((NR, capacity), 0) == line).astype(f32).astype(bf16)
    column_hot = iota((columns, capacity), 0) == column
    picked = jnp.dot(turned, line_hot, preferred_element_type=f32)
    looked, pushes = [], []
    for c in range(3):
        both = picked[2 * c * columns:(2 * c + 1) * columns] + picked[(2 * c + 1) * columns:(2 * c + 2) * columns]
        speed = jnp.sum(jnp.where(column_hot, both, 0.0), axis=0, keepdims=True)
        drag = (rows[c:c + 1] - speed * rows[3:4]).astype(bf16).astype(f32)
        looked.append(speed)
        pushes.append(jnp.where(column_hot, drag, 0.0).astype(bf16))
    nothing = jnp.zeros_like(looked[0])
    fluid[g] = jnp.concatenate((looked + [nothing]) * 2, 0)
    added = lax.dot_general(line_hot, jnp.concatenate(pushes, 0), (((1,), (1,)), ((), ())), preferred_element_type=f32)
    for c in range(3):
        deposit[c] += added[:, c * columns:(c + 1) * columns]


def split_dot(x, high, low):
    top = x.astype(bf16)
    rest = (x - top.astype(f32)).astype(bf16)
    out = jnp.dot(top, low, preferred_element_type=f32) + jnp.dot(rest, high, preferred_element_type=f32)
    return out + jnp.dot(top, high, preferred_element_type=f32)


def face_weights(viscosity, near, edge_left, edge_right):
    radius = radii()
    arc = 1.0 / (radius * (2.0 * math.pi / NTH)) ** 2
    nu = viscosity[...]
    return [
        0.5 * (nu + near[3]),
        (radius + 0.5) / radius * 0.5 * (nu + outward(nu)),
        (radius - 0.5) / radius * 0.5 * (nu + inward(nu)),
        arc * 0.5 * (nu + ahead(nu, edge_right[:, 3:4])),
        arc * 0.5 * (nu + behind(nu, edge_left[:, 7:8])),
    ]


def outward(x):
    return jnp.concatenate([x[1:], jnp.zeros_like(x[:1])], 0)


def inward(x):
    return jnp.concatenate([jnp.zeros_like(x[:1]), x[:-1]], 0)


def ahead(x, edge):
    columns = x.shape[1]
    return jnp.where(iota(x.shape, 1) == columns - 1, edge, pltpu.roll(x, columns - 1, 1))


def behind(x, edge):
    return jnp.where(iota(x.shape, 1) == 0, edge, pltpu.roll(x, 1, 1))


def most_of(c, speeds, near, edge_left, edge_right, deposit, weights):
    u = speeds[c]
    sides = (near[c], outward(u), inward(u), ahead(u, edge_right[:, c:c + 1]), behind(u, edge_left[:, 4 + c:5 + c]))
    total = deposit[c]
    for w, s in zip(weights, sides):
        total = total + w * (s - u)
    return u + STEP * total


def far_part(c, speeds, viscosity, far):
    return (0.5 * STEP) * (viscosity[...] + far[3]) * (far[c] - speeds[c])


def transform(pa, radial, azimuthal, high, low, partial):
    columns = radial.shape[1]
    radius = radii()
    flux = jnp.where(iota(radial.shape, 0) == NR - 1, 0.0, (radius + 0.5) * 0.5 * (radial + outward(radial)))
    divergence = (flux - inward(flux)) / radius
    across = azimuthal / (2.0 * (2.0 * math.pi / NTH) * radius)
    out = split_dot(jnp.concatenate([divergence, across], 1), high[...], low[...])
    for q in range(pa):
        partial[q % 2, q // 2] = out[:, q * columns:(q + 1) * columns]


def main_kernel(gz, pa, counts, rank_in, cell_in, parcels_in, velocity, viscosity, high_in, low_in, ratios,
                ustar, hat, second_in, fluid,
                rank, cell, parcels, speeds, nu, high, low, held, first, second, first_in,
                near, far, edges, edge_left, edge_right, deposit, partial, came, rest,
                lsem, fsend, frecv, send, recv, zsend, zrecv, wsend, wrecv, esend, erecv, psend, precv, rsend, rrecv,
                gsend, grecv, hsend, hrecv):
    me = lax.axis_index("gz")
    mp = lax.axis_index("pa")
    columns = nu.shape[1]
    loads = [
        pltpu.make_async_copy(a, b, lsem.at[i])
        for i, (a, b) in enumerate((
            (rank_in, rank), (cell_in, cell), (parcels_in, parcels), (velocity, speeds), (viscosity.at[0], nu),
            (high_in.at[mp], high), (low_in.at[mp], low), (ratios.at[mp], held)))
    ]
    for c in loads:
        c.start()
    barrier = pltpu.get_barrier_semaphore()

    def greet(o):
        pl.semaphore_signal(barrier, inc=1, device_id=(lax.rem(me + o, gz), mp), device_id_type=MESH)

    loop(1, gz, greet)
    others = [lax.rem(mp + o, pa) for o in range(1, pa)]
    for q in others:
        pl.semaphore_signal(barrier, inc=1, device_id=(me, q), device_id_type=MESH)

    def slab_copy(source, target, ssem, rsem, o):
        to = lax.rem(me + o, gz)
        return pltpu.make_async_remote_copy(
            src_ref=source.at[to], dst_ref=target.at[me], send_sem=ssem.at[o], recv_sem=rsem.at[o],
            device_id=(to, mp), device_id_type=MESH)

    def first_copy(o):
        return slab_copy(first, first_in, fsend, frecv, o)

    def second_copy(o):
        return slab_copy(second, second_in, send, recv, o)

    odd = lax.rem(me, 2)
    mate = me + 1 - 2 * odd
    stride = 2 - 4 * odd
    beyond, before = me + stride, me - stride
    has_beyond = jnp.logical_and(beyond >= 0, beyond < gz)
    has_before = jnp.logical_and(before >= 0, before < gz)
    half = NR // 2
    spots = [(f, pl.ds(r, half)) for r in (0, half) for f in (3, 1, 2)] + [(0, pl.ds(r, half)) for r in (0, half)]

    def trade(i):
        f, rows = spots[i]
        source = velocity.at[f, rows] if f < 3 else viscosity.at[0, rows]
        return pltpu.make_async_remote_copy(
            src_ref=source, dst_ref=near.at[f, rows], send_sem=zsend.at[i], recv_sem=zrecv.at[i],
            device_id=(mate, mp), device_id_type=MESH)

    def hand_on(i):
        f, rows = spots[i]
        return pltpu.make_async_remote_copy(
            src_ref=near.at[f, rows], dst_ref=far.at[f, rows], send_sem=wsend.at[i], recv_sem=wrecv.at[i],
            device_id=(lax.rem(beyond + gz, gz), mp), device_id_type=MESH)

    @pl.when(jnp.logical_not(has_before))
    def _():
        far[...] = jnp.zeros_like(far)

    pl.semaphore_wait(barrier, gz + pa - 2)
    for i in range(3):
        trade(i).start()
    for c in loads[:5]:
        c.wait()
    pack(gz, counts, rank, cell, parcels, first, second)
    loop(1, gz, lambda o: first_copy(o).start())
    for i in range(3, 6):
        trade(i).start()

    def pass_on(i):
        trade(i).wait_recv()

        @pl.when(has_beyond)
        def _():
            hand_on(i).start()

    def far_ready(numbers):
        @pl.when(has_before)
        def _():
            for i in numbers:
                hand_on(i).wait_recv()

    pieces, ends = [], []
    for c in range(3):
        turned = speeds[c].T
        top = turned.astype(bf16)
        pieces += [top, (turned - top.astype(f32)).astype(bf16)]
        ends.append(turned)
    ends.append(nu[...].T)
    edges[...] = jnp.concatenate([x[:1] for x in ends] + [x[columns - 1:] for x in ends], 0)
    right, left = lax.rem(mp + 1, pa), lax.rem(mp + pa - 1, pa)
    sides = [
        pltpu.make_async_remote_copy(
            src_ref=edges, dst_ref=target, send_sem=esend.at[i], recv_sem=erecv.at[i],
            device_id=(me, q), device_id_type=MESH)
        for i, (target, q) in enumerate(((edge_left, right), (edge_right, left)))
    ]
    for c in sides:
        c.start()
    for i in range(6, 8):
        trade(i).start()
    turned = jnp.concatenate(pieces, 0)
    deposit[...] = jnp.zeros_like(deposit)
    first_in[me] = first[me]
    second_in[me] = second[me]
    deposit_slab(me, first_in, turned, fluid, deposit)

    def take(o):
        first_copy(o).wait()
        deposit_slab(lax.rem(me + gz - o, gz), first_in, turned, fluid, deposit)

    done = 1
    for i in range(6):
        upto = 1 + (i + 1) * (gz - 1) // 6
        loop(done, upto, take)
        done = upto
        pass_on(i)
    for c in sides:
        c.wait()
    for c in loads[5:]:
        c.wait()
    edge_l, edge_r = edge_left[...].T, edge_right[...].T
    weights = face_weights(nu, near, edge_l, edge_r)
    for c in (1, 2):
        ustar[c] = most_of(c, speeds, near, edge_l, edge_r, deposit, weights)
    far_ready(range(6))
    radial, azimuthal = [ustar[c] + far_part(c, speeds, nu, far) for c in (1, 2)]
    ustar[1] = radial
    ustar[2] = azimuthal
    transform(pa, radial, azimuthal, high, low, partial)
    core = lax.rem(mp, 2)
    pair = mp + 1 - 2 * core
    place = mp // 2
    pairs = pa // 2
    order = [lax.rem(place + 1 + i, pairs) for i in range(pairs)]
    inner = [
        pltpu.make_async_remote_copy(
            src_ref=partial.at[1 - core, q], dst_ref=came.at[q], send_sem=psend.at[i], recv_sem=precv.at[i],
            device_id=(me, pair), device_id_type=MESH)
        for i, q in enumerate(order)
    ]
    for c in inner:
        c.start()
    outer = []
    for i, q in enumerate(order[:-1]):
        inner[i].wait_recv()
        came[q] = came[q] + partial[core, q]
        outer.append(pltpu.make_async_remote_copy(
            src_ref=came.at[q], dst_ref=rest.at[i], send_sem=rsend.at[i], recv_sem=rrecv.at[i],
            device_id=(me, 2 * q + core), device_id_type=MESH))
        outer[-1].start()
    for i in (6, 7):
        pass_on(i)
    loop(1, gz, lambda o: second_copy(o).start())
    weights = face_weights(nu, near, edge_l, edge_r)
    ustar[0] = most_of(0, speeds, near, edge_l, edge_r, deposit, weights)
    inner[-1].wait_recv()
    x = partial[core, place] + came[place]
    for i, c in enumerate(outer):
        c.wait()
        x = x + rest[i]
    radius = radii()
    mean = jnp.sum(radius * x, axis=0, keepdims=True) * (1.0 / (NR * (NR + NR / 2)))
    x = x - jnp.where(iota((1, columns), 1) + mp * columns == 0, mean, 0.0)
    stride, n = 1, 0
    while stride < NR:
        pad = jnp.zeros((stride, columns), f32)
        lower = jnp.concatenate([pad, x[:-stride]], 0)
        upper = jnp.concatenate([x[stride:], pad], 0)
        x = x - held[n] * lower - held[n + 1] * upper
        stride, n = stride * 2, n + 2
    hat[mp] = x * held[n]
    spread = [
        pltpu.make_async_remote_copy(
            src_ref=hat.at[mp], dst_ref=hat.at[mp], send_sem=gsend.at[i], recv_sem=grecv.at[i],
            device_id=(me, q), device_id_type=MESH)
        for i, q in enumerate([2 * q + core for q in order[:-1]] + [pair])
    ]
    for c in spread:
        c.start()
    far_ready((6, 7))
    ustar[0] = ustar[0] + far_part(0, speeds, nu, far)
    again = []
    for i in range(pairs - 1):
        q = 2 * lax.rem(place + 2 * pairs - 1 - i, pairs) + core
        spread[i].wait_recv()
        again.append(pltpu.make_async_remote_copy(
            src_ref=hat.at[q], dst_ref=hat.at[q], send_sem=hsend.at[i], recv_sem=hrecv.at[i],
            device_id=(me, pair), device_id_type=MESH))
        again[-1].start()
    spread[-1].wait_recv()
    for c in again:
        c.wait()
    for c in spread + inner:
        c.wait_send()
    for i in range(8):
        trade(i).wait_send()

    @pl.when(has_beyond)
    def _():
        for i in range(8):
            hand_on(i).wait_send()

    loop(1, gz, lambda o: second_copy(o).wait())


def finish_kernel(gz, pa, flat, where, hat, ustar, high, low, second, fluid, velocity_out, parcels_out):
    capacity = second.shape[2]
    x = jnp.concatenate([hat[q] for q in range(pa)], 1)
    slope = 0.5 * (jnp.concatenate([x[1:], x[-1:]], 0) - jnp.concatenate([x[:1], x[:-1]], 0))
    velocity_out[0] = ustar[0]
    velocity_out[1] = ustar[1] - split_dot(slope, high[0, 0], low[0, 0])
    turn = split_dot(x, high[0, 1], low[0, 1]) / (2.0 * (2.0 * math.pi / NTH) * radii())
    velocity_out[2] = ustar[2] - turn

    def slab(g, _):
        speed = fluid[g]
        for h in (0, 8):
            rows = second[g, h:h + 8]
            is_rate, rate = rates_of(rows)
            moved = (rows + STEP * rate * speed) / (1.0 + STEP * rate)
            rows = jnp.where(is_rate, rows, moved)
            if flat:
                parcels_out[h:h + 8, pl.ds(pl.multiple_of(g * capacity, 128), capacity)] = rows
            else:
                parcels_out[g, h:h + 8] = rows
        return 0

    lax.fori_loop(0, gz, slab, 0, unroll=gz <= 8)


def body(velocity, viscosity, parcels, dest_rank, dest_cell, counts):
    gz = lax.axis_size("gz")
    pa = lax.axis_size("pa")
    columns = viscosity.shape[2]
    block = parcels.shape[0]
    slots = 3 * block // gz
    capacity = -(-slots // 128) * 128
    flat = capacity == slots
    velocity = velocity.reshape(3, NR, columns)

    def shape(*s):
        return jax.ShapeDtypeStruct(s, f32)

    plain = pltpu.CompilerParams(vmem_limit_bytes=LIMIT)
    dma = pltpu.SemaphoreType.DMA
    where = lax.axis_index("pa").astype(jnp.int32).reshape(1)
    high, low = forward_table(pa)
    ratios = radial_ratios(pa)
    ANY = pl.BlockSpec(memory_space=pltpu.HBM)

    def hold(*s):
        return pltpu.VMEM(s, f32)

    ustar, hat, second, fluid = pl.pallas_call(
        functools.partial(main_kernel, gz, pa),
        out_shape=(shape(3, NR, columns), shape(pa, NR, columns), shape(gz, 16, capacity), shape(gz, 8, capacity)),
        in_specs=[pl.BlockSpec(memory_space=pltpu.SMEM)] + [ANY] * 8,
        out_specs=(VM,) * 4,
        scratch_shapes=[
            pltpu.VMEM((1, block), jnp.int32), pltpu.VMEM((1, block), jnp.int32), hold(16, block),
            hold(3, NR, columns), hold(NR, columns),
            pltpu.VMEM((2 * columns, NTH), bf16), pltpu.VMEM((2 * columns, NTH), bf16), hold(*ratios.shape[1:]),
            hold(gz, 8, capacity), hold(gz, 16, capacity), hold(gz, 8, capacity),
            hold(4, NR, columns), hold(4, NR, columns), hold(8, NR), hold(8, NR), hold(8, NR),
            hold(3, NR, columns), hold(2, pa // 2, NR, columns), hold(pa // 2, NR, columns), hold(pa // 2 - 1, NR, columns),
            dma((8,)), dma((gz,)), dma((gz,)), dma((gz,)), dma((gz,)), dma((8,)), dma((8,)), dma((8,)), dma((8,)),
            dma((2,)), dma((2,)), dma((pa // 2,)), dma((pa // 2,)), dma((pa // 2 - 1,)), dma((pa // 2 - 1,)),
            dma((pa // 2,)), dma((pa // 2,)), dma((pa // 2 - 1,)), dma((pa // 2 - 1,)),
        ],
        compiler_params=pltpu.CompilerParams(collective_id=0, has_side_effects=True, vmem_limit_bytes=LIMIT),
        name="step",
    )(counts, dest_rank.reshape(1, block), dest_cell.reshape(1, block), parcels.T, velocity,
      viscosity, high, low, ratios)
    high, low = inverse_table(pa)
    chosen = pl.BlockSpec((1, 2, NTH, columns), lambda i, w: (w[0], 0, 0, 0))
    velocity_out, parcels_out = pl.pallas_call(
        functools.partial(finish_kernel, gz, pa, flat),
        out_shape=(shape(3, NR, columns), shape(16, gz * slots) if flat else shape(gz, 16, capacity)),
        grid_spec=pltpu.PrefetchScalarGridSpec(
            num_scalar_prefetch=1, grid=(1,),
            in_specs=[VM, VM, chosen, chosen, VM, VM],
            out_specs=(VM, VM)),
        compiler_params=plain,
        name="finish",
    )(where, hat, ustar, high, low, second, fluid)
    if not flat:
        parcels_out = parcels_out[:, :, :slots].transpose(1, 0, 2).reshape(16, gz * slots)
    return velocity_out.reshape(3, 1, NR, columns), parcels_out.T


def solution(mesh):
    in_specs = (
        P(None, "gz", None, "pa"),
        P("gz", None, "pa"),
        P(("gz", "pa"), None),
        P(("gz", "pa"), None),
        P(("gz", "pa")),
        P(("gz", "pa")),
    )
    out_specs = (P(None, "gz", None, "pa"), P(("gz", "pa"), None))
    return jax.shard_map(body, mesh=mesh, in_specs=in_specs, out_specs=out_specs, check_vma=False)
```

```python
import functools
import math

import jax
import jax.numpy as jnp
import ml_dtypes
import numpy as np
from jax import lax
from jax.experimental import pallas as pl
from jax.experimental.pallas import tpu as pltpu
from jax.sharding import PartitionSpec as P

NR = 192
NTH = 512
STEP = 0.1
SHIFT = 0.0001
LIMIT = 56 * 1024 * 1024
MESH = pl.DeviceIdType.MESH
f32 = jnp.float32
bf16 = jnp.bfloat16
VM = pl.BlockSpec(memory_space=pltpu.VMEM)


def cas(n):
    x = 2.0 * np.pi / NTH * (n % NTH)
    return np.cos(x) + np.sin(x)


def halves(table):
    high = table.astype(np.float32).astype(ml_dtypes.bfloat16)
    low = (table - high.astype(np.float64)).astype(np.float32).astype(ml_dtypes.bfloat16)
    return high, low


@functools.lru_cache(None)
def forward_table(pa):
    columns = NTH // pa
    k = np.arange(NTH)[None, :]
    j = np.arange(NTH)[:, None]
    same = -cas(k * j)
    beside = -(cas(k * (j - 1)) - cas(k * (j + 1)))
    both = [np.concatenate([same[p * columns:(p + 1) * columns], beside[p * columns:(p + 1) * columns]], 0) for p in range(pa)]
    return halves(np.stack(both))


@functools.lru_cache(None)
def inverse_table(pa):
    columns = NTH // pa
    k = np.arange(NTH)[:, None]
    j = np.arange(NTH)[None, :]
    same = cas(k * j) / NTH
    beside = (cas(k * (j + 1)) - cas(k * (j - 1))) / NTH
    parts = []
    for p in range(pa):
        part = slice(p * columns, (p + 1) * columns)
        parts.append(np.stack([same[:, part], beside[:, part]]))
    return halves(np.stack(parts))


@functools.lru_cache(None)
def radial_ratios(pa):
    radius = NR + np.arange(NR) + 0.5
    step = 2.0 * np.pi / NTH
    arc = 1.0 / (radius * step) ** 2
    up = (radius + 0.5) / radius
    down = (radius - 0.5) / radius
    up[-1] = 0.0
    down[0] = 0.0
    k = np.arange(NTH)
    diagonal = SHIFT + arc[:, None] * (2.0 - 2.0 * np.cos(step * k))[None, :] + up[:, None] + down[:, None]
    lower = np.broadcast_to(-down[:, None], diagonal.shape)
    upper = np.broadcast_to(-up[:, None], diagonal.shape)

    def moved(x, s, fill):
        pad = np.full((abs(s), NTH), fill)
        return np.concatenate([pad, x[:-s]], 0) if s > 0 else np.concatenate([x[-s:], pad], 0)

    out = []
    stride = 1
    while stride < NR:
        low = lower / moved(diagonal, stride, 1.0)
        high = upper / moved(diagonal, -stride, 1.0)
        out += [low, high]
        diagonal = diagonal - low * moved(upper, stride, 0.0) - high * moved(lower, -stride, 0.0)
        lower = -low * moved(lower, stride, 0.0)
        upper = -high * moved(upper, -stride, 0.0)
        stride *= 2
    out.append(1.0 / diagonal)
    whole = np.stack(out).astype(np.float32)
    columns = NTH // pa
    return np.stack([whole[:, :, p * columns:(p + 1) * columns] for p in range(pa)])


def iota(shape, axis):
    return lax.broadcasted_iota(jnp.int32, shape, axis)


def radii():
    return (iota((NR, 1), 0) + NR).astype(f32) + 0.5


def rolled(x, s):
    return jnp.concatenate([x[s:], x[:s]], 0)


def rates_of(x):
    is_rate = iota(x.shape, 0) % 4 == 3
    w = jnp.where(is_rate, x, 0.0)
    return is_rate, w + rolled(w, 1) + rolled(w, 2) + rolled(w, 3)


def loop(first, last, step):
    if last - first <= 8:
        for i in range(first, last):
            step(i)
    else:
        lax.fori_loop(first, last, lambda i, _: (step(i), 0)[1], 0)


def thirds(x):
    one = x.astype(bf16).astype(f32)
    two = (x - one).astype(bf16).astype(f32)
    return [one, two, x - one - two]


def slots_of(gz, capacity, counts, rank):
    block = rank.shape[1]
    live = iota((1, block), 1) < counts[0]
    target = jnp.where(live, rank[...], gz)
    marks = (iota((gz, block), 0) == target).astype(f32)
    earlier = (iota((128, 128), 0) < iota((128, 128), 1)).astype(f32).astype(bf16)
    carry = jnp.zeros((gz, 1), f32)
    slots = []
    for b in range(block // 128):
        part = marks[:, 128 * b:128 * b + 128]
        before = jnp.dot(part.astype(bf16), earlier, preferred_element_type=f32) + carry
        slots.append(jnp.sum(before * part, axis=0, keepdims=True))
        carry = carry + jnp.sum(part, axis=1, keepdims=True)
    slot = jnp.concatenate(slots, 1).astype(jnp.int32)
    place = jnp.where(live, target * capacity + slot, -1)
    low_hot = (iota((128, block), 0) == (place & 127)).astype(f32).astype(bf16)
    return place >> 7, low_hot


def place_rows(gz, high, low_hot, table, target, combine):
    height = table.shape[0]
    tiles = target.shape[2] // 128

    def slab(g):
        left = [jnp.where(high == g * tiles + i, table, 0.0).astype(bf16) for i in range(tiles)]
        got = lax.dot_general(jnp.concatenate(left, 0), low_hot, (((1,), (1,)), ((), ())), preferred_element_type=f32)
        for i in range(tiles):
            target[g, :, 128 * i:128 * i + 128] = combine(got[height * i:height * i + height])

    loop(0, gz, slab)


def drag_table(parcels, cell):
    total = 0.0
    for half in (parcels[0:8], parcels[8:16]):
        is_rate, rate = rates_of(half)
        weight = rate / (1.0 + STEP * rate)
        total = total + jnp.where(is_rate, weight, weight * half)
    total = total + rolled(total, 4)
    first = iota(total.shape, 0) < 4
    one, two, three = thirds(total)
    cells = cell[...]
    line = ((cells >> 7) + 1).astype(f32)
    column = (cells & 127).astype(f32)
    row = iota(total.shape, 0)
    last = jnp.where(first, three, jnp.where(row == 4, line, jnp.where(row == 5, column, 0.0)))
    return jnp.concatenate([jnp.where(first, one, two), last], 0)


def drag_rows(r):
    sums = r[0:8] + rolled(r[0:8], 4) + r[8:16]
    return jnp.where(iota(sums.shape, 0) == 4, r[12:13] * 128.0 + r[13:14], sums)


def parcel_rows(r):
    return r[0:16] + r[16:32] + r[32:48]


def deposit_slab(g, came, turned, fluid, deposit, parts):
    columns = deposit.shape[2]
    rows = came[g]
    capacity = rows.shape[1]
    code = rows[4:5].astype(jnp.int32)
    line = (code >> 7) - 1
    column = code & 127
    line_hot = (iota((NR, capacity), 0) == line).astype(f32).astype(bf16)
    column_hot = iota((columns, capacity), 0) == column
    picked = jnp.dot(turned, line_hot, preferred_element_type=f32)
    pushes = []
    for i, c in enumerate(parts):
        both = picked[2 * i * columns:(2 * i + 1) * columns] + picked[(2 * i + 1) * columns:(2 * i + 2) * columns]
        speed = jnp.sum(jnp.where(column_hot, both, 0.0), axis=0, keepdims=True)
        drag = (rows[c:c + 1] - speed * rows[3:4]).astype(bf16).astype(f32)
        fluid[g, c:c + 1] = speed
        fluid[g, 4 + c:5 + c] = speed
        pushes.append(jnp.where(column_hot, drag, 0.0).astype(bf16))
    added = lax.dot_general(line_hot, jnp.concatenate(pushes, 0), (((1,), (1,)), ((), ())), preferred_element_type=f32)
    for i, c in enumerate(parts):
        deposit[c] += added[:, i * columns:(i + 1) * columns]


def split_dot(x, high, low):
    top = x.astype(bf16)
    rest = (x - top.astype(f32)).astype(bf16)
    out = jnp.dot(top, low, preferred_element_type=f32) + jnp.dot(rest, high, preferred_element_type=f32)
    return out + jnp.dot(top, high, preferred_element_type=f32)


def face_weights(viscosity, near, edge_left, edge_right):
    radius = radii()
    arc = 1.0 / (radius * (2.0 * math.pi / NTH)) ** 2
    nu = viscosity[...]
    return [
        0.5 * (nu + near[3]),
        (radius + 0.5) / radius * 0.5 * (nu + outward(nu)),
        (radius - 0.5) / radius * 0.5 * (nu + inward(nu)),
        arc * 0.5 * (nu + ahead(nu, edge_right[:, 3:4])),
        arc * 0.5 * (nu + behind(nu, edge_left[:, 7:8])),
    ]


def outward(x):
    return jnp.concatenate([x[1:], jnp.zeros_like(x[:1])], 0)


def inward(x):
    return jnp.concatenate([jnp.zeros_like(x[:1]), x[:-1]], 0)


def ahead(x, edge):
    columns = x.shape[1]
    return jnp.where(iota(x.shape, 1) == columns - 1, edge, pltpu.roll(x, columns - 1, 1))


def behind(x, edge):
    return jnp.where(iota(x.shape, 1) == 0, edge, pltpu.roll(x, 1, 1))


def most_of(c, speeds, near, edge_left, edge_right, deposit, weights):
    u = speeds[c]
    sides = (near[c], outward(u), inward(u), ahead(u, edge_right[:, c:c + 1]), behind(u, edge_left[:, 4 + c:5 + c]))
    total = deposit[c]
    for w, s in zip(weights, sides):
        total = total + w * (s - u)
    return u + STEP * total


def far_part(c, speeds, viscosity, far):
    return (0.5 * STEP) * (viscosity[...] + far[3]) * (far[c] - speeds[c])


def transform(pa, radial, azimuthal, high, low, partial):
    columns = radial.shape[1]
    radius = radii()
    flux = jnp.where(iota(radial.shape, 0) == NR - 1, 0.0, (radius + 0.5) * 0.5 * (radial + outward(radial)))
    divergence = (flux - inward(flux)) / radius
    across = azimuthal / (2.0 * (2.0 * math.pi / NTH) * radius)
    out = split_dot(jnp.concatenate([divergence, across], 1), high[...], low[...])
    for q in range(pa):
        partial[q % 2, q // 2] = out[:, q * columns:(q + 1) * columns]


def main_kernel(gz, pa, counts, rank_in, cell_in, parcels_in, velocity, viscosity, high_in, low_in, ratios,
                ustar, hat, second_in, fluid,
                rank, cell, parcels, speeds, nu, high, low, held, first, second, first_in,
                near, far, edges, edge_left, edge_right, deposit, partial, came, rest,
                lsem, fsend, frecv, send, recv, zsend, zrecv, wsend, wrecv, esend, erecv, psend, precv, rsend, rrecv,
                gsend, grecv, hsend, hrecv):
    me = lax.axis_index("gz")
    mp = lax.axis_index("pa")
    columns = nu.shape[1]
    loads = [
        pltpu.make_async_copy(a, b, lsem.at[i])
        for i, (a, b) in enumerate((
            (rank_in, rank), (cell_in, cell), (parcels_in, parcels), (velocity, speeds), (viscosity.at[0], nu),
            (high_in.at[mp], high), (low_in.at[mp], low), (ratios.at[mp], held)))
    ]
    for c in loads:
        c.start()
    barrier = pltpu.get_barrier_semaphore()

    def greet(o):
        pl.semaphore_signal(barrier, inc=1, device_id=(lax.rem(me + o, gz), mp), device_id_type=MESH)

    loop(1, gz, greet)
    others = [lax.rem(mp + o, pa) for o in range(1, pa)]
    for q in others:
        pl.semaphore_signal(barrier, inc=1, device_id=(me, q), device_id_type=MESH)

    def peer(o):
        to, bit = 0, 1
        while bit < gz:
            to = to + bit * lax.rem(me // bit + o // bit, 2)
            bit = bit * 2
        return to

    def slab_copy(source, target, ssem, rsem, o):
        to = peer(o)
        return pltpu.make_async_remote_copy(
            src_ref=source.at[to], dst_ref=target.at[me], send_sem=ssem.at[o], recv_sem=rsem.at[o],
            device_id=(to, mp), device_id_type=MESH)

    def first_copy(o):
        return slab_copy(first, first_in, fsend, frecv, o)

    def second_copy(o):
        return slab_copy(second, second_in, send, recv, o)

    odd = lax.rem(me, 2)
    mate = me + 1 - 2 * odd
    stride = 2 - 4 * odd
    beyond, before = me + stride, me - stride
    has_beyond = jnp.logical_and(beyond >= 0, beyond < gz)
    has_before = jnp.logical_and(before >= 0, before < gz)
    half = NR // 2
    spots = [(f, pl.ds(r, half)) for r in (0, half) for f in (3, 1, 2)] + [(0, pl.ds(r, half)) for r in (0, half)]

    def trade(i):
        f, rows = spots[i]
        source = velocity.at[f, rows] if f < 3 else viscosity.at[0, rows]
        return pltpu.make_async_remote_copy(
            src_ref=source, dst_ref=near.at[f, rows], send_sem=zsend.at[i], recv_sem=zrecv.at[i],
            device_id=(mate, mp), device_id_type=MESH)

    def hand_on(i):
        f, rows = spots[i]
        return pltpu.make_async_remote_copy(
            src_ref=near.at[f, rows], dst_ref=far.at[f, rows], send_sem=wsend.at[i], recv_sem=wrecv.at[i],
            device_id=(lax.rem(beyond + gz, gz), mp), device_id_type=MESH)

    @pl.when(jnp.logical_not(has_before))
    def _():
        far[...] = jnp.zeros_like(far)

    pl.semaphore_wait(barrier, gz + pa - 2)
    for i in range(3):
        trade(i).start()
    for c in loads[:5]:
        c.wait()
    high_part, low_hot = slots_of(gz, first.shape[2], counts, rank)
    values = parcels[...]
    place_rows(gz, high_part, low_hot, drag_table(values, cell), first, drag_rows)
    loop(1, gz, lambda o: first_copy(gz - o).start())
    for i in range(3, 6):
        trade(i).start()

    def pass_on(i):
        trade(i).wait_recv()

        @pl.when(has_beyond)
        def _():
            hand_on(i).start()

    def far_ready(numbers):
        @pl.when(has_before)
        def _():
            for i in numbers:
                hand_on(i).wait_recv()

    pieces, ends = [], []
    for c in range(3):
        turned = speeds[c].T
        top = turned.astype(bf16)
        pieces += [top, (turned - top.astype(f32)).astype(bf16)]
        ends.append(turned)
    ends.append(nu[...].T)
    edges[...] = jnp.concatenate([x[:1] for x in ends] + [x[columns - 1:] for x in ends], 0)
    right, left = lax.rem(mp + 1, pa), lax.rem(mp + pa - 1, pa)
    sides = [
        pltpu.make_async_remote_copy(
            src_ref=edges, dst_ref=target, send_sem=esend.at[i], recv_sem=erecv.at[i],
            device_id=(me, q), device_id_type=MESH)
        for i, (target, q) in enumerate(((edge_left, right), (edge_right, left)))
    ]
    for c in sides:
        c.start()
    for i in range(6, 8):
        trade(i).start()
    place_rows(gz, high_part, low_hot, jnp.concatenate(thirds(values), 0), second, parcel_rows)
    turned = jnp.concatenate(pieces[2:], 0)
    turned_axial = jnp.concatenate(pieces[:2], 0)
    fluid[...] = jnp.zeros_like(fluid)
    deposit[...] = jnp.zeros_like(deposit)
    first_in[me] = first[me]
    second_in[me] = second[me]
    deposit_slab(me, first_in, turned, fluid, deposit, (1, 2))

    def take(o):
        first_copy(o).wait()
        deposit_slab(peer(o), first_in, turned, fluid, deposit, (1, 2))

    done = 1
    for i in range(6):
        upto = 1 + (i + 1) * (gz - 1) // 6
        loop(done, upto, take)
        done = upto
        pass_on(i)
    for c in sides:
        c.wait()
    for c in loads[5:]:
        c.wait()
    edge_l, edge_r = edge_left[...].T, edge_right[...].T
    weights = face_weights(nu, near, edge_l, edge_r)
    for c in (1, 2):
        ustar[c] = most_of(c, speeds, near, edge_l, edge_r, deposit, weights)
    far_ready(range(6))
    radial, azimuthal = [ustar[c] + far_part(c, speeds, nu, far) for c in (1, 2)]
    ustar[1] = radial
    ustar[2] = azimuthal
    transform(pa, radial, azimuthal, high, low, partial)
    core = lax.rem(mp, 2)
    pair = mp + 1 - 2 * core
    place = mp // 2
    pairs = pa // 2
    order = [lax.rem(place + 1 + i, pairs) for i in range(pairs)]
    inner = [
        pltpu.make_async_remote_copy(
            src_ref=partial.at[1 - core, q], dst_ref=came.at[q], send_sem=psend.at[i], recv_sem=precv.at[i],
            device_id=(me, pair), device_id_type=MESH)
        for i, q in enumerate(order)
    ]
    for c in inner:
        c.start()
    outer = []
    for i, q in enumerate(order[:-1]):
        inner[i].wait_recv()
        came[q] = came[q] + partial[core, q]
        outer.append(pltpu.make_async_remote_copy(
            src_ref=came.at[q], dst_ref=rest.at[i], send_sem=rsend.at[i], recv_sem=rrecv.at[i],
            device_id=(me, 2 * q + core), device_id_type=MESH))
        outer[-1].start()
    for i in (6, 7):
        pass_on(i)
    loop(1, gz, lambda o: second_copy(gz - o).start())

    def axial(o):
        deposit_slab(peer(o), first_in, turned_axial, fluid, deposit, (0,))

    loop(0, gz // 2, axial)
    inner[-1].wait_recv()
    x = partial[core, place] + came[place]
    for i, c in enumerate(outer):
        c.wait()
        x = x + rest[i]
    radius = radii()
    mean = jnp.sum(radius * x, axis=0, keepdims=True) * (1.0 / (NR * (NR + NR / 2)))
    x = x - jnp.where(iota((1, columns), 1) + mp * columns == 0, mean, 0.0)
    stride, n = 1, 0
    while stride < NR:
        pad = jnp.zeros((stride, columns), f32)
        lower = jnp.concatenate([pad, x[:-stride]], 0)
        upper = jnp.concatenate([x[stride:], pad], 0)
        x = x - held[n] * lower - held[n + 1] * upper
        stride, n = stride * 2, n + 2
    hat[mp] = x * held[n]
    spread = [
        pltpu.make_async_remote_copy(
            src_ref=hat.at[mp], dst_ref=hat.at[mp], send_sem=gsend.at[i], recv_sem=grecv.at[i],
            device_id=(me, q), device_id_type=MESH)
        for i, q in enumerate([2 * q + core for q in order[:-1]] + [pair])
    ]
    for c in spread:
        c.start()
    again = []
    for i in range(pairs - 1):
        q = 2 * lax.rem(place + 2 * pairs - 1 - i, pairs) + core
        spread[i].wait_recv()
        again.append(pltpu.make_async_remote_copy(
            src_ref=hat.at[q], dst_ref=hat.at[q], send_sem=hsend.at[i], recv_sem=hrecv.at[i],
            device_id=(me, pair), device_id_type=MESH))
        again[-1].start()
    loop(gz // 2, gz, axial)
    weights = face_weights(nu, near, edge_l, edge_r)
    ustar[0] = most_of(0, speeds, near, edge_l, edge_r, deposit, weights)
    far_ready((6, 7))
    ustar[0] = ustar[0] + far_part(0, speeds, nu, far)
    spread[-1].wait_recv()
    for c in again:
        c.wait()
    for c in spread + inner:
        c.wait_send()
    for i in range(8):
        trade(i).wait_send()

    @pl.when(has_beyond)
    def _():
        for i in range(8):
            hand_on(i).wait_send()

    loop(1, gz, lambda o: second_copy(o).wait())


def finish_kernel(gz, pa, flat, where, hat, ustar, high, low, second, fluid, velocity_out, parcels_out):
    capacity = second.shape[2]
    x = jnp.concatenate([hat[q] for q in range(pa)], 1)
    slope = 0.5 * (jnp.concatenate([x[1:], x[-1:]], 0) - jnp.concatenate([x[:1], x[:-1]], 0))
    velocity_out[0] = ustar[0]
    velocity_out[1] = ustar[1] - split_dot(slope, high[0, 0], low[0, 0])
    turn = split_dot(x, high[0, 1], low[0, 1]) / (2.0 * (2.0 * math.pi / NTH) * radii())
    velocity_out[2] = ustar[2] - turn

    def slab(g, _):
        speed = fluid[g]
        for h in (0, 8):
            rows = second[g, h:h + 8]
            is_rate, rate = rates_of(rows)
            moved = (rows + STEP * rate * speed) / (1.0 + STEP * rate)
            rows = jnp.where(is_rate, rows, moved)
            if flat:
                parcels_out[h:h + 8, pl.ds(pl.multiple_of(g * capacity, 128), capacity)] = rows
            else:
                parcels_out[g, h:h + 8] = rows
        return 0

    lax.fori_loop(0, gz, slab, 0, unroll=gz <= 8)


def body(velocity, viscosity, parcels, dest_rank, dest_cell, counts):
    gz = lax.axis_size("gz")
    pa = lax.axis_size("pa")
    columns = viscosity.shape[2]
    block = parcels.shape[0]
    slots = 3 * block // gz
    capacity = -(-slots // 128) * 128
    flat = capacity == slots
    velocity = velocity.reshape(3, NR, columns)

    def shape(*s):
        return jax.ShapeDtypeStruct(s, f32)

    plain = pltpu.CompilerParams(vmem_limit_bytes=LIMIT)
    dma = pltpu.SemaphoreType.DMA
    where = lax.axis_index("pa").astype(jnp.int32).reshape(1)
    high, low = forward_table(pa)
    ratios = radial_ratios(pa)
    ANY = pl.BlockSpec(memory_space=pltpu.HBM)

    def hold(*s):
        return pltpu.VMEM(s, f32)

    ustar, hat, second, fluid = pl.pallas_call(
        functools.partial(main_kernel, gz, pa),
        out_shape=(shape(3, NR, columns), shape(pa, NR, columns), shape(gz, 16, capacity), shape(gz, 8, capacity)),
        in_specs=[pl.BlockSpec(memory_space=pltpu.SMEM)] + [ANY] * 8,
        out_specs=(VM,) * 4,
        scratch_shapes=[
            pltpu.VMEM((1, block), jnp.int32), pltpu.VMEM((1, block), jnp.int32), hold(16, block),
            hold(3, NR, columns), hold(NR, columns),
            pltpu.VMEM((2 * columns, NTH), bf16), pltpu.VMEM((2 * columns, NTH), bf16), hold(*ratios.shape[1:]),
            hold(gz, 8, capacity), hold(gz, 16, capacity), hold(gz, 8, capacity),
            hold(4, NR, columns), hold(4, NR, columns), hold(8, NR), hold(8, NR), hold(8, NR),
            hold(3, NR, columns), hold(2, pa // 2, NR, columns), hold(pa // 2, NR, columns), hold(pa // 2 - 1, NR, columns),
            dma((8,)), dma((gz,)), dma((gz,)), dma((gz,)), dma((gz,)), dma((8,)), dma((8,)), dma((8,)), dma((8,)),
            dma((2,)), dma((2,)), dma((pa // 2,)), dma((pa // 2,)), dma((pa // 2 - 1,)), dma((pa // 2 - 1,)),
            dma((pa // 2,)), dma((pa // 2,)), dma((pa // 2 - 1,)), dma((pa // 2 - 1,)),
        ],
        compiler_params=pltpu.CompilerParams(collective_id=0, has_side_effects=True, vmem_limit_bytes=LIMIT),
        name="step",
    )(counts, dest_rank.reshape(1, block), dest_cell.reshape(1, block), parcels.T, velocity,
      viscosity, high, low, ratios)
    high, low = inverse_table(pa)
    chosen = pl.BlockSpec((1, 2, NTH, columns), lambda i, w: (w[0], 0, 0, 0))
    velocity_out, parcels_out = pl.pallas_call(
        functools.partial(finish_kernel, gz, pa, flat),
        out_shape=(shape(3, NR, columns), shape(16, gz * slots) if flat else shape(gz, 16, capacity)),
        grid_spec=pltpu.PrefetchScalarGridSpec(
            num_scalar_prefetch=1, grid=(1,),
            in_specs=[VM, VM, chosen, chosen, VM, VM],
            out_specs=(VM, VM)),
        compiler_params=plain,
        name="finish",
    )(where, hat, ustar, high, low, second, fluid)
    if not flat:
        parcels_out = parcels_out[:, :, :slots].transpose(1, 0, 2).reshape(16, gz * slots)
    return velocity_out.reshape(3, 1, NR, columns), parcels_out.T


def solution(mesh):
    in_specs = (
        P(None, "gz", None, "pa"),
        P("gz", None, "pa"),
        P(("gz", "pa"), None),
        P(("gz", "pa"), None),
        P(("gz", "pa")),
        P(("gz", "pa")),
    )
    out_specs = (P(None, "gz", None, "pa"), P(("gz", "pa"), None))
    return jax.shard_map(body, mesh=mesh, in_specs=in_specs, out_specs=out_specs, check_vma=False)
```

```python
import functools
import math

import jax
import jax.numpy as jnp
import ml_dtypes
import numpy as np
from jax import lax
from jax.experimental import pallas as pl
from jax.experimental.pallas import tpu as pltpu
from jax.sharding import PartitionSpec as P

NR = 192
NTH = 512
STEP = 0.1
SHIFT = 0.0001
LIMIT = 56 * 1024 * 1024
MESH = pl.DeviceIdType.MESH
f32 = jnp.float32
bf16 = jnp.bfloat16
VM = pl.BlockSpec(memory_space=pltpu.VMEM)


def cas(n):
    x = 2.0 * np.pi / NTH * (n % NTH)
    return np.cos(x) + np.sin(x)


def halves(table):
    high = table.astype(np.float32).astype(ml_dtypes.bfloat16)
    low = (table - high.astype(np.float64)).astype(np.float32).astype(ml_dtypes.bfloat16)
    return high, low


@functools.lru_cache(None)
def forward_table(pa):
    columns = NTH // pa
    k = np.arange(NTH)[None, :]
    j = np.arange(NTH)[:, None]
    same = -cas(k * j)
    beside = -(cas(k * (j - 1)) - cas(k * (j + 1)))
    both = [np.concatenate([same[p * columns:(p + 1) * columns], beside[p * columns:(p + 1) * columns]], 0) for p in range(pa)]
    return halves(np.stack(both))


@functools.lru_cache(None)
def inverse_table(pa):
    columns = NTH // pa
    k = np.arange(NTH)[:, None]
    j = np.arange(NTH)[None, :]
    same = cas(k * j) / NTH
    beside = (cas(k * (j + 1)) - cas(k * (j - 1))) / NTH
    parts = []
    for p in range(pa):
        part = slice(p * columns, (p + 1) * columns)
        parts.append(np.stack([same[:, part], beside[:, part]]).reshape(2, pa, columns, columns))
    return halves(np.stack(parts))


@functools.lru_cache(None)
def radial_ratios(pa):
    radius = NR + np.arange(NR) + 0.5
    step = 2.0 * np.pi / NTH
    arc = 1.0 / (radius * step) ** 2
    up = (radius + 0.5) / radius
    down = (radius - 0.5) / radius
    up[-1] = 0.0
    down[0] = 0.0
    k = np.arange(NTH)
    diagonal = SHIFT + arc[:, None] * (2.0 - 2.0 * np.cos(step * k))[None, :] + up[:, None] + down[:, None]
    lower = np.broadcast_to(-down[:, None], diagonal.shape)
    upper = np.broadcast_to(-up[:, None], diagonal.shape)

    def moved(x, s, fill):
        pad = np.full((abs(s), NTH), fill)
        return np.concatenate([pad, x[:-s]], 0) if s > 0 else np.concatenate([x[-s:], pad], 0)

    out = []
    stride = 1
    while stride < NR:
        low = lower / moved(diagonal, stride, 1.0)
        high = upper / moved(diagonal, -stride, 1.0)
        out += [low, high]
        diagonal = diagonal - low * moved(upper, stride, 0.0) - high * moved(lower, -stride, 0.0)
        lower = -low * moved(lower, stride, 0.0)
        upper = -high * moved(upper, -stride, 0.0)
        stride *= 2
    out.append(1.0 / diagonal)
    whole = np.stack(out).astype(np.float32)
    columns = NTH // pa
    return np.stack([whole[:, :, p * columns:(p + 1) * columns] for p in range(pa)])


def iota(shape, axis):
    return lax.broadcasted_iota(jnp.int32, shape, axis)


def radii():
    return (iota((NR, 1), 0) + NR).astype(f32) + 0.5


def rolled(x, s):
    return jnp.concatenate([x[s:], x[:s]], 0)


def rates_of(x):
    is_rate = iota(x.shape, 0) % 4 == 3
    w = jnp.where(is_rate, x, 0.0)
    return is_rate, w + rolled(w, 1) + rolled(w, 2) + rolled(w, 3)


def loop(first, last, step):
    if last - first <= 8:
        for i in range(first, last):
            step(i)
    else:
        lax.fori_loop(first, last, lambda i, _: (step(i), 0)[1], 0)


def thirds(x):
    one = x.astype(bf16).astype(f32)
    two = (x - one).astype(bf16).astype(f32)
    return [one, two, x - one - two]


def slots_of(gz, capacity, counts, rank):
    block = rank.shape[1]
    live = iota((1, block), 1) < counts[0]
    target = jnp.where(live, rank[...], gz)
    marks = (iota((gz, block), 0) == target).astype(f32)
    earlier = (iota((128, 128), 0) < iota((128, 128), 1)).astype(f32).astype(bf16)
    carry = jnp.zeros((gz, 1), f32)
    slots = []
    for b in range(block // 128):
        part = marks[:, 128 * b:128 * b + 128]
        before = jnp.dot(part.astype(bf16), earlier, preferred_element_type=f32) + carry
        slots.append(jnp.sum(before * part, axis=0, keepdims=True))
        carry = carry + jnp.sum(part, axis=1, keepdims=True)
    slot = jnp.concatenate(slots, 1).astype(jnp.int32)
    place = jnp.where(live, target * capacity + slot, -1)
    low_hot = (iota((128, block), 0) == (place & 127)).astype(f32).astype(bf16)
    return place >> 7, low_hot


def place_rows(gz, high, low_hot, table, target, combine):
    height = table.shape[0]
    tiles = target.shape[2] // 128

    def slab(g):
        left = [jnp.where(high == g * tiles + i, table, 0.0).astype(bf16) for i in range(tiles)]
        got = lax.dot_general(jnp.concatenate(left, 0), low_hot, (((1,), (1,)), ((), ())), preferred_element_type=f32)
        for i in range(tiles):
            target[g, :, 128 * i:128 * i + 128] = combine(got[height * i:height * i + height])

    loop(0, gz, slab)


def drag_table(parcels, cell):
    total = 0.0
    for half in (parcels[0:8], parcels[8:16]):
        is_rate, rate = rates_of(half)
        weight = rate / (1.0 + STEP * rate)
        total = total + jnp.where(is_rate, weight, weight * half)
    total = total + rolled(total, 4)
    first = iota(total.shape, 0) < 4
    one, two, three = thirds(total)
    cells = cell[...]
    line = ((cells >> 7) + 1).astype(f32)
    column = (cells & 127).astype(f32)
    row = iota(total.shape, 0)
    last = jnp.where(first, three, jnp.where(row == 4, line, jnp.where(row == 5, column, 0.0)))
    return jnp.concatenate([jnp.where(first, one, two), last], 0)


def drag_rows(r):
    sums = r[0:8] + rolled(r[0:8], 4) + r[8:16]
    return jnp.where(iota(sums.shape, 0) == 4, r[12:13] * 128.0 + r[13:14], sums)


def parcel_rows(r):
    return r[0:16] + r[16:32] + r[32:48]


def deposit_slab(g, came, turned, fluid, deposit, parts):
    columns = deposit.shape[2]
    rows = came[g]
    capacity = rows.shape[1]
    code = rows[4:5].astype(jnp.int32)
    line = (code >> 7) - 1
    column = code & 127
    line_hot = (iota((NR, capacity), 0) == line).astype(f32).astype(bf16)
    column_hot = iota((columns, capacity), 0) == column
    picked = jnp.dot(turned, line_hot, preferred_element_type=f32)
    pushes = []
    for i, c in enumerate(parts):
        both = picked[2 * i * columns:(2 * i + 1) * columns] + picked[(2 * i + 1) * columns:(2 * i + 2) * columns]
        speed = jnp.sum(jnp.where(column_hot, both, 0.0), axis=0, keepdims=True)
        drag = (rows[c:c + 1] - speed * rows[3:4]).astype(bf16).astype(f32)
        fluid[g, c:c + 1] = speed
        fluid[g, 4 + c:5 + c] = speed
        pushes.append(jnp.where(column_hot, drag, 0.0).astype(bf16))
    added = lax.dot_general(line_hot, jnp.concatenate(pushes, 0), (((1,), (1,)), ((), ())), preferred_element_type=f32)
    for i, c in enumerate(parts):
        deposit[c] += added[:, i * columns:(i + 1) * columns]


def split_dot(x, high, low):
    top = x.astype(bf16)
    rest = (x - top.astype(f32)).astype(bf16)
    out = jnp.dot(top, low, preferred_element_type=f32) + jnp.dot(rest, high, preferred_element_type=f32)
    return out + jnp.dot(top, high, preferred_element_type=f32)


def face_weights(viscosity, near, edge_left, edge_right):
    radius = radii()
    arc = 1.0 / (radius * (2.0 * math.pi / NTH)) ** 2
    nu = viscosity[...]
    return [
        0.5 * (nu + near[3]),
        (radius + 0.5) / radius * 0.5 * (nu + outward(nu)),
        (radius - 0.5) / radius * 0.5 * (nu + inward(nu)),
        arc * 0.5 * (nu + ahead(nu, edge_right[:, 3:4])),
        arc * 0.5 * (nu + behind(nu, edge_left[:, 7:8])),
    ]


def outward(x):
    return jnp.concatenate([x[1:], jnp.zeros_like(x[:1])], 0)


def inward(x):
    return jnp.concatenate([jnp.zeros_like(x[:1]), x[:-1]], 0)


def ahead(x, edge):
    columns = x.shape[1]
    return jnp.where(iota(x.shape, 1) == columns - 1, edge, pltpu.roll(x, columns - 1, 1))


def behind(x, edge):
    return jnp.where(iota(x.shape, 1) == 0, edge, pltpu.roll(x, 1, 1))


def most_of(c, speeds, near, edge_left, edge_right, deposit, weights):
    u = speeds[c]
    sides = (near[c], outward(u), inward(u), ahead(u, edge_right[:, c:c + 1]), behind(u, edge_left[:, 4 + c:5 + c]))
    total = deposit[c]
    for w, s in zip(weights, sides):
        total = total + w * (s - u)
    return u + STEP * total


def far_part(c, speeds, viscosity, far):
    return (0.5 * STEP) * (viscosity[...] + far[3]) * (far[c] - speeds[c])


def transform(pa, radial, azimuthal, high, low, partial):
    columns = radial.shape[1]
    radius = radii()
    flux = jnp.where(iota(radial.shape, 0) == NR - 1, 0.0, (radius + 0.5) * 0.5 * (radial + outward(radial)))
    divergence = (flux - inward(flux)) / radius
    across = azimuthal / (2.0 * (2.0 * math.pi / NTH) * radius)
    out = split_dot(jnp.concatenate([divergence, across], 1), high[...], low[...])
    for q in range(pa):
        partial[q % 2, q // 2] = out[:, q * columns:(q + 1) * columns]


def main_kernel(gz, pa, flat, counts, rank_in, cell_in, parcels_in, velocity, viscosity, high_in, low_in, ratios,
                high_back, low_back, velocity_out, parcels_out,
                ustar, hat, second_in, fluid, back_high, back_low, rank, cell, parcels, speeds, nu, high, low, held, first, second, first_in,
                near, far, edges, edge_left, edge_right, deposit, partial, came, rest,
                lsem, fsend, frecv, send, recv, zsend, zrecv, wsend, wrecv, esend, erecv, psend, precv, rsend, rrecv,
                gsend, grecv, hsend, hrecv):
    me = lax.axis_index("gz")
    mp = lax.axis_index("pa")
    columns = nu.shape[1]
    loads = [
        pltpu.make_async_copy(a, b, lsem.at[i])
        for i, (a, b) in enumerate((
            (rank_in, rank), (cell_in, cell), (parcels_in, parcels), (velocity, speeds), (viscosity.at[0], nu),
            (high_in.at[mp], high), (low_in.at[mp], low), (ratios.at[mp], held),
            (high_back.at[mp], back_high), (low_back.at[mp], back_low)))
    ]
    for c in loads:
        c.start()
    barrier = pltpu.get_barrier_semaphore()

    def greet(o):
        pl.semaphore_signal(barrier, inc=1, device_id=(lax.rem(me + o, gz), mp), device_id_type=MESH)

    loop(1, gz, greet)
    others = [lax.rem(mp + o, pa) for o in range(1, pa)]
    for q in others:
        pl.semaphore_signal(barrier, inc=1, device_id=(me, q), device_id_type=MESH)

    def peer(o):
        to, bit = 0, 1
        while bit < gz:
            to = to + bit * lax.rem(me // bit + o // bit, 2)
            bit = bit * 2
        return to

    def slab_copy(source, target, ssem, rsem, o):
        to = peer(o)
        return pltpu.make_async_remote_copy(
            src_ref=source.at[to], dst_ref=target.at[me], send_sem=ssem.at[o], recv_sem=rsem.at[o],
            device_id=(to, mp), device_id_type=MESH)

    def first_copy(o):
        return slab_copy(first, first_in, fsend, frecv, o)

    def second_copy(o):
        return slab_copy(second, second_in, send, recv, o)

    odd = lax.rem(me, 2)
    mate = me + 1 - 2 * odd
    stride = 2 - 4 * odd
    beyond, before = me + stride, me - stride
    has_beyond = jnp.logical_and(beyond >= 0, beyond < gz)
    has_before = jnp.logical_and(before >= 0, before < gz)
    half = NR // 2
    spots = [(f, pl.ds(r, half)) for r in (0, half) for f in (3, 1, 2)] + [(0, pl.ds(r, half)) for r in (0, half)]

    def trade(i):
        f, rows = spots[i]
        source = velocity.at[f, rows] if f < 3 else viscosity.at[0, rows]
        return pltpu.make_async_remote_copy(
            src_ref=source, dst_ref=near.at[f, rows], send_sem=zsend.at[i], recv_sem=zrecv.at[i],
            device_id=(mate, mp), device_id_type=MESH)

    def hand_on(i):
        f, rows = spots[i]
        return pltpu.make_async_remote_copy(
            src_ref=near.at[f, rows], dst_ref=far.at[f, rows], send_sem=wsend.at[i], recv_sem=wrecv.at[i],
            device_id=(lax.rem(beyond + gz, gz), mp), device_id_type=MESH)

    @pl.when(jnp.logical_not(has_before))
    def _():
        far[...] = jnp.zeros_like(far)

    pl.semaphore_wait(barrier, gz + pa - 2)
    for i in range(3):
        trade(i).start()
    for c in loads[:5]:
        c.wait()
    high_part, low_hot = slots_of(gz, first.shape[2], counts, rank)
    values = parcels[...]
    place_rows(gz, high_part, low_hot, drag_table(values, cell), first, drag_rows)
    loop(1, gz, lambda o: first_copy(gz - o).start())
    for i in range(3, 6):
        trade(i).start()

    def pass_on(i):
        trade(i).wait_recv()

        @pl.when(has_beyond)
        def _():
            hand_on(i).start()

    def far_ready(numbers):
        @pl.when(has_before)
        def _():
            for i in numbers:
                hand_on(i).wait_recv()

    pieces, ends = [], []
    for c in range(3):
        turned = speeds[c].T
        top = turned.astype(bf16)
        pieces += [top, (turned - top.astype(f32)).astype(bf16)]
        ends.append(turned)
    ends.append(nu[...].T)
    edges[...] = jnp.concatenate([x[:1] for x in ends] + [x[columns - 1:] for x in ends], 0)
    right, left = lax.rem(mp + 1, pa), lax.rem(mp + pa - 1, pa)
    sides = [
        pltpu.make_async_remote_copy(
            src_ref=edges, dst_ref=target, send_sem=esend.at[i], recv_sem=erecv.at[i],
            device_id=(me, q), device_id_type=MESH)
        for i, (target, q) in enumerate(((edge_left, right), (edge_right, left)))
    ]
    for c in sides:
        c.start()
    for i in range(6, 8):
        trade(i).start()
    place_rows(gz, high_part, low_hot, jnp.concatenate(thirds(values), 0), second, parcel_rows)
    turned = jnp.concatenate(pieces[2:], 0)
    turned_axial = jnp.concatenate(pieces[:2], 0)
    fluid[...] = jnp.zeros_like(fluid)
    deposit[...] = jnp.zeros_like(deposit)
    first_in[me] = first[me]
    second_in[me] = second[me]
    deposit_slab(me, first_in, turned, fluid, deposit, (1, 2))

    def take(o):
        first_copy(o).wait()
        deposit_slab(peer(o), first_in, turned, fluid, deposit, (1, 2))

    done = 1
    for i in range(6):
        upto = 1 + (i + 1) * (gz - 1) // 6
        loop(done, upto, take)
        done = upto
        pass_on(i)
    loop(1, gz, lambda o: second_copy(gz - o).start())
    for c in sides:
        c.wait()
    for c in loads[5:]:
        c.wait()
    edge_l, edge_r = edge_left[...].T, edge_right[...].T
    weights = face_weights(nu, near, edge_l, edge_r)
    for c in (1, 2):
        ustar[c] = most_of(c, speeds, near, edge_l, edge_r, deposit, weights)
    far_ready(range(6))
    radial, azimuthal = [ustar[c] + far_part(c, speeds, nu, far) for c in (1, 2)]
    ustar[1] = radial
    ustar[2] = azimuthal
    transform(pa, radial, azimuthal, high, low, partial)
    core = lax.rem(mp, 2)
    pair = mp + 1 - 2 * core
    place = mp // 2
    pairs = pa // 2
    order = [lax.rem(place + 1 + i, pairs) for i in range(pairs)]
    inner = [
        pltpu.make_async_remote_copy(
            src_ref=partial.at[1 - core, q], dst_ref=came.at[q], send_sem=psend.at[i], recv_sem=precv.at[i],
            device_id=(me, pair), device_id_type=MESH)
        for i, q in enumerate(order)
    ]
    for c in inner:
        c.start()
    outer = []
    for i, q in enumerate(order[:-1]):
        inner[i].wait_recv()
        came[q] = came[q] + partial[core, q]
        outer.append(pltpu.make_async_remote_copy(
            src_ref=came.at[q], dst_ref=rest.at[i], send_sem=rsend.at[i], recv_sem=rrecv.at[i],
            device_id=(me, 2 * q + core), device_id_type=MESH))
        outer[-1].start()
    for i in (6, 7):
        pass_on(i)

    def axial(o):
        deposit_slab(peer(o), first_in, turned_axial, fluid, deposit, (0,))

    loop(0, gz // 2, axial)
    inner[-1].wait_recv()
    x = partial[core, place] + came[place]
    for i, c in enumerate(outer):
        c.wait()
        x = x + rest[i]
    radius = radii()
    mean = jnp.sum(radius * x, axis=0, keepdims=True) * (1.0 / (NR * (NR + NR / 2)))
    x = x - jnp.where(iota((1, columns), 1) + mp * columns == 0, mean, 0.0)
    stride, n = 1, 0
    while stride < NR:
        pad = jnp.zeros((stride, columns), f32)
        lower = jnp.concatenate([pad, x[:-stride]], 0)
        upper = jnp.concatenate([x[stride:], pad], 0)
        x = x - held[n] * lower - held[n + 1] * upper
        stride, n = stride * 2, n + 2
    hat[mp] = x * held[n]
    spread = [
        pltpu.make_async_remote_copy(
            src_ref=hat.at[mp], dst_ref=hat.at[mp], send_sem=gsend.at[i], recv_sem=grecv.at[i],
            device_id=(me, q), device_id_type=MESH)
        for i, q in enumerate([2 * q + core for q in order[:-1]] + [pair])
    ]
    for c in spread:
        c.start()

    def back(q, sums):
        block = hat[q]
        slope = 0.5 * (jnp.concatenate([block[1:], block[-1:]], 0) - jnp.concatenate([block[:1], block[:-1]], 0))
        return (sums[0] + split_dot(slope, back_high[0, q], back_low[0, q]),
                sums[1] + split_dot(block, back_high[1, q], back_low[1, q]))

    grads = back(mp, (0.0, 0.0))
    loop(gz // 2, gz, axial)
    spread[-1].wait_recv()
    grads = back(2 * place + 1 - core, grads)
    again, froms = [], []
    for i in range(pairs - 1):
        froms.append(2 * lax.rem(place + 2 * pairs - 1 - i, pairs))
        q = froms[-1] + core
        spread[i].wait_recv()
        again.append(pltpu.make_async_remote_copy(
            src_ref=hat.at[q], dst_ref=hat.at[q], send_sem=hsend.at[i], recv_sem=hrecv.at[i],
            device_id=(me, pair), device_id_type=MESH))
        again[-1].start()
    for q in froms:
        grads = back(q + core, grads)
    weights = face_weights(nu, near, edge_l, edge_r)
    axial_speed = most_of(0, speeds, near, edge_l, edge_r, deposit, weights)
    far_ready((6, 7))
    velocity_out[0] = axial_speed + far_part(0, speeds, nu, far)
    for i, q in enumerate(froms):
        again[i].wait()
        grads = back(q + 1 - core, grads)
    velocity_out[1] = ustar[1] - grads[0]
    velocity_out[2] = ustar[2] - grads[1] / (2.0 * (2.0 * math.pi / NTH) * radii())
    for c in spread + inner:
        c.wait_send()
    for i in range(8):
        trade(i).wait_send()

    @pl.when(has_beyond)
    def _():
        for i in range(8):
            hand_on(i).wait_send()

    def arrive(o):
        g = peer(o)
        if not (isinstance(o, int) and o == 0):
            second_copy(o).wait()
        rows = move_rows(second_in[g], fluid[g])
        if flat:
            capacity = rows.shape[1]
            parcels_out[:, pl.ds(pl.multiple_of(g * capacity, 128), capacity)] = rows
        else:
            parcels_out[g] = rows

    arrive(0)
    loop(1, gz, arrive)


def move_rows(rows, speed):
    out = []
    for h in (0, 8):
        part = rows[h:h + 8]
        is_rate, rate = rates_of(part)
        out.append(jnp.where(is_rate, part, (part + STEP * rate * speed) / (1.0 + STEP * rate)))
    return jnp.concatenate(out, 0)


def body(velocity, viscosity, parcels, dest_rank, dest_cell, counts):
    gz = lax.axis_size("gz")
    pa = lax.axis_size("pa")
    columns = viscosity.shape[2]
    block = parcels.shape[0]
    slots = 3 * block // gz
    capacity = -(-slots // 128) * 128
    flat = capacity == slots
    velocity = velocity.reshape(3, NR, columns)

    def shape(*s):
        return jax.ShapeDtypeStruct(s, f32)

    dma = pltpu.SemaphoreType.DMA
    high, low = forward_table(pa)
    high_back, low_back = inverse_table(pa)
    ratios = radial_ratios(pa)
    ANY = pl.BlockSpec(memory_space=pltpu.HBM)

    def hold(*s):
        return pltpu.VMEM(s, f32)

    velocity_out, parcels_out = pl.pallas_call(
        functools.partial(main_kernel, gz, pa, flat),
        out_shape=(shape(3, NR, columns), shape(16, gz * slots) if flat else shape(gz, 16, capacity)),
        in_specs=[pl.BlockSpec(memory_space=pltpu.SMEM)] + [ANY] * 10,
        out_specs=(VM, VM),
        scratch_shapes=[
            hold(3, NR, columns), hold(pa, NR, columns), hold(gz, 16, capacity), hold(gz, 8, capacity),
            pltpu.VMEM((2, pa, columns, columns), bf16), pltpu.VMEM((2, pa, columns, columns), bf16),
            pltpu.VMEM((1, block), jnp.int32), pltpu.VMEM((1, block), jnp.int32), hold(16, block),
            hold(3, NR, columns), hold(NR, columns),
            pltpu.VMEM((2 * columns, NTH), bf16), pltpu.VMEM((2 * columns, NTH), bf16), hold(*ratios.shape[1:]),
            hold(gz, 8, capacity), hold(gz, 16, capacity), hold(gz, 8, capacity),
            hold(4, NR, columns), hold(4, NR, columns), hold(8, NR), hold(8, NR), hold(8, NR),
            hold(3, NR, columns), hold(2, pa // 2, NR, columns), hold(pa // 2, NR, columns), hold(pa // 2 - 1, NR, columns),
            dma((10,)), dma((gz,)), dma((gz,)), dma((gz,)), dma((gz,)), dma((8,)), dma((8,)), dma((8,)), dma((8,)),
            dma((2,)), dma((2,)), dma((pa // 2,)), dma((pa // 2,)), dma((pa // 2 - 1,)), dma((pa // 2 - 1,)),
            dma((pa // 2,)), dma((pa // 2,)), dma((pa // 2 - 1,)), dma((pa // 2 - 1,)),
        ],
        compiler_params=pltpu.CompilerParams(collective_id=0, has_side_effects=True, vmem_limit_bytes=LIMIT),
        name="step",
    )(counts, dest_rank.reshape(1, block), dest_cell.reshape(1, block), parcels.T, velocity,
      viscosity, high, low, ratios, high_back, low_back)
    if not flat:
        parcels_out = parcels_out[:, :, :slots].transpose(1, 0, 2).reshape(16, gz * slots)
    return velocity_out.reshape(3, 1, NR, columns), parcels_out.T


def solution(mesh):
    in_specs = (
        P(None, "gz", None, "pa"),
        P("gz", None, "pa"),
        P(("gz", "pa"), None),
        P(("gz", "pa"), None),
        P(("gz", "pa")),
        P(("gz", "pa")),
    )
    out_specs = (P(None, "gz", None, "pa"), P(("gz", "pa"), None))
    return jax.shard_map(body, mesh=mesh, in_specs=in_specs, out_specs=out_specs, check_vma=False)
```

```python
import functools
import math

import jax
import jax.numpy as jnp
import ml_dtypes
import numpy as np
from jax import lax
from jax.experimental import pallas as pl
from jax.experimental.pallas import tpu as pltpu
from jax.sharding import PartitionSpec as P

NR = 192
NTH = 512
STEP = 0.1
SHIFT = 0.0001
LIMIT = 56 * 1024 * 1024
MESH = pl.DeviceIdType.MESH
f32 = jnp.float32
bf16 = jnp.bfloat16
VM = pl.BlockSpec(memory_space=pltpu.VMEM)


def cas(n):
    x = 2.0 * np.pi / NTH * (n % NTH)
    return np.cos(x) + np.sin(x)


def halves(table):
    high = table.astype(np.float32).astype(ml_dtypes.bfloat16)
    low = (table - high.astype(np.float64)).astype(np.float32).astype(ml_dtypes.bfloat16)
    return high, low


@functools.lru_cache(None)
def forward_table(pa):
    columns = NTH // pa
    k = np.arange(NTH)[None, :]
    j = np.arange(NTH)[:, None]
    same = -cas(k * j)
    beside = -(cas(k * (j - 1)) - cas(k * (j + 1)))
    both = [np.concatenate([same[p * columns:(p + 1) * columns], beside[p * columns:(p + 1) * columns]], 0) for p in range(pa)]
    return halves(np.stack(both))


@functools.lru_cache(None)
def inverse_table(pa):
    columns = NTH // pa
    k = np.arange(NTH)[:, None]
    j = np.arange(NTH)[None, :]
    same = cas(k * j) / NTH
    beside = (cas(k * (j + 1)) - cas(k * (j - 1))) / NTH
    parts = []
    for p in range(pa):
        part = slice(p * columns, (p + 1) * columns)
        parts.append(np.stack([same[:, part], beside[:, part]]))
    return halves(np.stack(parts))


@functools.lru_cache(None)
def radial_ratios(pa):
    radius = NR + np.arange(NR) + 0.5
    step = 2.0 * np.pi / NTH
    arc = 1.0 / (radius * step) ** 2
    up = (radius + 0.5) / radius
    down = (radius - 0.5) / radius
    up[-1] = 0.0
    down[0] = 0.0
    k = np.arange(NTH)
    diagonal = SHIFT + arc[:, None] * (2.0 - 2.0 * np.cos(step * k))[None, :] + up[:, None] + down[:, None]
    lower = np.broadcast_to(-down[:, None], diagonal.shape)
    upper = np.broadcast_to(-up[:, None], diagonal.shape)

    def moved(x, s, fill):
        pad = np.full((abs(s), NTH), fill)
        return np.concatenate([pad, x[:-s]], 0) if s > 0 else np.concatenate([x[-s:], pad], 0)

    out = []
    stride = 1
    while stride < NR:
        low = lower / moved(diagonal, stride, 1.0)
        high = upper / moved(diagonal, -stride, 1.0)
        out += [low, high]
        diagonal = diagonal - low * moved(upper, stride, 0.0) - high * moved(lower, -stride, 0.0)
        lower = -low * moved(lower, stride, 0.0)
        upper = -high * moved(upper, -stride, 0.0)
        stride *= 2
    out.append(1.0 / diagonal)
    whole = np.stack(out).astype(np.float32)
    columns = NTH // pa
    return np.stack([whole[:, :, p * columns:(p + 1) * columns] for p in range(pa)])


def iota(shape, axis):
    return lax.broadcasted_iota(jnp.int32, shape, axis)


def radii():
    return (iota((NR, 1), 0) + NR).astype(f32) + 0.5


def rolled(x, s):
    return jnp.concatenate([x[s:], x[:s]], 0)


def rates_of(x):
    is_rate = iota(x.shape, 0) % 4 == 3
    w = jnp.where(is_rate, x, 0.0)
    return is_rate, w + rolled(w, 1) + rolled(w, 2) + rolled(w, 3)


def loop(first, last, step):
    if last - first <= 8:
        for i in range(first, last):
            step(i)
    else:
        lax.fori_loop(first, last, lambda i, _: (step(i), 0)[1], 0)


def thirds(x):
    one = x.astype(bf16).astype(f32)
    two = (x - one).astype(bf16).astype(f32)
    return [one, two, x - one - two]


def slots_of(gz, capacity, counts, rank):
    block = rank.shape[1]
    live = iota((1, block), 1) < counts[0]
    target = jnp.where(live, rank[...], gz)
    marks = (iota((gz, block), 0) == target).astype(f32)
    earlier = (iota((128, 128), 0) < iota((128, 128), 1)).astype(f32).astype(bf16)
    carry = jnp.zeros((gz, 1), f32)
    slots = []
    for b in range(block // 128):
        part = marks[:, 128 * b:128 * b + 128]
        before = jnp.dot(part.astype(bf16), earlier, preferred_element_type=f32) + carry
        slots.append(jnp.sum(before * part, axis=0, keepdims=True))
        carry = carry + jnp.sum(part, axis=1, keepdims=True)
    slot = jnp.concatenate(slots, 1).astype(jnp.int32)
    place = jnp.where(live, target * capacity + slot, -1)
    low_hot = (iota((128, block), 0) == (place & 127)).astype(f32).astype(bf16)
    return place >> 7, low_hot


def place_rows(gz, high, low_hot, table, target, combine):
    height = table.shape[0]
    tiles = target.shape[2] // 128

    def slab(g):
        left = [jnp.where(high == g * tiles + i, table, 0.0).astype(bf16) for i in range(tiles)]
        got = lax.dot_general(jnp.concatenate(left, 0), low_hot, (((1,), (1,)), ((), ())), preferred_element_type=f32)
        for i in range(tiles):
            target[g, :, 128 * i:128 * i + 128] = combine(got[height * i:height * i + height])

    loop(0, gz, slab)


def drag_table(parcels, cell):
    total = 0.0
    for half in (parcels[0:8], parcels[8:16]):
        is_rate, rate = rates_of(half)
        weight = rate / (1.0 + STEP * rate)
        total = total + jnp.where(is_rate, weight, weight * half)
    total = total + rolled(total, 4)
    first = iota(total.shape, 0) < 4
    one, two, three = thirds(total)
    cells = cell[...]
    line = ((cells >> 7) + 1).astype(f32)
    column = (cells & 127).astype(f32)
    row = iota(total.shape, 0)
    last = jnp.where(first, three, jnp.where(row == 4, line, jnp.where(row == 5, column, 0.0)))
    return jnp.concatenate([jnp.where(first, one, two), last], 0)


def drag_rows(r):
    sums = r[0:8] + rolled(r[0:8], 4) + r[8:16]
    return jnp.where(iota(sums.shape, 0) == 4, r[12:13] * 128.0 + r[13:14], sums)


def parcel_rows(r):
    return r[0:16] + r[16:32] + r[32:48]


def deposit_slab(g, came, turned, fluid, deposit, parts):
    columns = deposit.shape[2]
    rows = came[g]
    capacity = rows.shape[1]
    code = rows[4:5].astype(jnp.int32)
    line = (code >> 7) - 1
    column = code & 127
    line_hot = (iota((NR, capacity), 0) == line).astype(f32).astype(bf16)
    column_hot = iota((columns, capacity), 0) == column
    picked = jnp.dot(turned, line_hot, preferred_element_type=f32)
    pushes = []
    for i, c in enumerate(parts):
        both = picked[2 * i * columns:(2 * i + 1) * columns] + picked[(2 * i + 1) * columns:(2 * i + 2) * columns]
        speed = jnp.sum(jnp.where(column_hot, both, 0.0), axis=0, keepdims=True)
        drag = (rows[c:c + 1] - speed * rows[3:4]).astype(bf16).astype(f32)
        fluid[g, c:c + 1] = speed
        fluid[g, 4 + c:5 + c] = speed
        pushes.append(jnp.where(column_hot, drag, 0.0).astype(bf16))
    added = lax.dot_general(line_hot, jnp.concatenate(pushes, 0), (((1,), (1,)), ((), ())), preferred_element_type=f32)
    for i, c in enumerate(parts):
        deposit[c] += added[:, i * columns:(i + 1) * columns]


def split_dot(x, high, low):
    top = x.astype(bf16)
    rest = (x - top.astype(f32)).astype(bf16)
    out = jnp.dot(top, low, preferred_element_type=f32) + jnp.dot(rest, high, preferred_element_type=f32)
    return out + jnp.dot(top, high, preferred_element_type=f32)


def face_weights(viscosity, near, edge_left, edge_right):
    radius = radii()
    arc = 1.0 / (radius * (2.0 * math.pi / NTH)) ** 2
    nu = viscosity[...]
    return [
        0.5 * (nu + near[3]),
        (radius + 0.5) / radius * 0.5 * (nu + outward(nu)),
        (radius - 0.5) / radius * 0.5 * (nu + inward(nu)),
        arc * 0.5 * (nu + ahead(nu, edge_right[:, 3:4])),
        arc * 0.5 * (nu + behind(nu, edge_left[:, 7:8])),
    ]


def outward(x):
    return jnp.concatenate([x[1:], jnp.zeros_like(x[:1])], 0)


def inward(x):
    return jnp.concatenate([jnp.zeros_like(x[:1]), x[:-1]], 0)


def ahead(x, edge):
    columns = x.shape[1]
    return jnp.where(iota(x.shape, 1) == columns - 1, edge, pltpu.roll(x, columns - 1, 1))


def behind(x, edge):
    return jnp.where(iota(x.shape, 1) == 0, edge, pltpu.roll(x, 1, 1))


def most_of(c, speeds, near, edge_left, edge_right, deposit, weights):
    u = speeds[c]
    sides = (near[c], outward(u), inward(u), ahead(u, edge_right[:, c:c + 1]), behind(u, edge_left[:, 4 + c:5 + c]))
    total = deposit[c]
    for w, s in zip(weights, sides):
        total = total + w * (s - u)
    return u + STEP * total


def far_part(c, speeds, viscosity, far):
    return (0.5 * STEP) * (viscosity[...] + far[3]) * (far[c] - speeds[c])


def transform(pa, radial, azimuthal, high, low, partial):
    columns = radial.shape[1]
    radius = radii()
    flux = jnp.where(iota(radial.shape, 0) == NR - 1, 0.0, (radius + 0.5) * 0.5 * (radial + outward(radial)))
    divergence = (flux - inward(flux)) / radius
    across = azimuthal / (2.0 * (2.0 * math.pi / NTH) * radius)
    out = split_dot(jnp.concatenate([divergence, across], 1), high[...], low[...])
    for q in range(pa):
        partial[q % 2, q // 2] = out[:, q * columns:(q + 1) * columns]


def main_kernel(gz, pa, counts, rank_in, cell_in, parcels_in, velocity, viscosity, high_in, low_in, ratios,
                ustar, hat, second_in, fluid,
                rank, cell, parcels, speeds, nu, high, low, held, first, second, first_in,
                near, far, edges, edge_left, edge_right, deposit, partial, came, rest,
                lsem, fsend, frecv, send, recv, zsend, zrecv, wsend, wrecv, esend, erecv, psend, precv, rsend, rrecv,
                gsend, grecv, hsend, hrecv):
    me = lax.axis_index("gz")
    mp = lax.axis_index("pa")
    columns = nu.shape[1]
    loads = [
        pltpu.make_async_copy(a, b, lsem.at[i])
        for i, (a, b) in enumerate((
            (rank_in, rank), (cell_in, cell), (parcels_in, parcels), (velocity, speeds), (viscosity.at[0], nu),
            (high_in.at[mp], high), (low_in.at[mp], low), (ratios.at[mp], held)))
    ]
    for c in loads:
        c.start()
    barrier = pltpu.get_barrier_semaphore()

    def greet(o):
        pl.semaphore_signal(barrier, inc=1, device_id=(lax.rem(me + o, gz), mp), device_id_type=MESH)

    loop(1, gz, greet)
    others = [lax.rem(mp + o, pa) for o in range(1, pa)]
    for q in others:
        pl.semaphore_signal(barrier, inc=1, device_id=(me, q), device_id_type=MESH)

    def peer(o):
        to, bit = 0, 1
        while bit < gz:
            to = to + bit * lax.rem(me // bit + o // bit, 2)
            bit = bit * 2
        return to

    def slab_copy(source, target, ssem, rsem, o):
        to = peer(o)
        return pltpu.make_async_remote_copy(
            src_ref=source.at[to], dst_ref=target.at[me], send_sem=ssem.at[o], recv_sem=rsem.at[o],
            device_id=(to, mp), device_id_type=MESH)

    def first_copy(o):
        return slab_copy(first, first_in, fsend, frecv, o)

    def second_copy(o):
        return slab_copy(second, second_in, send, recv, o)

    odd = lax.rem(me, 2)
    mate = me + 1 - 2 * odd
    stride = 2 - 4 * odd
    beyond, before = me + stride, me - stride
    has_beyond = jnp.logical_and(beyond >= 0, beyond < gz)
    has_before = jnp.logical_and(before >= 0, before < gz)
    half = NR // 2
    spots = [(f, pl.ds(r, half)) for r in (0, half) for f in (3, 1, 2)] + [(0, pl.ds(r, half)) for r in (0, half)]

    def trade(i):
        f, rows = spots[i]
        source = velocity.at[f, rows] if f < 3 else viscosity.at[0, rows]
        return pltpu.make_async_remote_copy(
            src_ref=source, dst_ref=near.at[f, rows], send_sem=zsend.at[i], recv_sem=zrecv.at[i],
            device_id=(mate, mp), device_id_type=MESH)

    def hand_on(i):
        f, rows = spots[i]
        return pltpu.make_async_remote_copy(
            src_ref=near.at[f, rows], dst_ref=far.at[f, rows], send_sem=wsend.at[i], recv_sem=wrecv.at[i],
            device_id=(lax.rem(beyond + gz, gz), mp), device_id_type=MESH)

    @pl.when(jnp.logical_not(has_before))
    def _():
        far[...] = jnp.zeros_like(far)

    pl.semaphore_wait(barrier, gz + pa - 2)
    for i in range(3):
        trade(i).start()
    for c in loads[:5]:
        c.wait()
    high_part, low_hot = slots_of(gz, first.shape[2], counts, rank)
    values = parcels[...]
    place_rows(gz, high_part, low_hot, drag_table(values, cell), first, drag_rows)
    loop(1, gz, lambda o: first_copy(gz - o).start())
    for i in range(3, 6):
        trade(i).start()

    def pass_on(i):
        trade(i).wait_recv()

        @pl.when(has_beyond)
        def _():
            hand_on(i).start()

    def far_ready(numbers):
        @pl.when(has_before)
        def _():
            for i in numbers:
                hand_on(i).wait_recv()

    for i in (0, 1):
        pass_on(i)
    pieces, ends = [], []
    for c in range(3):
        turned = speeds[c].T
        top = turned.astype(bf16)
        pieces += [top, (turned - top.astype(f32)).astype(bf16)]
        ends.append(turned)
    ends.append(nu[...].T)
    edges[...] = jnp.concatenate([x[:1] for x in ends] + [x[columns - 1:] for x in ends], 0)
    right, left = lax.rem(mp + 1, pa), lax.rem(mp + pa - 1, pa)
    sides = [
        pltpu.make_async_remote_copy(
            src_ref=edges, dst_ref=target, send_sem=esend.at[i], recv_sem=erecv.at[i],
            device_id=(me, q), device_id_type=MESH)
        for i, (target, q) in enumerate(((edge_left, right), (edge_right, left)))
    ]
    for c in sides:
        c.start()
    for i in range(6, 8):
        trade(i).start()
    place_rows(gz, high_part, low_hot, jnp.concatenate(thirds(values), 0), second, parcel_rows)
    pass_on(2)
    turned = jnp.concatenate(pieces[2:], 0)
    turned_axial = jnp.concatenate(pieces[:2], 0)
    fluid[...] = jnp.zeros_like(fluid)
    deposit[...] = jnp.zeros_like(deposit)
    first_in[me] = first[me]
    second_in[me] = second[me]
    deposit_slab(me, first_in, turned, fluid, deposit, (1, 2))

    def take(o):
        first_copy(o).wait()
        deposit_slab(peer(o), first_in, turned, fluid, deposit, (1, 2))

    done = 1
    for i in range(3, 6):
        pass_on(i)
        upto = min(gz, done + 1 + gz // 8)
        loop(done, upto, take)
        done = upto
    loop(done, gz, take)
    for c in sides:
        c.wait()
    for c in loads[5:]:
        c.wait()
    edge_l, edge_r = edge_left[...].T, edge_right[...].T
    weights = face_weights(nu, near, edge_l, edge_r)
    for c in (1, 2):
        ustar[c] = most_of(c, speeds, near, edge_l, edge_r, deposit, weights)
    far_ready(range(6))
    loop(1, gz, lambda o: second_copy(gz - o).start())
    radial, azimuthal = [ustar[c] + far_part(c, speeds, nu, far) for c in (1, 2)]
    ustar[1] = radial
    ustar[2] = azimuthal
    transform(pa, radial, azimuthal, high, low, partial)
    core = lax.rem(mp, 2)
    pair = mp + 1 - 2 * core
    place = mp // 2
    pairs = pa // 2
    order = [lax.rem(place + 1 + i, pairs) for i in range(pairs)]
    inner = [
        pltpu.make_async_remote_copy(
            src_ref=partial.at[1 - core, q], dst_ref=came.at[q], send_sem=psend.at[i], recv_sem=precv.at[i],
            device_id=(me, pair), device_id_type=MESH)
        for i, q in enumerate(order)
    ]
    for c in inner:
        c.start()
    outer = []
    for i, q in enumerate(order[:-1]):
        inner[i].wait_recv()
        came[q] = came[q] + partial[core, q]
        outer.append(pltpu.make_async_remote_copy(
            src_ref=came.at[q], dst_ref=rest.at[i], send_sem=rsend.at[i], recv_sem=rrecv.at[i],
            device_id=(me, 2 * q + core), device_id_type=MESH))
        outer[-1].start()
    for i in (6, 7):
        pass_on(i)

    def axial(o):
        deposit_slab(peer(o), first_in, turned_axial, fluid, deposit, (0,))

    loop(0, gz // 2, axial)
    inner[-1].wait_recv()
    x = partial[core, place] + came[place]
    for i, c in enumerate(outer):
        c.wait()
        x = x + rest[i]
    radius = radii()
    mean = jnp.sum(radius * x, axis=0, keepdims=True) * (1.0 / (NR * (NR + NR / 2)))
    x = x - jnp.where(iota((1, columns), 1) + mp * columns == 0, mean, 0.0)
    stride, n = 1, 0
    while stride < NR:
        pad = jnp.zeros((stride, columns), f32)
        lower = jnp.concatenate([pad, x[:-stride]], 0)
        upper = jnp.concatenate([x[stride:], pad], 0)
        x = x - held[n] * lower - held[n + 1] * upper
        stride, n = stride * 2, n + 2
    hat[mp] = x * held[n]
    spread = [
        pltpu.make_async_remote_copy(
            src_ref=hat.at[mp], dst_ref=hat.at[mp], send_sem=gsend.at[i], recv_sem=grecv.at[i],
            device_id=(me, q), device_id_type=MESH)
        for i, q in enumerate([2 * q + core for q in order[:-1]] + [pair])
    ]
    for c in spread:
        c.start()
    again = []
    for i in range(pairs - 1):
        q = 2 * lax.rem(place + 2 * pairs - 1 - i, pairs) + core
        spread[i].wait_recv()
        again.append(pltpu.make_async_remote_copy(
            src_ref=hat.at[q], dst_ref=hat.at[q], send_sem=hsend.at[i], recv_sem=hrecv.at[i],
            device_id=(me, pair), device_id_type=MESH))
        again[-1].start()
    loop(gz // 2, gz, axial)
    weights = face_weights(nu, near, edge_l, edge_r)
    ustar[0] = most_of(0, speeds, near, edge_l, edge_r, deposit, weights)
    far_ready((6, 7))
    ustar[0] = ustar[0] + far_part(0, speeds, nu, far)
    spread[-1].wait_recv()
    for c in again:
        c.wait()
    for c in spread + inner:
        c.wait_send()
    for i in range(8):
        trade(i).wait_send()

    @pl.when(has_beyond)
    def _():
        for i in range(8):
            hand_on(i).wait_send()

    loop(1, gz, lambda o: second_copy(o).wait())


def finish_kernel(gz, pa, flat, where, hat, ustar, high, low, second, fluid, velocity_out, parcels_out):
    capacity = second.shape[2]
    x = jnp.concatenate([hat[q] for q in range(pa)], 1)
    slope = 0.5 * (jnp.concatenate([x[1:], x[-1:]], 0) - jnp.concatenate([x[:1], x[:-1]], 0))
    velocity_out[0] = ustar[0]
    velocity_out[1] = ustar[1] - split_dot(slope, high[0, 0], low[0, 0])
    turn = split_dot(x, high[0, 1], low[0, 1]) / (2.0 * (2.0 * math.pi / NTH) * radii())
    velocity_out[2] = ustar[2] - turn

    def slab(g, _):
        speed = fluid[g]
        for h in (0, 8):
            rows = second[g, h:h + 8]
            is_rate, rate = rates_of(rows)
            moved = (rows + STEP * rate * speed) / (1.0 + STEP * rate)
            rows = jnp.where(is_rate, rows, moved)
            if flat:
                parcels_out[h:h + 8, pl.ds(pl.multiple_of(g * capacity, 128), capacity)] = rows
            else:
                parcels_out[g, h:h + 8] = rows
        return 0

    lax.fori_loop(0, gz, slab, 0, unroll=gz <= 8)


def body(velocity, viscosity, parcels, dest_rank, dest_cell, counts):
    gz = lax.axis_size("gz")
    pa = lax.axis_size("pa")
    columns = viscosity.shape[2]
    block = parcels.shape[0]
    slots = 3 * block // gz
    capacity = -(-slots // 128) * 128
    flat = capacity == slots
    velocity = velocity.reshape(3, NR, columns)

    def shape(*s):
        return jax.ShapeDtypeStruct(s, f32)

    plain = pltpu.CompilerParams(vmem_limit_bytes=LIMIT)
    dma = pltpu.SemaphoreType.DMA
    where = lax.axis_index("pa").astype(jnp.int32).reshape(1)
    high, low = forward_table(pa)
    ratios = radial_ratios(pa)
    ANY = pl.BlockSpec(memory_space=pltpu.HBM)

    def hold(*s):
        return pltpu.VMEM(s, f32)

    ustar, hat, second, fluid = pl.pallas_call(
        functools.partial(main_kernel, gz, pa),
        out_shape=(shape(3, NR, columns), shape(pa, NR, columns), shape(gz, 16, capacity), shape(gz, 8, capacity)),
        in_specs=[pl.BlockSpec(memory_space=pltpu.SMEM)] + [ANY] * 8,
        out_specs=(VM,) * 4,
        scratch_shapes=[
            pltpu.VMEM((1, block), jnp.int32), pltpu.VMEM((1, block), jnp.int32), hold(16, block),
            hold(3, NR, columns), hold(NR, columns),
            pltpu.VMEM((2 * columns, NTH), bf16), pltpu.VMEM((2 * columns, NTH), bf16), hold(*ratios.shape[1:]),
            hold(gz, 8, capacity), hold(gz, 16, capacity), hold(gz, 8, capacity),
            hold(4, NR, columns), hold(4, NR, columns), hold(8, NR), hold(8, NR), hold(8, NR),
            hold(3, NR, columns), hold(2, pa // 2, NR, columns), hold(pa // 2, NR, columns), hold(pa // 2 - 1, NR, columns),
            dma((8,)), dma((gz,)), dma((gz,)), dma((gz,)), dma((gz,)), dma((8,)), dma((8,)), dma((8,)), dma((8,)),
            dma((2,)), dma((2,)), dma((pa // 2,)), dma((pa // 2,)), dma((pa // 2 - 1,)), dma((pa // 2 - 1,)),
            dma((pa // 2,)), dma((pa // 2,)), dma((pa // 2 - 1,)), dma((pa // 2 - 1,)),
        ],
        compiler_params=pltpu.CompilerParams(collective_id=0, has_side_effects=True, vmem_limit_bytes=LIMIT),
        name="step",
    )(counts, dest_rank.reshape(1, block), dest_cell.reshape(1, block), parcels.T, velocity,
      viscosity, high, low, ratios)
    high, low = inverse_table(pa)
    chosen = pl.BlockSpec((1, 2, NTH, columns), lambda i, w: (w[0], 0, 0, 0))
    velocity_out, parcels_out = pl.pallas_call(
        functools.partial(finish_kernel, gz, pa, flat),
        out_shape=(shape(3, NR, columns), shape(16, gz * slots) if flat else shape(gz, 16, capacity)),
        grid_spec=pltpu.PrefetchScalarGridSpec(
            num_scalar_prefetch=1, grid=(1,),
            in_specs=[VM, VM, chosen, chosen, VM, VM],
            out_specs=(VM, VM)),
        compiler_params=plain,
        name="finish",
    )(where, hat, ustar, high, low, second, fluid)
    if not flat:
        parcels_out = parcels_out[:, :, :slots].transpose(1, 0, 2).reshape(16, gz * slots)
    return velocity_out.reshape(3, 1, NR, columns), parcels_out.T


def solution(mesh):
    in_specs = (
        P(None, "gz", None, "pa"),
        P("gz", None, "pa"),
        P(("gz", "pa"), None),
        P(("gz", "pa"), None),
        P(("gz", "pa")),
        P(("gz", "pa")),
    )
    out_specs = (P(None, "gz", None, "pa"), P(("gz", "pa"), None))
    return jax.shard_map(body, mesh=mesh, in_specs=in_specs, out_specs=out_specs, check_vma=False)
```

```python
import functools
import math

import jax
import jax.numpy as jnp
import ml_dtypes
import numpy as np
from jax import lax
from jax.experimental import pallas as pl
from jax.experimental.pallas import tpu as pltpu
from jax.sharding import PartitionSpec as P

NR = 192
NTH = 512
STEP = 0.1
SHIFT = 0.0001
LIMIT = 56 * 1024 * 1024
MESH = pl.DeviceIdType.MESH
f32 = jnp.float32
bf16 = jnp.bfloat16
VM = pl.BlockSpec(memory_space=pltpu.VMEM)


def cas(n):
    x = 2.0 * np.pi / NTH * (n % NTH)
    return np.cos(x) + np.sin(x)


def halves(table):
    high = table.astype(np.float32).astype(ml_dtypes.bfloat16)
    low = (table - high.astype(np.float64)).astype(np.float32).astype(ml_dtypes.bfloat16)
    return high, low


@functools.lru_cache(None)
def forward_table(pa):
    columns = NTH // pa
    k = np.arange(NTH)[None, :]
    j = np.arange(NTH)[:, None]
    same = -cas(k * j)
    beside = -(cas(k * (j - 1)) - cas(k * (j + 1)))
    both = [np.concatenate([same[p * columns:(p + 1) * columns], beside[p * columns:(p + 1) * columns]], 0) for p in range(pa)]
    return halves(np.stack(both))


@functools.lru_cache(None)
def inverse_table(pa):
    columns = NTH // pa
    k = np.arange(NTH)[:, None]
    j = np.arange(NTH)[None, :]
    same = cas(k * j) / NTH
    beside = (cas(k * (j + 1)) - cas(k * (j - 1))) / NTH
    parts = []
    for p in range(pa):
        part = slice(p * columns, (p + 1) * columns)
        parts.append(np.stack([same[:, part], beside[:, part]]))
    return halves(np.stack(parts))


@functools.lru_cache(None)
def radial_ratios(pa):
    radius = NR + np.arange(NR) + 0.5
    step = 2.0 * np.pi / NTH
    arc = 1.0 / (radius * step) ** 2
    up = (radius + 0.5) / radius
    down = (radius - 0.5) / radius
    up[-1] = 0.0
    down[0] = 0.0
    k = np.arange(NTH)
    diagonal = SHIFT + arc[:, None] * (2.0 - 2.0 * np.cos(step * k))[None, :] + up[:, None] + down[:, None]
    lower = np.broadcast_to(-down[:, None], diagonal.shape)
    upper = np.broadcast_to(-up[:, None], diagonal.shape)

    def moved(x, s, fill):
        pad = np.full((abs(s), NTH), fill)
        return np.concatenate([pad, x[:-s]], 0) if s > 0 else np.concatenate([x[-s:], pad], 0)

    out = []
    stride = 1
    while stride < NR:
        low = lower / moved(diagonal, stride, 1.0)
        high = upper / moved(diagonal, -stride, 1.0)
        out += [low, high]
        diagonal = diagonal - low * moved(upper, stride, 0.0) - high * moved(lower, -stride, 0.0)
        lower = -low * moved(lower, stride, 0.0)
        upper = -high * moved(upper, -stride, 0.0)
        stride *= 2
    out.append(1.0 / diagonal)
    whole = np.stack(out).astype(np.float32)
    columns = NTH // pa
    return np.stack([whole[:, :, p * columns:(p + 1) * columns] for p in range(pa)])


def iota(shape, axis):
    return lax.broadcasted_iota(jnp.int32, shape, axis)


def radii():
    return (iota((NR, 1), 0) + NR).astype(f32) + 0.5


def rolled(x, s):
    return jnp.concatenate([x[s:], x[:s]], 0)


def rates_of(x):
    is_rate = iota(x.shape, 0) % 4 == 3
    w = jnp.where(is_rate, x, 0.0)
    return is_rate, w + rolled(w, 1) + rolled(w, 2) + rolled(w, 3)


def loop(first, last, step):
    if last - first <= 8:
        for i in range(first, last):
            step(i)
    else:
        lax.fori_loop(first, last, lambda i, _: (step(i), 0)[1], 0)


def thirds(x):
    one = x.astype(bf16).astype(f32)
    two = (x - one).astype(bf16).astype(f32)
    return [one, two, x - one - two]


def slots_of(gz, capacity, counts, rank):
    block = rank.shape[1]
    live = iota((1, block), 1) < counts[0]
    target = jnp.where(live, rank[...], gz)
    marks = (iota((gz, block), 0) == target).astype(f32)
    earlier = (iota((128, 128), 0) < iota((128, 128), 1)).astype(f32).astype(bf16)
    carry = jnp.zeros((gz, 1), f32)
    slots = []
    for b in range(block // 128):
        part = marks[:, 128 * b:128 * b + 128]
        before = jnp.dot(part.astype(bf16), earlier, preferred_element_type=f32) + carry
        slots.append(jnp.sum(before * part, axis=0, keepdims=True))
        carry = carry + jnp.sum(part, axis=1, keepdims=True)
    slot = jnp.concatenate(slots, 1).astype(jnp.int32)
    place = jnp.where(live, target * capacity + slot, -1)
    low_hot = (iota((128, block), 0) == (place & 127)).astype(f32).astype(bf16)
    return place >> 7, low_hot


def place_rows(gz, high, low_hot, table, target, combine):
    height = table.shape[0]
    tiles = target.shape[2] // 128

    def slab(g):
        left = [jnp.where(high == g * tiles + i, table, 0.0).astype(bf16) for i in range(tiles)]
        got = lax.dot_general(jnp.concatenate(left, 0), low_hot, (((1,), (1,)), ((), ())), preferred_element_type=f32)
        for i in range(tiles):
            target[g, :, 128 * i:128 * i + 128] = combine(got[height * i:height * i + height])

    loop(0, gz, slab)


def drag_table(parcels, cell):
    total = 0.0
    for half in (parcels[0:8], parcels[8:16]):
        is_rate, rate = rates_of(half)
        weight = rate / (1.0 + STEP * rate)
        total = total + jnp.where(is_rate, weight, weight * half)
    total = total + rolled(total, 4)
    first = iota(total.shape, 0) < 4
    one, two, three = thirds(total)
    cells = cell[...]
    line = ((cells >> 7) + 1).astype(f32)
    column = (cells & 127).astype(f32)
    row = iota(total.shape, 0)
    last = jnp.where(first, three, jnp.where(row == 4, line, jnp.where(row == 5, column, 0.0)))
    return jnp.concatenate([jnp.where(first, one, two), last], 0)


def drag_rows(r):
    sums = r[0:8] + rolled(r[0:8], 4) + r[8:16]
    return jnp.where(iota(sums.shape, 0) == 4, r[12:13] * 128.0 + r[13:14], sums)


def parcel_rows(r):
    return r[0:16] + r[16:32] + r[32:48]


def deposit_slab(g, came, turned, fluid, deposit, parts):
    columns = deposit.shape[2]
    rows = came[g]
    capacity = rows.shape[1]
    code = rows[4:5].astype(jnp.int32)
    line = (code >> 7) - 1
    column = code & 127
    line_hot = (iota((NR, capacity), 0) == line).astype(f32).astype(bf16)
    column_hot = iota((columns, capacity), 0) == column
    picked = jnp.dot(turned, line_hot, preferred_element_type=f32)
    pushes = []
    for i, c in enumerate(parts):
        both = picked[2 * i * columns:(2 * i + 1) * columns] + picked[(2 * i + 1) * columns:(2 * i + 2) * columns]
        speed = jnp.sum(jnp.where(column_hot, both, 0.0), axis=0, keepdims=True)
        drag = (rows[c:c + 1] - speed * rows[3:4]).astype(bf16).astype(f32)
        fluid[g, c:c + 1] = speed
        fluid[g, 4 + c:5 + c] = speed
        pushes.append(jnp.where(column_hot, drag, 0.0).astype(bf16))
    added = lax.dot_general(line_hot, jnp.concatenate(pushes, 0), (((1,), (1,)), ((), ())), preferred_element_type=f32)
    for i, c in enumerate(parts):
        deposit[c] += added[:, i * columns:(i + 1) * columns]


def split_dot(x, high, low):
    top = x.astype(bf16)
    rest = (x - top.astype(f32)).astype(bf16)
    out = jnp.dot(top, low, preferred_element_type=f32) + jnp.dot(rest, high, preferred_element_type=f32)
    return out + jnp.dot(top, high, preferred_element_type=f32)


def face_weights(viscosity, near, edge_left, edge_right):
    radius = radii()
    arc = 1.0 / (radius * (2.0 * math.pi / NTH)) ** 2
    nu = viscosity[...]
    return [
        0.5 * (nu + near[3]),
        (radius + 0.5) / radius * 0.5 * (nu + outward(nu)),
        (radius - 0.5) / radius * 0.5 * (nu + inward(nu)),
        arc * 0.5 * (nu + ahead(nu, edge_right[:, 3:4])),
        arc * 0.5 * (nu + behind(nu, edge_left[:, 7:8])),
    ]


def outward(x):
    return jnp.concatenate([x[1:], jnp.zeros_like(x[:1])], 0)


def inward(x):
    return jnp.concatenate([jnp.zeros_like(x[:1]), x[:-1]], 0)


def ahead(x, edge):
    columns = x.shape[1]
    return jnp.where(iota(x.shape, 1) == columns - 1, edge, pltpu.roll(x, columns - 1, 1))


def behind(x, edge):
    return jnp.where(iota(x.shape, 1) == 0, edge, pltpu.roll(x, 1, 1))


def most_of(c, speeds, near, edge_left, edge_right, deposit, weights):
    u = speeds[c]
    sides = (near[c], outward(u), inward(u), ahead(u, edge_right[:, c:c + 1]), behind(u, edge_left[:, 4 + c:5 + c]))
    total = deposit[c]
    for w, s in zip(weights, sides):
        total = total + w * (s - u)
    return u + STEP * total


def far_part(c, speeds, viscosity, far):
    return (0.5 * STEP) * (viscosity[...] + far[3]) * (far[c] - speeds[c])


def transform(pa, radial, azimuthal, high, low, partial):
    columns = radial.shape[1]
    radius = radii()
    flux = jnp.where(iota(radial.shape, 0) == NR - 1, 0.0, (radius + 0.5) * 0.5 * (radial + outward(radial)))
    divergence = (flux - inward(flux)) / radius
    across = azimuthal / (2.0 * (2.0 * math.pi / NTH) * radius)
    out = split_dot(jnp.concatenate([divergence, across], 1), high[...], low[...])
    for q in range(pa):
        partial[q % 2, q // 2] = out[:, q * columns:(q + 1) * columns]


def main_kernel(gz, pa, counts, rank_in, cell_in, parcels_in, velocity, viscosity, high_in, low_in, ratios,
                ustar, hat, second_in, fluid,
                rank, cell, parcels, speeds, nu, high, low, held, first, second, first_in,
                near, far, edges, edge_left, edge_right, deposit, partial, came, rest,
                lsem, fsend, frecv, send, recv, zsend, zrecv, wsend, wrecv, esend, erecv, psend, precv, rsend, rrecv,
                gsend, grecv, hsend, hrecv):
    me = lax.axis_index("gz")
    mp = lax.axis_index("pa")
    columns = nu.shape[1]
    loads = [
        pltpu.make_async_copy(a, b, lsem.at[i])
        for i, (a, b) in enumerate((
            (rank_in, rank), (cell_in, cell), (parcels_in, parcels), (velocity, speeds), (viscosity.at[0], nu),
            (high_in.at[mp], high), (low_in.at[mp], low), (ratios.at[mp], held)))
    ]
    for c in loads:
        c.start()
    barrier = pltpu.get_barrier_semaphore()

    def greet(o):
        pl.semaphore_signal(barrier, inc=1, device_id=(lax.rem(me + o, gz), mp), device_id_type=MESH)

    loop(1, gz, greet)
    others = [lax.rem(mp + o, pa) for o in range(1, pa)]
    for q in others:
        pl.semaphore_signal(barrier, inc=1, device_id=(me, q), device_id_type=MESH)

    def peer(o):
        to, bit = 0, 1
        while bit < gz:
            to = to + bit * lax.rem(me // bit + o // bit, 2)
            bit = bit * 2
        return to

    def slab_copy(source, target, ssem, rsem, o):
        to = peer(o)
        return pltpu.make_async_remote_copy(
            src_ref=source.at[to], dst_ref=target.at[me], send_sem=ssem.at[o], recv_sem=rsem.at[o],
            device_id=(to, mp), device_id_type=MESH)

    def first_copy(o):
        return slab_copy(first, first_in, fsend, frecv, o)

    def second_copy(o):
        return slab_copy(second, second_in, send, recv, o)

    odd = lax.rem(me, 2)
    mate = me + 1 - 2 * odd
    stride = 2 - 4 * odd
    beyond, before = me + stride, me - stride
    has_beyond = jnp.logical_and(beyond >= 0, beyond < gz)
    has_before = jnp.logical_and(before >= 0, before < gz)
    half = NR // 2
    spots = [(f, pl.ds(r, half)) for r in (0, half) for f in (3, 1, 2)] + [(0, pl.ds(r, half)) for r in (0, half)]

    def trade(i):
        f, rows = spots[i]
        source = velocity.at[f, rows] if f < 3 else viscosity.at[0, rows]
        return pltpu.make_async_remote_copy(
            src_ref=source, dst_ref=near.at[f, rows], send_sem=zsend.at[i], recv_sem=zrecv.at[i],
            device_id=(mate, mp), device_id_type=MESH)

    def hand_on(i):
        f, rows = spots[i]
        return pltpu.make_async_remote_copy(
            src_ref=near.at[f, rows], dst_ref=far.at[f, rows], send_sem=wsend.at[i], recv_sem=wrecv.at[i],
            device_id=(lax.rem(beyond + gz, gz), mp), device_id_type=MESH)

    @pl.when(jnp.logical_not(has_before))
    def _():
        far[...] = jnp.zeros_like(far)

    pl.semaphore_wait(barrier, gz + pa - 2)
    for i in range(3):
        trade(i).start()
    for c in loads[:5]:
        c.wait()
    high_part, low_hot = slots_of(gz, first.shape[2], counts, rank)
    values = parcels[...]
    place_rows(gz, high_part, low_hot, drag_table(values, cell), first, drag_rows)
    loop(1, gz, lambda o: first_copy(gz - o).start())
    for i in range(3, 6):
        trade(i).start()

    def pass_on(i):
        trade(i).wait_recv()

        @pl.when(has_beyond)
        def _():
            hand_on(i).start()

    def far_ready(numbers):
        @pl.when(has_before)
        def _():
            for i in numbers:
                hand_on(i).wait_recv()

    for i in (0, 1):
        pass_on(i)
    pieces, ends = [], []
    for c in range(3):
        turned = speeds[c].T
        top = turned.astype(bf16)
        pieces += [top, (turned - top.astype(f32)).astype(bf16)]
        ends.append(turned)
    ends.append(nu[...].T)
    edges[...] = jnp.concatenate([x[:1] for x in ends] + [x[columns - 1:] for x in ends], 0)
    right, left = lax.rem(mp + 1, pa), lax.rem(mp + pa - 1, pa)
    sides = [
        pltpu.make_async_remote_copy(
            src_ref=edges, dst_ref=target, send_sem=esend.at[i], recv_sem=erecv.at[i],
            device_id=(me, q), device_id_type=MESH)
        for i, (target, q) in enumerate(((edge_left, right), (edge_right, left)))
    ]
    for c in sides:
        c.start()
    for i in range(6, 8):
        trade(i).start()
    place_rows(gz, high_part, low_hot, jnp.concatenate(thirds(values), 0), second, parcel_rows)
    pass_on(2)
    turned = jnp.concatenate(pieces[2:], 0)
    turned_axial = jnp.concatenate(pieces[:2], 0)
    fluid[...] = jnp.zeros_like(fluid)
    deposit[...] = jnp.zeros_like(deposit)
    first_in[me] = first[me]
    second_in[me] = second[me]
    deposit_slab(me, first_in, turned, fluid, deposit, (1, 2))

    def take(o):
        first_copy(o).wait()
        deposit_slab(peer(o), first_in, turned, fluid, deposit, (1, 2))

    done = 1
    for i in range(3, 6):
        pass_on(i)
        upto = min(gz, done + 1 + gz // 8)
        loop(done, upto, take)
        done = upto
    loop(done, gz, take)
    for c in sides:
        c.wait()
    for c in loads[5:]:
        c.wait()
    edge_l, edge_r = edge_left[...].T, edge_right[...].T
    weights = face_weights(nu, near, edge_l, edge_r)
    for c in (1, 2):
        ustar[c] = most_of(c, speeds, near, edge_l, edge_r, deposit, weights)
    far_ready(range(6))
    radial, azimuthal = [ustar[c] + far_part(c, speeds, nu, far) for c in (1, 2)]
    ustar[1] = radial
    ustar[2] = azimuthal
    transform(pa, radial, azimuthal, high, low, partial)
    core = lax.rem(mp, 2)
    pair = mp + 1 - 2 * core
    place = mp // 2
    pairs = pa // 2
    order = [lax.rem(place + 1 + i, pairs) for i in range(pairs)]
    inner = [
        pltpu.make_async_remote_copy(
            src_ref=partial.at[1 - core, q], dst_ref=came.at[q], send_sem=psend.at[i], recv_sem=precv.at[i],
            device_id=(me, pair), device_id_type=MESH)
        for i, q in enumerate(order)
    ]
    for c in inner:
        c.start()
    outer = []
    for i, q in enumerate(order[:-1]):
        inner[i].wait_recv()
        came[q] = came[q] + partial[core, q]
        outer.append(pltpu.make_async_remote_copy(
            src_ref=came.at[q], dst_ref=rest.at[i], send_sem=rsend.at[i], recv_sem=rrecv.at[i],
            device_id=(me, 2 * q + core), device_id_type=MESH))
        outer[-1].start()
    for i in (6, 7):
        pass_on(i)
    loop(1, gz, lambda o: second_copy(gz - o).start())

    def axial(o):
        deposit_slab(peer(o), first_in, turned_axial, fluid, deposit, (0,))

    loop(0, gz // 2, axial)
    inner[-1].wait_recv()
    x = partial[core, place] + came[place]
    for i, c in enumerate(outer):
        c.wait()
        x = x + rest[i]
    radius = radii()
    mean = jnp.sum(radius * x, axis=0, keepdims=True) * (1.0 / (NR * (NR + NR / 2)))
    x = x - jnp.where(iota((1, columns), 1) + mp * columns == 0, mean, 0.0)
    stride, n = 1, 0
    while stride < NR:
        pad = jnp.zeros((stride, columns), f32)
        lower = jnp.concatenate([pad, x[:-stride]], 0)
        upper = jnp.concatenate([x[stride:], pad], 0)
        x = x - held[n] * lower - held[n + 1] * upper
        stride, n = stride * 2, n + 2
    hat[mp] = x * held[n]
    spread = [
        pltpu.make_async_remote_copy(
            src_ref=hat.at[mp], dst_ref=hat.at[mp], send_sem=gsend.at[i], recv_sem=grecv.at[i],
            device_id=(me, q), device_id_type=MESH)
        for i, q in enumerate([2 * q + core for q in order[:-1]] + [pair])
    ]
    for c in spread:
        c.start()
    again = []
    for i in range(pairs - 1):
        q = 2 * lax.rem(place + 2 * pairs - 1 - i, pairs) + core
        spread[i].wait_recv()
        again.append(pltpu.make_async_remote_copy(
            src_ref=hat.at[q], dst_ref=hat.at[q], send_sem=hsend.at[i], recv_sem=hrecv.at[i],
            device_id=(me, pair), device_id_type=MESH))
        again[-1].start()
    loop(gz // 2, gz, axial)
    weights = face_weights(nu, near, edge_l, edge_r)
    ustar[0] = most_of(0, speeds, near, edge_l, edge_r, deposit, weights)
    far_ready((6, 7))
    ustar[0] = ustar[0] + far_part(0, speeds, nu, far)
    spread[-1].wait_recv()
    for c in again:
        c.wait()
    for c in spread + inner:
        c.wait_send()
    for i in range(8):
        trade(i).wait_send()

    @pl.when(has_beyond)
    def _():
        for i in range(8):
            hand_on(i).wait_send()

    loop(1, gz, lambda o: second_copy(o).wait())


def finish_kernel(gz, pa, flat, where, hat, ustar, high, low, second, fluid, velocity_out, parcels_out):
    capacity = second.shape[2]
    x = jnp.concatenate([hat[q] for q in range(pa)], 1)
    slope = 0.5 * (jnp.concatenate([x[1:], x[-1:]], 0) - jnp.concatenate([x[:1], x[:-1]], 0))
    velocity_out[0] = ustar[0]
    velocity_out[1] = ustar[1] - split_dot(slope, high[0, 0], low[0, 0])
    turn = split_dot(x, high[0, 1], low[0, 1]) / (2.0 * (2.0 * math.pi / NTH) * radii())
    velocity_out[2] = ustar[2] - turn

    def slab(g, _):
        speed = fluid[g]
        for h in (0, 8):
            rows = second[g, h:h + 8]
            is_rate, rate = rates_of(rows)
            moved = (rows + STEP * rate * speed) / (1.0 + STEP * rate)
            rows = jnp.where(is_rate, rows, moved)
            if flat:
                parcels_out[h:h + 8, pl.ds(pl.multiple_of(g * capacity, 128), capacity)] = rows
            else:
                parcels_out[g, h:h + 8] = rows
        return 0

    lax.fori_loop(0, gz, slab, 0, unroll=gz <= 8)


def body(velocity, viscosity, parcels, dest_rank, dest_cell, counts):
    gz = lax.axis_size("gz")
    pa = lax.axis_size("pa")
    columns = viscosity.shape[2]
    block = parcels.shape[0]
    slots = 3 * block // gz
    capacity = -(-slots // 128) * 128
    flat = capacity == slots
    velocity = velocity.reshape(3, NR, columns)

    def shape(*s):
        return jax.ShapeDtypeStruct(s, f32)

    plain = pltpu.CompilerParams(vmem_limit_bytes=LIMIT)
    dma = pltpu.SemaphoreType.DMA
    where = lax.axis_index("pa").astype(jnp.int32).reshape(1)
    high, low = forward_table(pa)
    ratios = radial_ratios(pa)
    ANY = pl.BlockSpec(memory_space=pltpu.HBM)

    def hold(*s):
        return pltpu.VMEM(s, f32)

    ustar, hat, second, fluid = pl.pallas_call(
        functools.partial(main_kernel, gz, pa),
        out_shape=(shape(3, NR, columns), shape(pa, NR, columns), shape(gz, 16, capacity), shape(gz, 8, capacity)),
        in_specs=[pl.BlockSpec(memory_space=pltpu.SMEM)] + [ANY] * 8,
        out_specs=(VM,) * 4,
        scratch_shapes=[
            pltpu.VMEM((1, block), jnp.int32), pltpu.VMEM((1, block), jnp.int32), hold(16, block),
            hold(3, NR, columns), hold(NR, columns),
            pltpu.VMEM((2 * columns, NTH), bf16), pltpu.VMEM((2 * columns, NTH), bf16), hold(*ratios.shape[1:]),
            hold(gz, 8, capacity), hold(gz, 16, capacity), hold(gz, 8, capacity),
            hold(4, NR, columns), hold(4, NR, columns), hold(8, NR), hold(8, NR), hold(8, NR),
            hold(3, NR, columns), hold(2, pa // 2, NR, columns), hold(pa // 2, NR, columns), hold(pa // 2 - 1, NR, columns),
            dma((8,)), dma((gz,)), dma((gz,)), dma((gz,)), dma((gz,)), dma((8,)), dma((8,)), dma((8,)), dma((8,)),
            dma((2,)), dma((2,)), dma((pa // 2,)), dma((pa // 2,)), dma((pa // 2 - 1,)), dma((pa // 2 - 1,)),
            dma((pa // 2,)), dma((pa // 2,)), dma((pa // 2 - 1,)), dma((pa // 2 - 1,)),
        ],
        compiler_params=pltpu.CompilerParams(collective_id=0, has_side_effects=True, vmem_limit_bytes=LIMIT),
        name="step",
    )(counts, dest_rank.reshape(1, block), dest_cell.reshape(1, block), parcels.T, velocity,
      viscosity, high, low, ratios)
    high, low = inverse_table(pa)
    chosen = pl.BlockSpec((1, 2, NTH, columns), lambda i, w: (w[0], 0, 0, 0))
    velocity_out, parcels_out = pl.pallas_call(
        functools.partial(finish_kernel, gz, pa, flat),
        out_shape=(shape(3, NR, columns), shape(16, gz * slots) if flat else shape(gz, 16, capacity)),
        grid_spec=pltpu.PrefetchScalarGridSpec(
            num_scalar_prefetch=1, grid=(1,),
            in_specs=[VM, VM, chosen, chosen, VM, VM],
            out_specs=(VM, VM)),
        compiler_params=plain,
        name="finish",
    )(where, hat, ustar, high, low, second, fluid)
    if not flat:
        parcels_out = parcels_out[:, :, :slots].transpose(1, 0, 2).reshape(16, gz * slots)
    return velocity_out.reshape(3, 1, NR, columns), parcels_out.T


def solution(mesh):
    in_specs = (
        P(None, "gz", None, "pa"),
        P("gz", None, "pa"),
        P(("gz", "pa"), None),
        P(("gz", "pa"), None),
        P(("gz", "pa")),
        P(("gz", "pa")),
    )
    out_specs = (P(None, "gz", None, "pa"), P(("gz", "pa"), None))
    return jax.shard_map(body, mesh=mesh, in_specs=in_specs, out_specs=out_specs, check_vma=False)
```
